32 devices in a mesh: seq: 8 (over y, x, core), head: 4 (over z).
Axes of the slice: x: 2, y: 2, z: 4, core: 2. Of those that a mesh axis runs over, the one named last changes fastest.
Arguments:
- queries: bfloat16 [4096, 4096], P('seq', 'head'), may hold values from -15 to 15
- keys: bfloat16 [4096, 2048], P('seq', 'head'), may hold values from -6 to 6
- values: bfloat16 [4096, 2048], P('seq', 'head'), may hold values from -6 to 6
- out_grad: bfloat16 [4096, 4096], P('seq', 'head'), may hold values from -48 to 48
- normed: bfloat16 [4096, 4608], P('seq'), may hold values from -1.1953125 to 1.1953125
- w_query: bfloat16 [4608, 4096], P(None, 'head'), may hold values from -0.125 to 0.125
- w_key: bfloat16 [4608, 2048], P(None, 'head'), may hold values from -0.125 to 0.125
- w_value: bfloat16 [4608, 2048], P(None, 'head'), may hold values from -0.125 to 0.125
- valid_len: int32 [8], replicated, may hold values from 128 to 512, as said below
Outputs:
- grad_x: bfloat16 [4096, 4608], P('seq', 'head')
- grad_wq: bfloat16 [4608, 4096], P('seq', 'head')
- grad_wk: bfloat16 [4608, 2048], P('seq', 'head')
- grad_wv: bfloat16 [4608, 2048], P('seq', 'head')
The draws below stay inside these ranges and needn't reach their ends.
Inputs may be any that keep to these rules, and one draw needn't show every extreme that they name: `valid_len`: every entry lies between 128 and 512; some shard is full and some shard has exactly 128 live slots.
All inputs are finite; a program needn't handle non-finite values.
Results may differ from the reference program's by a relative error of at most 0.024.
Values may be sent and summed in bfloat16 or wider, within the bound.
No kernel may reach another device: no remote copies, remote signals or barrier semaphores. Data moves between devices by JAX's collectives and lax.ppermute only.
A program may use at most 256 MiB of HBM per device.

```python
import jax
import jax.numpy as jnp
from jax import lax

D = 4608
H = 32
KVH = 16
HD = 128
WINDOW = 4096
TOK_DEV = 512
SHARDS = 8
TOKENS = 4096
REACH = 8


def draw_valid_len(key, part):
    shortest = TOK_DEV // 4
    lengths = jax.random.randint(jax.random.fold_in(key, 11), (SHARDS,), shortest, TOK_DEV + 1)
    chosen = jax.random.permutation(jax.random.fold_in(key, 12), SHARDS)
    lengths = lengths.at[chosen[0]].set(TOK_DEV)
    lengths = lengths.at[chosen[1]].set(shortest)
    return lengths.astype(jnp.int32)


def raised(entries, rng, source, target, blocks, factor):
    def block_of(dim):
        return (jnp.arange(entries.shape[dim]) // (entries.shape[dim] // blocks)).reshape((-1,) + (1,) * (entries.ndim - 1 - dim))

    near = jax.random.permutation(rng, blocks)[block_of(target)]
    other_side = (block_of(target) + blocks // 2) % blocks
    return jnp.where((block_of(source) == near) | (block_of(source) == other_side), factor * entries, entries)


def steps_of(key, extent, shards, smallest, high):
    factor_of = 1.0
    for position, blocks in shards:
        heights = jax.random.uniform(jax.random.fold_in(jax.random.fold_in(key, 6), position), (blocks,), jnp.float32, smallest / len(shards), high / len(shards))
        factor_of = factor_of * jnp.repeat(jnp.exp(heights), extent[position] // blocks).reshape((-1,) + (1,) * (len(extent) - 1 - position))
    return factor_of


def scatter_about(key, shape, width, bound, shards=(), kind=jnp.bfloat16):
    level = steps_of(key, shape, shards, -0.22, 0.18) if shards else 1.0
    values = jax.random.normal(key, shape, jnp.float32) * width * level
    return jnp.minimum(jnp.maximum(values, -bound), bound).astype(kind)


def heavy_noise(own_key, extent, width, most, cuts, heavy, kind=jnp.bfloat16):
    values = width * jax.random.normal(own_key, extent, jnp.float32)
    if cuts:
        values = values * steps_of(own_key, extent, cuts, -0.22, 0.18)
    return jnp.clip(raised(values, jax.random.fold_in(own_key, 3), *heavy), -most, most).astype(kind)


def setup_inputs(seed: int = 0) -> dict:
    seeds = jax.random.split(jax.random.key(seed), 10)
    queries = scatter_about(seeds[0], (TOKENS, H * HD), 2.5, 15.0, ((0, 8), (1, 4)))
    keys = scatter_about(seeds[1], (TOKENS, KVH * HD), 1.0, 6.0, ((0, 8), (1, 4)))
    values = scatter_about(seeds[2], (TOKENS, KVH * HD), 1.0, 6.0, ((0, 8), (1, 4)))
    out_grad = scatter_about(seeds[3], (TOKENS, H * HD), 8.0, 48.0, ((0, 8), (1, 4)))
    normed = heavy_noise(seeds[4], (TOKENS, D), 0.2, 1.1953125, ((0, 8),), (0, 1, 8, 2.0))
    w_query = heavy_noise(seeds[5], (D, H * HD), D ** -0.5, 0.125, ((1, 4),), (1, 0, 4, 2.0))
    w_key = heavy_noise(seeds[6], (D, KVH * HD), D ** -0.5, 0.125, ((1, 4),), (1, 0, 4, 2.0))
    w_value = heavy_noise(seeds[7], (D, KVH * HD), D ** -0.5, 0.125, ((1, 4),), (1, 0, 4, 2.0))
    valid_len = draw_valid_len(jax.random.fold_in(seeds[9], 71), 0)
    return dict(queries=queries, keys=keys, values=values, out_grad=out_grad, normed=normed, w_query=w_query, w_key=w_key, w_value=w_value, valid_len=valid_len)


SOFT_CAP = 50.0
ROPE_BASE = 10000.0


def to_bfloat(array_in):
    return lax.optimization_barrier(array_in.astype(jnp.bfloat16)).astype(jnp.float32)


def rotate_back(gradient, positions, head_count):
    row_count = gradient.shape[0]
    half_width = HD // 2
    inverse_freq = ROPE_BASE ** (-(jnp.arange(half_width, dtype=jnp.float32) * (2.0 / HD)))
    angles = positions.astype(jnp.float32)[:, None] * inverse_freq[None, :]
    cosine = jnp.cos(angles)[:, None, :]
    sine_part = jnp.sin(angles)[:, None, :]
    per_head = gradient.reshape(row_count, head_count, HD)
    leading = per_head[:, :, :half_width]
    trailing = per_head[:, :, half_width:]
    rotated = jnp.concatenate([leading * cosine + trailing * sine_part, trailing * cosine - leading * sine_part], axis=2)
    return rotated.reshape(row_count, head_count * HD)


def times_t(left, right):
    return lax.dot_general(left, right, (((1,), (1,)), ((), ())), preferred_element_type=jnp.float32)


def inner_rows(left, right):
    return lax.dot_general(left, right, (((0,), (0,)), ((), ())), preferred_element_type=jnp.float32)


def reference(queries, keys, values, out_grad, normed, w_query, w_key, w_value, valid_len):
    group_size = H // KVH
    lead_rows = REACH * TOK_DEV
    span_rows = (REACH + 1) * TOK_DEV
    score_scale = (D // H) ** -0.5
    kv_width = KVH * HD
    positions = jnp.arange(TOKENS, dtype=jnp.int32)
    token_valid = (positions % TOK_DEV) < valid_len[positions // TOK_DEV]
    grad_rows = jnp.where(token_valid[:, None], out_grad, jnp.zeros_like(out_grad))
    key_value = jnp.concatenate([keys, values], axis=1)
    padded_kv = jnp.concatenate([jnp.zeros((lead_rows, 2 * kv_width), key_value.dtype), key_value], axis=0)
    padded_valid = jnp.concatenate([jnp.zeros((lead_rows,), dtype=bool), token_valid])

    def one_shard(carried, shard_index):
        first_row = (shard_index * TOK_DEV).astype(jnp.int32)
        query_blocks = lax.dynamic_slice_in_dim(queries, first_row, TOK_DEV, 0).astype(jnp.float32).reshape(TOK_DEV, KVH, group_size, HD)
        grad_blocks = lax.dynamic_slice_in_dim(grad_rows, first_row, TOK_DEV, 0).astype(jnp.float32).reshape(TOK_DEV, KVH, group_size, HD)
        window_kv = lax.dynamic_slice_in_dim(padded_kv, first_row, span_rows, 0).astype(jnp.float32)
        key_block = window_kv[:, :kv_width].reshape(span_rows, KVH, HD)
        value_block = window_kv[:, kv_width:].reshape(span_rows, KVH, HD)
        key_valid = lax.dynamic_slice_in_dim(padded_valid, first_row, span_rows, 0)
        query_pos = first_row + jnp.arange(TOK_DEV, dtype=jnp.int32)
        key_pos = first_row - lead_rows + jnp.arange(span_rows, dtype=jnp.int32)
        offset_gap = query_pos[:, None] - key_pos[None, :]
        allowed = (offset_gap >= 0) & (offset_gap < WINDOW) & (key_pos[None, :] >= 0) & (key_valid[None, :] | (offset_gap == 0))
        raw_scores = jnp.einsum("qhgd,khd->hgqk", query_blocks, key_block) * score_scale
        capped = SOFT_CAP * jnp.tanh(raw_scores / SOFT_CAP)
        running = jnp.sum(jnp.where(allowed, jnp.exp(capped), 0.0), axis=-1, keepdims=True)
        exact = jnp.where(allowed, jnp.exp(capped - jnp.log(running)), 0.0)
        rounded = to_bfloat(exact)
        attended = jnp.einsum("hgqk,khd->qhgd", rounded, value_block)
        row_delta = jnp.sum(grad_blocks * attended, axis=-1)
        grad_probs = jnp.einsum("qhgd,khd->hgqk", grad_blocks, value_block)
        grad_scores = exact * (grad_probs - jnp.transpose(row_delta, (1, 2, 0))[..., None]) * (1.0 - (capped / SOFT_CAP) ** 2)
        grad_scores = to_bfloat(grad_scores)
        query_grad = jnp.einsum("hgqk,khd->qhgd", grad_scores, key_block) * score_scale
        key_grad = jnp.einsum("hgqk,qhgd->khd", grad_scores, query_blocks) * score_scale
        value_grad = jnp.einsum("hgqk,qhgd->khd", rounded, grad_blocks)
        update = jnp.concatenate([key_grad.reshape(span_rows, kv_width), value_grad.reshape(span_rows, kv_width)], axis=1)
        current = lax.dynamic_slice_in_dim(carried, first_row, span_rows, 0)
        carried = lax.dynamic_update_slice_in_dim(carried, current + update, first_row, 0)
        return carried, query_grad.reshape(TOK_DEV, H * HD)

    initial = jnp.zeros((lead_rows + TOKENS, 2 * kv_width), jnp.float32)
    summed, query_parts = lax.scan(one_shard, initial, jnp.arange(SHARDS, dtype=jnp.int32))
    summed = summed[lead_rows:]
    query_grad = query_parts.reshape(TOKENS, H * HD)
    query_pre = rotate_back(query_grad, positions, H).astype(jnp.bfloat16)
    key_pre = rotate_back(summed[:, :kv_width], positions, KVH).astype(jnp.bfloat16)
    value_pre = summed[:, kv_width:].astype(jnp.bfloat16)
    grad_x = (times_t(query_pre, w_query) + times_t(key_pre, w_key) + times_t(value_pre, w_value)).astype(jnp.bfloat16)
    grad_wq = inner_rows(normed, query_pre).astype(jnp.bfloat16)
    grad_wk = inner_rows(normed, key_pre).astype(jnp.bfloat16)
    grad_wv = inner_rows(normed, value_pre).astype(jnp.bfloat16)
    return (grad_x, grad_wq, grad_wk, grad_wv)
```

```python
import functools
import math

import jax
import jax.numpy as jnp
from jax import lax
from jax.experimental import pallas as pl
from jax.experimental.pallas import tpu as pltpu
from jax.sharding import PartitionSpec as P

D = 4608
H = 32
HD = 128
WINDOW = 4096


SOFT_CAP = 50.0
ROPE_BASE = 10000.0


def passed_along(value, axis, by):
    size = lax.axis_size(axis)
    pairs = [(i, i + by) for i in range(size) if 0 <= i + by < size]
    return lax.ppermute(value, axis, pairs)


def rotate_back(gradient, positions, head_count):
    row_count = gradient.shape[0]
    half_width = HD // 2
    inverse_freq = ROPE_BASE ** (-(jnp.arange(half_width, dtype=jnp.float32) * (2.0 / HD)))
    angles = positions.astype(jnp.float32)[:, None] * inverse_freq[None, :]
    cosine = jnp.cos(angles)[:, None, :]
    sine_part = jnp.sin(angles)[:, None, :]
    per_head = gradient.reshape(row_count, head_count, HD)
    leading = per_head[:, :, :half_width]
    trailing = per_head[:, :, half_width:]
    rotated = jnp.concatenate(
        [leading * cosine + trailing * sine_part, trailing * cosine - leading * sine_part], axis=2
    )
    return rotated.reshape(row_count, head_count * HD)


def times_t(left, right):
    return lax.dot_general(
        left, right, (((1,), (1,)), ((), ())), preferred_element_type=jnp.float32
    )


def inner_rows(left, right):
    return lax.dot_general(
        left, right, (((0,), (0,)), ((), ())), preferred_element_type=jnp.float32
    )


def general_body(queries, keys, values, out_grad, normed, w_query, w_key, w_value, valid_len):
    row_count = queries.shape[0]
    kv_heads = keys.shape[1] // HD
    head_count = queries.shape[1] // HD
    group_size = head_count // kv_heads
    kv_width = kv_heads * HD
    hop_count = WINDOW // row_count
    score_scale = (D // H) ** (-0.5)
    shard_index = lax.axis_index("seq")
    last_shard = valid_len.shape[0] - 1
    row_iota = jnp.arange(row_count, dtype=jnp.int32)
    query_pos = shard_index * row_count + row_iota
    own_valid = row_iota < valid_len[shard_index]
    grad_rows = jnp.where(own_valid[:, None], out_grad, jnp.zeros_like(out_grad))
    query_blocks = queries.reshape(row_count, kv_heads, group_size, HD)
    grad_blocks = grad_rows.reshape(row_count, kv_heads, group_size, HD)
    key_value = jnp.concatenate([keys, values], axis=1)
    arrived = [key_value]
    moving = key_value
    for distance in range(1, hop_count + 1):
        moving = passed_along(moving, "seq", 1)
        arrived.append(moving)
    allowed_list = []
    capped_list = []
    running = jnp.zeros((kv_heads, group_size, row_count), jnp.float32)
    for distance in range(hop_count + 1):
        key_pos = (shard_index - distance) * row_count + row_iota
        owner = jnp.clip(shard_index - distance, 0, last_shard)
        key_valid = row_iota < valid_len[owner]
        offset_gap = query_pos[:, None] - key_pos[None, :]
        allowed = (
            (offset_gap >= 0)
            & (offset_gap < WINDOW)
            & (key_pos[None, :] >= 0)
            & (key_valid[None, :] | (offset_gap == 0))
        )
        key_block = arrived[distance][:, :kv_width].reshape(row_count, kv_heads, HD)
        raw_scores = (
            jnp.einsum(
                "qhgd,khd->hgqk", query_blocks, key_block, preferred_element_type=jnp.float32
            )
            * score_scale
        )
        capped = SOFT_CAP * jnp.tanh(raw_scores / SOFT_CAP)
        running = running + jnp.sum(jnp.where(allowed, jnp.exp(capped), 0.0), axis=-1)
        allowed_list.append(allowed)
        capped_list.append(capped)
    log_total = jnp.log(running)[..., None]
    attended = jnp.zeros((row_count, kv_heads, group_size, HD), jnp.float32)
    for distance in range(hop_count + 1):
        value_block = arrived[distance][:, kv_width:].reshape(row_count, kv_heads, HD)
        rounded = jnp.where(
            allowed_list[distance], jnp.exp(capped_list[distance] - log_total), 0.0
        ).astype(jnp.bfloat16)
        attended = attended + jnp.einsum(
            "hgqk,khd->qhgd", rounded, value_block, preferred_element_type=jnp.float32
        )
    row_delta = jnp.sum(grad_blocks.astype(jnp.float32) * attended, axis=-1)
    delta_cols = jnp.transpose(row_delta, (1, 2, 0))[..., None]
    query_grad = jnp.zeros((row_count, kv_heads, group_size, HD), jnp.float32)
    partials = [None] * (hop_count + 1)
    for distance in range(hop_count, -1, -1):
        key_block = arrived[distance][:, :kv_width].reshape(row_count, kv_heads, HD)
        value_block = arrived[distance][:, kv_width:].reshape(row_count, kv_heads, HD)
        capped = capped_list[distance]
        exact = jnp.where(allowed_list[distance], jnp.exp(capped - log_total), 0.0)
        rounded = exact.astype(jnp.bfloat16)
        grad_probs = jnp.einsum(
            "qhgd,khd->hgqk", grad_blocks, value_block, preferred_element_type=jnp.float32
        )
        grad_scores = (exact * (grad_probs - delta_cols) * (1.0 - (capped / SOFT_CAP) ** 2)).astype(
            jnp.bfloat16
        )
        query_grad = (
            query_grad
            + jnp.einsum(
                "hgqk,khd->qhgd", grad_scores, key_block, preferred_element_type=jnp.float32
            )
            * score_scale
        )
        key_grad = (
            jnp.einsum(
                "hgqk,qhgd->khd", grad_scores, query_blocks, preferred_element_type=jnp.float32
            )
            * score_scale
        )
        value_grad = jnp.einsum(
            "hgqk,qhgd->khd", rounded, grad_blocks, preferred_element_type=jnp.float32
        )
        partials[distance] = jnp.concatenate(
            [key_grad.reshape(row_count, kv_width), value_grad.reshape(row_count, kv_width)], axis=1
        )
    carried = partials[hop_count]
    for distance in range(hop_count - 1, -1, -1):
        carried = (
            passed_along(carried.astype(jnp.bfloat16), "seq", -1).astype(carried.dtype)
            + partials[distance]
        )
    query_pre = rotate_back(
        query_grad.reshape(row_count, head_count * HD), query_pos, head_count
    ).astype(jnp.bfloat16)
    key_pre = rotate_back(carried[:, :kv_width], query_pos, kv_heads).astype(jnp.bfloat16)
    value_pre = carried[:, kv_width:].astype(jnp.bfloat16)
    input_terms = (
        times_t(query_pre, w_query) + times_t(key_pre, w_key) + times_t(value_pre, w_value)
    )
    grad_x = lax.psum_scatter(
        input_terms.astype(jnp.bfloat16), "head", scatter_dimension=1, tiled=True
    )
    stacked = jnp.concatenate([query_pre, key_pre, value_pre], axis=1)
    weight_total = lax.psum_scatter(
        inner_rows(normed, stacked).astype(jnp.bfloat16), "seq", scatter_dimension=0, tiled=True
    ).astype(jnp.float32)
    query_cols = head_count * HD
    grad_wq = weight_total[:, :query_cols].astype(jnp.bfloat16)
    grad_wk = weight_total[:, query_cols : query_cols + kv_width].astype(jnp.bfloat16)
    grad_wv = weight_total[:, query_cols + kv_width :].astype(jnp.bfloat16)
    return (grad_x, grad_wq, grad_wk, grad_wv)
QB = 512
KB = 512
NT = (((1,), (1,)), ((), ()))
NN = (((1,), (0,)), ((), ()))


def dot(a, b, dims):
    return lax.dot_general(a, b, dims, preferred_element_type=jnp.float32)


def attention_kernel(shards, rows, score_scale, place, lens, *refs):
    n = shards
    qg_in = refs[:n]
    mine_in = refs[n : 2 * n]
    peer_in = refs[2 * n : 3 * n]
    cos_r, sin_r, cos_s, sin_s = refs[3 * n : 3 * n + 4]
    dq_out, keep_out, give_out = refs[3 * n + 4 : 3 * n + 7]
    (qg_st, kv_st, q2, k2, kT, gx, vx, vT, probs, slopes, dq, dk, dv, oT, dqT, qT, gT, sems) = refs[3 * n + 7 :]
    me = place[0]
    core = lax.rem(me, 2)
    copies = []
    for m in range(n):
        shard = place[1 + m]
        copies.append(pltpu.make_async_copy(qg_in[m], qg_st.at[shard], sems.at[0, m]))
        copies.append(pltpu.make_async_copy(mine_in[m], kv_st.at[core, shard], sems.at[1, m]))
        copies.append(pltpu.make_async_copy(peer_in[m], kv_st.at[1 - core, shard], sems.at[2, m]))
    for copy in copies:
        copy.start()
    total_rows = n * rows
    dk[...] = jnp.zeros_like(dk)
    dv[...] = jnp.zeros_like(dv)
    for copy in copies:
        copy.wait()

    piece = 128
    lane = lax.broadcasted_iota(jnp.int32, (piece, HD), 1)

    def pack_shard(shard, offset):
        valid = lens[shard]

        def pack_piece(i, _):
            src = pl.multiple_of(i * piece, piece)
            dst = pl.multiple_of(offset + i * piece, 16)
            live = (lax.broadcasted_iota(jnp.int32, (piece, HD), 0) + src) < valid
            at = pl.ds(src, piece)
            to = pl.ds(dst, piece)
            q = jnp.where(live, qg_st[shard, at, :HD].astype(jnp.float32), 0.0) * (score_scale / SOFT_CAP)
            hi = q.astype(jnp.bfloat16)
            q2[to, :HD] = hi
            q2[to, HD:] = (q - hi.astype(jnp.float32)).astype(jnp.bfloat16)
            zero = jnp.zeros((piece, HD), jnp.bfloat16)
            gx[to, :HD] = jnp.where(live, qg_st[shard, at, HD:], zero)
            k = jnp.where(live, kv_st[0, shard, at, :], zero)
            k2[to, :HD] = k
            k2[to, HD:] = k
            vx[to, :HD] = jnp.where(live, kv_st[1, shard, at, :], zero)
            vx[to, HD:] = jnp.where(live, 1.0, 0.0).astype(jnp.bfloat16)
            return 0

        lax.fori_loop(0, rows // piece, pack_piece, 0)
        return offset + ((valid + 15) // 16) * 16

    end = lax.fori_loop(0, n, pack_shard, jnp.int32(0))
    tail = pl.ds(pl.multiple_of(end, 16), KB)
    for ref in (q2, k2, gx, vx):
        ref[tail, :] = jnp.zeros((KB, 2 * HD), jnp.bfloat16)
    blocks = pl.cdiv(end, QB)

    def turn(i, _):
        at = pl.ds(pl.multiple_of(i * KB, KB), KB)
        kT[:, at] = k2[at, :HD].T
        vT[:, at] = vx[at, :].T
        return 0

    lax.fori_loop(0, pl.cdiv(end, KB), turn, 0)

    def block(b, _):
        first = pl.multiple_of(b * QB, QB)
        own = pl.ds(first, QB)
        full = first // KB
        qT[...] = q2[own, :].T
        oT[...] = jnp.zeros_like(oT)
        dqT[...] = jnp.zeros_like(dqT)

        def forward(c, masked):
            at = pl.ds(pl.multiple_of(c * KB, KB), KB)
            t = jnp.tanh(dot(k2[at, :], qT[...], NN))
            e = jnp.exp2(t * (SOFT_CAP * math.log2(math.e)))
            if masked:
                key = lax.broadcasted_iota(jnp.int32, (KB, QB), 0) + c * KB
                query = lax.broadcasted_iota(jnp.int32, (KB, QB), 1) + first
                e = jnp.where(key <= query, e, 0.0)
            pb = e.astype(jnp.bfloat16)
            probs[at, :] = pb
            slopes[at, :] = (e * (1.0 - t * t)).astype(jnp.bfloat16)
            oT[...] += dot(vT[:, at], pb, NN)

        lax.fori_loop(0, full, lambda c, _: (forward(c, False), 0)[1], 0)
        forward(full, True)
        o = oT[...].T
        inv = 1.0 / o[:, HD:]
        g = gx[own, :HD].astype(jnp.float32)
        delta = jnp.sum(g * o[:, :HD], axis=1, keepdims=True) * inv
        lanes = lax.broadcasted_iota(jnp.int32, (QB, HD), 1)
        d0 = delta.astype(jnp.bfloat16).astype(jnp.float32)
        d1 = (delta - d0).astype(jnp.bfloat16).astype(jnp.float32)
        d2 = delta - d0 - d1
        gx[own, HD:] = -jnp.where(
            lanes == 0, d0, jnp.where(lanes == 1, d1, jnp.where(lanes == 2, d2, 0.0))
        ).astype(jnp.bfloat16)
        gT[...] = gx[own, :].T
        gs = (g * inv).astype(jnp.bfloat16)
        q = q2[own, :HD].astype(jnp.float32) + q2[own, HD:].astype(jnp.float32)
        qs = (q * (inv * SOFT_CAP)).astype(jnp.bfloat16)

        def backward(c, _):
            at = pl.ds(pl.multiple_of(c * KB, KB), KB)
            dp = dot(vx[at, :], gT[...], NN)
            ds = slopes[at, :] * dp.astype(jnp.bfloat16)
            dqT[...] += dot(kT[:, at], ds, NN)
            dk[at, :] += dot(ds, qs, NN)
            dv[at, :] += dot(probs[at, :], gs, NN)
            return 0

        lax.fori_loop(0, full + 1, backward, 0)
        dq[own, :] = dqT[...].T * (inv * score_scale)
        return 0

    lax.fori_loop(0, blocks, block, 0)

    def unpack(j, _):
        shard = place[1 + j]
        offset = lax.fori_loop(0, shard, lambda s, o: o + ((lens[s] + 15) // 16) * 16, jnp.int32(0))
        valid = lens[shard]
        ca, sa = cos_s[pl.ds(shard, 1), :], sin_s[pl.ds(shard, 1), :]

        def unpack_piece(i, _):
            dst = pl.multiple_of(i * piece, piece)
            src = pl.ds(pl.multiple_of(offset + i * piece, 16), piece)
            live = (lax.broadcasted_iota(jnp.int32, (piece, HD), 0) + dst) < valid
            cb, sb = cos_r[pl.ds(dst, piece), :], sin_r[pl.ds(dst, piece), :]
            cosine = ca * cb - sa * sb
            sine = sa * cb + ca * sb
            sine = jnp.where(lane < HD // 2, sine, -sine)

            def rotate(x):
                return x * cosine + pltpu.roll(x, HD // 2, 1) * sine

            to = pl.ds(pl.multiple_of(j * rows + i * piece, piece), piece)
            dq_out[to, :] = jnp.where(live, rotate(dq[src, :]), 0.0).astype(jnp.bfloat16)
            key_part = jnp.where(live, rotate(dk[src, :]), 0.0)
            value_part = jnp.where(live, dv[src, :], 0.0)
            keep_out[to, :] = jnp.where(core == 0, key_part, value_part)
            swapped = j + 1 - 2 * lax.rem(j, 2)
            to = pl.ds(pl.multiple_of(swapped * rows + i * piece, piece), piece)
            give_out[to, :] = jnp.where(core == 0, value_part, key_part).astype(jnp.bfloat16)
            return 0

        lax.fori_loop(0, rows // piece, unpack_piece, 0)
        return 0

    lax.fori_loop(0, n, unpack, 0)


def attention(place, lens, qg, mine, peer, tables, score_scale):
    n = len(qg)
    rows = qg[0].shape[0]
    tokens = n * rows
    room = tokens + 2 * KB
    bf, f32 = jnp.bfloat16, jnp.float32
    any_spec = pl.BlockSpec(memory_space=pl.ANY)
    smem = pl.BlockSpec(memory_space=pltpu.SMEM)
    vmem = pl.BlockSpec(memory_space=pltpu.VMEM)
    return pl.pallas_call(
        functools.partial(attention_kernel, n, rows, score_scale),
        out_shape=(
            jax.ShapeDtypeStruct((tokens, HD), bf),
            jax.ShapeDtypeStruct((tokens, HD), f32),
            jax.ShapeDtypeStruct((tokens, HD), bf),
        ),
        in_specs=[smem, smem] + [any_spec] * (3 * n) + [vmem] * 4,
        out_specs=(vmem, vmem, vmem),
        scratch_shapes=[
            pltpu.VMEM((n, rows, 2 * HD), bf),
            pltpu.VMEM((2, n, rows, HD), bf),
            pltpu.VMEM((room, 2 * HD), bf),
            pltpu.VMEM((room, 2 * HD), bf),
            pltpu.VMEM((HD, room), bf),
            pltpu.VMEM((room, 2 * HD), bf),
            pltpu.VMEM((room, 2 * HD), bf),
            pltpu.VMEM((2 * HD, room), bf),
            pltpu.VMEM((room, QB), bf),
            pltpu.VMEM((room, QB), bf),
            pltpu.VMEM((room, HD), f32),
            pltpu.VMEM((room, HD), f32),
            pltpu.VMEM((room, HD), f32),
            pltpu.VMEM((2 * HD, QB), f32),
            pltpu.VMEM((HD, QB), f32),
            pltpu.VMEM((2 * HD, QB), bf),
            pltpu.VMEM((2 * HD, QB), bf),
            pltpu.SemaphoreType.DMA((3, n)),
        ],
        compiler_params=pltpu.CompilerParams(vmem_limit_bytes=48 * 1024 * 1024),
        cost_estimate=pl.CostEstimate(
            flops=12 * tokens * tokens * HD, bytes_accessed=16 * tokens * HD, transcendentals=tokens * tokens
        ),
        name="attention",
    )(place, lens, *qg, *mine, *peer, *tables)


def tables(rows, shards):
    half = HD // 2
    freq = 10000.0 ** (-(jnp.arange(half, dtype=jnp.float32) * (2.0 / HD)))
    freq = jnp.concatenate([freq, freq])[None, :]
    within = jnp.arange(rows, dtype=jnp.float32)[:, None] * freq
    start = (jnp.arange(shards, dtype=jnp.float32) * rows)[:, None] * freq
    return jnp.cos(within), jnp.sin(within), jnp.cos(start), jnp.sin(start)


def pack_kernel(place, q, k, v, g, *refs):
    n = (len(refs) - 1) // 2
    qg, kv, sems = refs[:n], refs[n : 2 * n], refs[2 * n]
    copies = []
    for m in range(n):
        to = place[1 + m]
        cols = pl.ds(pl.multiple_of(to * HD, HD), HD)
        kv_cols = pl.ds(pl.multiple_of((to // 2) * HD, HD), HD)
        key_copy = pltpu.make_async_copy(k.at[:, kv_cols], kv[m], sems.at[2, m])
        value_copy = pltpu.make_async_copy(v.at[:, kv_cols], kv[m], sems.at[2, m])
        pl.when(lax.rem(to, 2) == 0)(key_copy.start)
        pl.when(lax.rem(to, 2) == 1)(value_copy.start)
        copies.append(key_copy)
    for m in range(n):
        cols = pl.ds(pl.multiple_of(place[1 + m] * HD, HD), HD)
        for which, src in ((0, q), (1, g)):
            copy = pltpu.make_async_copy(src.at[:, cols], qg[m].at[:, pl.ds(which * HD, HD)], sems.at[which, m])
            copy.start()
            copies.append(copy)
    for copy in copies:
        copy.wait()


def pack(place, q, k, v, g, n):
    rows = q.shape[0]
    any_spec = pl.BlockSpec(memory_space=pl.ANY)
    out = pl.pallas_call(
        pack_kernel,
        out_shape=[jax.ShapeDtypeStruct((rows, 2 * HD), q.dtype)] * n + [jax.ShapeDtypeStruct((rows, HD), q.dtype)] * n,
        in_specs=[pl.BlockSpec(memory_space=pltpu.SMEM)] + [any_spec] * 4,
        out_specs=[any_spec] * (2 * n),
        scratch_shapes=[pltpu.SemaphoreType.DMA((3, n))],
        name="pack",
    )(place, q, k, v, g)
    return out[:n], out[n:]


def line_up_kernel(place, *refs):
    n = (len(refs) - 2) // 2
    left, right = refs[:n], refs[n : 2 * n]
    out, sems = refs[2 * n :]
    copies = []
    for m in range(n):
        chip = place[1 + 2 * m] // 2
        for which, src in ((0, left), (1, right)):
            cols = pl.ds(pl.multiple_of((which * n + chip) * HD, HD), HD)
            copies.append(pltpu.make_async_copy(src[m], out.at[:, cols], sems.at[which, m]))
    for copy in copies:
        copy.start()
    for copy in copies:
        copy.wait()


def line_up(place, left, right):
    n = len(left)
    any_spec = pl.BlockSpec(memory_space=pl.ANY)
    return pl.pallas_call(
        line_up_kernel,
        out_shape=jax.ShapeDtypeStruct((left[0].shape[0], 2 * n * HD), left[0].dtype),
        in_specs=[pl.BlockSpec(memory_space=pltpu.SMEM)] + [any_spec] * (2 * n),
        out_specs=any_spec,
        scratch_shapes=[pltpu.SemaphoreType.DMA((2, n))],
        name="line_up",
    )(place, *left, *right)


def swap(value, axis, by):
    size = lax.axis_size(axis)
    return lax.ppermute(value, axis, [(i, i ^ by) for i in range(size)])


def middle_swap(value):
    return lax.ppermute(value, "head", [(0, 0), (1, 2), (2, 1), (3, 3)])


def wide(value):
    return value.astype(jnp.float32)


def interleave(even, odd):
    rows, width = even.shape
    pair = jnp.stack([even.reshape(rows, width // HD, HD), odd.reshape(rows, width // HD, HD)], axis=2)
    return pair.reshape(rows, 2 * width)


BLOCK_ORDER = ((3, 2, 1, 0), (0, 3, 2, 1), (3, 0, 1, 2), (0, 1, 2, 3))


def block_body(queries, keys, values, out_grad, normed, w_query, w_key, w_value, valid_len):
    bf = jnp.bfloat16
    seq_size = lax.axis_size("seq")
    rows = queries.shape[0]
    score_scale = (D // H) ** (-0.5)
    me = lax.axis_index("seq")
    core = me % 2
    chip = me // 2
    level = lax.axis_index("head")
    chips = seq_size // 2
    place = jnp.stack([me] + [me ^ m for m in range(seq_size)]).astype(jnp.int32)

    qg, kv = pack(place, queries, keys, values, out_grad, seq_size)
    kv = [kv[0]] + [swap(kv[m], "seq", m) for m in range(1, seq_size)]
    qg = [qg[0]] + [swap(qg[m], "seq", m) for m in range(1, seq_size)]
    kv_peer = [swap(kv[m ^ 1], "seq", 1) for m in range(seq_size)]
    normed_pair = jnp.concatenate([normed, swap(normed, "seq", 1)], axis=0)

    width = normed.shape[1]
    own_rows = width // seq_size
    turned = normed_pair.T
    strips = []
    for m in range(chips):
        first = (chip ^ m) * 2
        strips.append(
            jnp.concatenate(
                [
                    lax.dynamic_slice_in_dim(turned, (first + core) * own_rows, own_rows, 0),
                    lax.dynamic_slice_in_dim(turned, (first + 1 - core) * own_rows, own_rows, 0),
                ],
                axis=0,
            )
        )
    strips = lax.optimization_barrier(strips)

    dq, keep, give = attention(place, valid_len, qg, kv, kv_peer, tables(rows, seq_size), score_scale)
    dkv = (keep + wide(swap(give, "seq", 1))).astype(bf)
    dq_parts = [dq[2 * rows * m : 2 * rows * (m + 1)] for m in range(chips)]
    dkv_parts = [dkv[2 * rows * m : 2 * rows * (m + 1)] for m in range(chips)]
    dq_parts = [dq_parts[0]] + [swap(dq_parts[m], "seq", 2 * m) for m in range(1, chips)]
    dkv_parts = [dkv_parts[0]] + [swap(dkv_parts[m], "seq", 2 * m) for m in range(1, chips)]
    lined = line_up(place, dq_parts, dkv_parts)
    half = chips * HD

    mine = lined[:rows]
    other = swap(lined[rows:], "seq", 1)
    even = jnp.where(core == 0, mine, other)
    odd = jnp.where(core == 0, other, mine)
    dq_own = interleave(even[:, :half], odd[:, :half])
    dk_own, dv_own = even[:, half:], odd[:, half:]

    block_width = width // lax.axis_size("head")
    order = jnp.array(BLOCK_ORDER, jnp.int32)
    parts = []
    for i in range(len(BLOCK_ORDER)):
        at = order[level, i] * block_width
        cut = [lax.dynamic_slice_in_dim(w, at, block_width, 0) for w in (w_query, w_key, w_value)]
        parts.append(times_t(dq_own, cut[0]) + times_t(dk_own, cut[1]) + times_t(dv_own, cut[2]))
    inner = (level == 1) | (level == 2)
    first_in = swap(parts[0].astype(bf), "head", 1)
    second_out, first_in = lax.optimization_barrier((parts[1].astype(bf), first_in))
    second_in = swap(second_out, "head", 1)
    first_mid = middle_swap((parts[1] + wide(first_in)).astype(bf))
    second_mid = middle_swap((parts[2] + wide(second_in)).astype(bf))
    third_in = swap(jnp.where(inner, first_mid, parts[2].astype(bf)), "head", 1)
    grad_x = (parts[3] + wide(third_in) + wide(jnp.where(inner, second_mid, first_in))).astype(bf)

    left = [jnp.dot(strips[m], lined[:, :half], preferred_element_type=jnp.float32) for m in range(chips)]
    right = [jnp.dot(strips[m], lined[:, half:], preferred_element_type=jnp.float32) for m in range(chips)]
    left3, left1 = swap(left[3].astype(bf), "seq", 2), swap(left[1].astype(bf), "seq", 2)
    right3, right2 = swap(right[3].astype(bf), "seq", 4), swap(right[2].astype(bf), "seq", 4)
    left_last = swap((left[2] + wide(left3)).astype(bf), "seq", 4)
    right_last = swap((right[1] + wide(right3)).astype(bf), "seq", 2)
    left_sum = (left[0] + wide(left1) + wide(left_last)).astype(bf)
    right_sum = (right[0] + wide(right2) + wide(right_last)).astype(bf)
    left_other = swap(left_sum[own_rows:], "seq", 1)
    right_other = swap(right_sum[own_rows:], "seq", 1)
    left_mine, right_mine = left_sum[:own_rows], right_sum[:own_rows]
    grad_wq = interleave(jnp.where(core == 0, left_mine, left_other), jnp.where(core == 0, left_other, left_mine))
    grad_wk = jnp.where(core == 0, right_mine, right_other)
    grad_wv = jnp.where(core == 0, right_other, right_mine)
    return (grad_x, grad_wq, grad_wk, grad_wv)


def solution(mesh):
    square = mesh.shape["seq"] == 8 and mesh.shape["head"] == 4
    body = block_body if square else general_body
    placed = (
        P("seq", "head"),
        P("seq", "head"),
        P("seq", "head"),
        P("seq", "head"),
        P("seq", None),
        P(None, "head"),
        P(None, "head"),
        P(None, "head"),
        P(),
    )
    return jax.shard_map(
        body,
        mesh=mesh,
        in_specs=placed,
        out_specs=(P("seq", "head"), P("seq", "head"), P("seq", "head"), P("seq", "head")),
        check_vma=False,
    )
```

```python
import functools
import math

import jax
import jax.numpy as jnp
from jax import lax
from jax.experimental import pallas as pl
from jax.experimental.pallas import tpu as pltpu
from jax.sharding import PartitionSpec as P

D = 4608
H = 32
HD = 128
WINDOW = 4096


SOFT_CAP = 50.0
ROPE_BASE = 10000.0


def passed_along(value, axis, by):
    size = lax.axis_size(axis)
    pairs = [(i, i + by) for i in range(size) if 0 <= i + by < size]
    return lax.ppermute(value, axis, pairs)


def rotate_back(gradient, positions, head_count):
    row_count = gradient.shape[0]
    half_width = HD // 2
    inverse_freq = ROPE_BASE ** (-(jnp.arange(half_width, dtype=jnp.float32) * (2.0 / HD)))
    angles = positions.astype(jnp.float32)[:, None] * inverse_freq[None, :]
    cosine = jnp.cos(angles)[:, None, :]
    sine_part = jnp.sin(angles)[:, None, :]
    per_head = gradient.reshape(row_count, head_count, HD)
    leading = per_head[:, :, :half_width]
    trailing = per_head[:, :, half_width:]
    rotated = jnp.concatenate(
        [leading * cosine + trailing * sine_part, trailing * cosine - leading * sine_part], axis=2
    )
    return rotated.reshape(row_count, head_count * HD)


def times_t(left, right):
    return lax.dot_general(
        left, right, (((1,), (1,)), ((), ())), preferred_element_type=jnp.float32
    )


def inner_rows(left, right):
    return lax.dot_general(
        left, right, (((0,), (0,)), ((), ())), preferred_element_type=jnp.float32
    )


def general_body(queries, keys, values, out_grad, normed, w_query, w_key, w_value, valid_len):
    row_count = queries.shape[0]
    kv_heads = keys.shape[1] // HD
    head_count = queries.shape[1] // HD
    group_size = head_count // kv_heads
    kv_width = kv_heads * HD
    hop_count = WINDOW // row_count
    score_scale = (D // H) ** (-0.5)
    shard_index = lax.axis_index("seq")
    last_shard = valid_len.shape[0] - 1
    row_iota = jnp.arange(row_count, dtype=jnp.int32)
    query_pos = shard_index * row_count + row_iota
    own_valid = row_iota < valid_len[shard_index]
    grad_rows = jnp.where(own_valid[:, None], out_grad, jnp.zeros_like(out_grad))
    query_blocks = queries.reshape(row_count, kv_heads, group_size, HD)
    grad_blocks = grad_rows.reshape(row_count, kv_heads, group_size, HD)
    key_value = jnp.concatenate([keys, values], axis=1)
    arrived = [key_value]
    moving = key_value
    for distance in range(1, hop_count + 1):
        moving = passed_along(moving, "seq", 1)
        arrived.append(moving)
    allowed_list = []
    capped_list = []
    running = jnp.zeros((kv_heads, group_size, row_count), jnp.float32)
    for distance in range(hop_count + 1):
        key_pos = (shard_index - distance) * row_count + row_iota
        owner = jnp.clip(shard_index - distance, 0, last_shard)
        key_valid = row_iota < valid_len[owner]
        offset_gap = query_pos[:, None] - key_pos[None, :]
        allowed = (
            (offset_gap >= 0)
            & (offset_gap < WINDOW)
            & (key_pos[None, :] >= 0)
            & (key_valid[None, :] | (offset_gap == 0))
        )
        key_block = arrived[distance][:, :kv_width].reshape(row_count, kv_heads, HD)
        raw_scores = (
            jnp.einsum(
                "qhgd,khd->hgqk", query_blocks, key_block, preferred_element_type=jnp.float32
            )
            * score_scale
        )
        capped = SOFT_CAP * jnp.tanh(raw_scores / SOFT_CAP)
        running = running + jnp.sum(jnp.where(allowed, jnp.exp(capped), 0.0), axis=-1)
        allowed_list.append(allowed)
        capped_list.append(capped)
    log_total = jnp.log(running)[..., None]
    attended = jnp.zeros((row_count, kv_heads, group_size, HD), jnp.float32)
    for distance in range(hop_count + 1):
        value_block = arrived[distance][:, kv_width:].reshape(row_count, kv_heads, HD)
        rounded = jnp.where(
            allowed_list[distance], jnp.exp(capped_list[distance] - log_total), 0.0
        ).astype(jnp.bfloat16)
        attended = attended + jnp.einsum(
            "hgqk,khd->qhgd", rounded, value_block, preferred_element_type=jnp.float32
        )
    row_delta = jnp.sum(grad_blocks.astype(jnp.float32) * attended, axis=-1)
    delta_cols = jnp.transpose(row_delta, (1, 2, 0))[..., None]
    query_grad = jnp.zeros((row_count, kv_heads, group_size, HD), jnp.float32)
    partials = [None] * (hop_count + 1)
    for distance in range(hop_count, -1, -1):
        key_block = arrived[distance][:, :kv_width].reshape(row_count, kv_heads, HD)
        value_block = arrived[distance][:, kv_width:].reshape(row_count, kv_heads, HD)
        capped = capped_list[distance]
        exact = jnp.where(allowed_list[distance], jnp.exp(capped - log_total), 0.0)
        rounded = exact.astype(jnp.bfloat16)
        grad_probs = jnp.einsum(
            "qhgd,khd->hgqk", grad_blocks, value_block, preferred_element_type=jnp.float32
        )
        grad_scores = (exact * (grad_probs - delta_cols) * (1.0 - (capped / SOFT_CAP) ** 2)).astype(
            jnp.bfloat16
        )
        query_grad = (
            query_grad
            + jnp.einsum(
                "hgqk,khd->qhgd", grad_scores, key_block, preferred_element_type=jnp.float32
            )
            * score_scale
        )
        key_grad = (
            jnp.einsum(
                "hgqk,qhgd->khd", grad_scores, query_blocks, preferred_element_type=jnp.float32
            )
            * score_scale
        )
        value_grad = jnp.einsum(
            "hgqk,qhgd->khd", rounded, grad_blocks, preferred_element_type=jnp.float32
        )
        partials[distance] = jnp.concatenate(
            [key_grad.reshape(row_count, kv_width), value_grad.reshape(row_count, kv_width)], axis=1
        )
    carried = partials[hop_count]
    for distance in range(hop_count - 1, -1, -1):
        carried = (
            passed_along(carried.astype(jnp.bfloat16), "seq", -1).astype(carried.dtype)
            + partials[distance]
        )
    query_pre = rotate_back(
        query_grad.reshape(row_count, head_count * HD), query_pos, head_count
    ).astype(jnp.bfloat16)
    key_pre = rotate_back(carried[:, :kv_width], query_pos, kv_heads).astype(jnp.bfloat16)
    value_pre = carried[:, kv_width:].astype(jnp.bfloat16)
    input_terms = (
        times_t(query_pre, w_query) + times_t(key_pre, w_key) + times_t(value_pre, w_value)
    )
    grad_x = lax.psum_scatter(
        input_terms.astype(jnp.bfloat16), "head", scatter_dimension=1, tiled=True
    )
    stacked = jnp.concatenate([query_pre, key_pre, value_pre], axis=1)
    weight_total = lax.psum_scatter(
        inner_rows(normed, stacked).astype(jnp.bfloat16), "seq", scatter_dimension=0, tiled=True
    ).astype(jnp.float32)
    query_cols = head_count * HD
    grad_wq = weight_total[:, :query_cols].astype(jnp.bfloat16)
    grad_wk = weight_total[:, query_cols : query_cols + kv_width].astype(jnp.bfloat16)
    grad_wv = weight_total[:, query_cols + kv_width :].astype(jnp.bfloat16)
    return (grad_x, grad_wq, grad_wk, grad_wv)
QB = 512
KB = 512
PACK_ROWS = 128
SHARE_COLS = 384
MIB = 1024 * 1024
NT = (((1,), (1,)), ((), ()))
NN = (((1,), (0,)), ((), ()))


def dot(a, b, dims):
    return lax.dot_general(a, b, dims, preferred_element_type=jnp.float32)


def attention_kernel(shards, rows, score_scale, place, lens, *refs):
    n = shards
    qg_in = refs[:n]
    mine_in, peer_in = refs[n], refs[n + 1]
    cos_r, sin_r, cos_s, sin_s = refs[n + 2 : n + 6]
    dq_out, keep_out, give_out = refs[n + 6 : n + 9]
    (q2, k2, kT, gx, vx, alive, probs, slopes, dps, dq, dk, dv, dqT, qT, gT, sems) = refs[n + 9 :]
    me = place[0]
    core = lax.rem(me, 2)
    copies = []
    for m in range(n):
        to = pl.ds(pl.multiple_of(place[1 + m] * rows, rows), rows)
        mine_at = pl.ds(pl.multiple_of((2 + core) * HD, HD), HD)
        peer_at = pl.ds(pl.multiple_of((3 - core) * HD, HD), HD)
        copies.append(pltpu.make_async_copy(qg_in[m], probs.at[to, pl.ds(0, 2 * HD)], sems.at[0, m]))
        copies.append(pltpu.make_async_copy(mine_in.at[m], probs.at[to, mine_at], sems.at[1, m]))
        copies.append(pltpu.make_async_copy(peer_in.at[m ^ 1], probs.at[to, peer_at], sems.at[2, m]))
    for copy in copies:
        copy.start()
    total_rows = n * rows
    dk[...] = jnp.zeros_like(dk)
    dv[...] = jnp.zeros_like(dv)
    for copy in copies:
        copy.wait()

    piece = 128
    lane = lax.broadcasted_iota(jnp.int32, (piece, HD), 1)

    def pack_shard(shard, offset):
        valid = lens[shard]

        def pack_piece(i, _):
            src = pl.multiple_of(i * piece, piece)
            dst = pl.multiple_of(offset + i * piece, 16)
            live = (lax.broadcasted_iota(jnp.int32, (piece, HD), 0) + src) < valid
            at = pl.ds(pl.multiple_of(shard * rows + src, piece), piece)
            to = pl.ds(dst, piece)
            q = jnp.where(live, probs[at, :HD].astype(jnp.float32), 0.0) * (score_scale / SOFT_CAP)
            hi = q.astype(jnp.bfloat16)
            q2[to, :HD] = hi
            q2[to, HD:] = (q - hi.astype(jnp.float32)).astype(jnp.bfloat16)
            zero = jnp.zeros((piece, HD), jnp.bfloat16)
            gx[to, :] = jnp.where(live, probs[at, HD : 2 * HD], zero)
            k = jnp.where(live, probs[at, 2 * HD : 3 * HD], zero)
            k2[to, :HD] = k
            k2[to, HD:] = k
            vx[to, :] = jnp.where(live, probs[at, 3 * HD : 4 * HD], zero)
            alive[to, :] = jnp.where(live, 1.0, 0.0)
            return 0

        lax.fori_loop(0, rows // piece, pack_piece, 0)
        return offset + ((valid + 15) // 16) * 16

    end = lax.fori_loop(0, n, pack_shard, jnp.int32(0))
    tail = pl.ds(pl.multiple_of(end, 16), KB)
    for ref in (q2, k2, gx, vx, alive):
        ref[tail, :] = jnp.zeros((KB, ref.shape[1]), ref.dtype)
    blocks = pl.cdiv(end, QB)

    def turn(i, _):
        at = pl.ds(pl.multiple_of(i * KB, KB), KB)
        kT[:, at] = k2[at, :HD].T
        return 0

    lax.fori_loop(0, pl.cdiv(end, KB), turn, 0)

    def block(b, _):
        first = pl.multiple_of(b * QB, QB)
        own = pl.ds(first, QB)
        full = first // KB
        qT[...] = q2[own, :].T
        gT[...] = gx[own, :].T
        dqT[...] = jnp.zeros_like(dqT)

        def forward(c, sums, masked):
            at = pl.ds(pl.multiple_of(c * KB, KB), KB)
            t = jnp.tanh(dot(k2[at, :], qT[...], NN))
            dp = dot(vx[at, :], gT[...], NN)
            e = jnp.exp2(t * (SOFT_CAP * math.log2(math.e)))
            e = e * jnp.concatenate([alive[at, :]] * (QB // HD), axis=1)
            if masked:
                key = lax.broadcasted_iota(jnp.int32, (KB, QB), 0) + c * KB
                query = lax.broadcasted_iota(jnp.int32, (KB, QB), 1) + first
                e = jnp.where(key <= query, e, 0.0)
            probs[at, :] = e.astype(jnp.bfloat16)
            slopes[at, :] = (e * (1.0 - t * t)).astype(jnp.bfloat16)
            dps[at, :] = dp
            total, weighted = sums
            return total + jnp.sum(e, axis=0, keepdims=True), weighted + jnp.sum(e * dp, axis=0, keepdims=True)

        zero = jnp.zeros((1, QB), jnp.float32)
        sums = lax.fori_loop(0, full, lambda c, sums: forward(c, sums, False), (zero, zero))
        total, weighted = forward(full, sums, True)
        inv = 1.0 / total
        delta = weighted * inv
        gs = (gT[...].astype(jnp.float32) * inv).astype(jnp.bfloat16).T
        q = qT[:HD, :].astype(jnp.float32) + qT[HD:, :].astype(jnp.float32)
        qs = (q * (inv * SOFT_CAP)).astype(jnp.bfloat16).T

        def backward(c, _):
            at = pl.ds(pl.multiple_of(c * KB, KB), KB)
            ds = slopes[at, :] * (dps[at, :] - delta).astype(jnp.bfloat16)
            dqT[...] += dot(kT[:, at], ds, NN)
            dk[at, :] += dot(ds, qs, NN)
            dv[at, :] += dot(probs[at, :], gs, NN)
            return 0

        lax.fori_loop(0, full + 1, backward, 0)
        dq[own, :] = (dqT[...] * (inv * score_scale)).T
        return 0

    lax.fori_loop(0, blocks, block, 0)

    def unpack(j, _):
        shard = place[1 + j]
        offset = lax.fori_loop(0, shard, lambda s, o: o + ((lens[s] + 15) // 16) * 16, jnp.int32(0))
        valid = lens[shard]
        ca, sa = cos_s[pl.ds(shard, 1), :], sin_s[pl.ds(shard, 1), :]

        def unpack_piece(i, _):
            dst = pl.multiple_of(i * piece, piece)
            src = pl.ds(pl.multiple_of(offset + i * piece, 16), piece)
            live = (lax.broadcasted_iota(jnp.int32, (piece, HD), 0) + dst) < valid
            cb, sb = cos_r[pl.ds(dst, piece), :], sin_r[pl.ds(dst, piece), :]
            cosine = ca * cb - sa * sb
            sine = sa * cb + ca * sb
            sine = jnp.where(lane < HD // 2, sine, -sine)

            def rotate(x):
                return x * cosine + pltpu.roll(x, HD // 2, 1) * sine

            to = pl.ds(pl.multiple_of(j * rows + i * piece, piece), piece)
            dq_out[to, :] = jnp.where(live, rotate(dq[src, :]), 0.0).astype(jnp.bfloat16)
            key_part = jnp.where(live, rotate(dk[src, :]), 0.0)
            value_part = jnp.where(live, dv[src, :], 0.0)
            keep_out[to, :] = jnp.where(core == 0, key_part, value_part)
            swapped = j + 1 - 2 * lax.rem(j, 2)
            to = pl.ds(pl.multiple_of(swapped * rows + i * piece, piece), piece)
            give_out[to, :] = jnp.where(core == 0, value_part, key_part).astype(jnp.bfloat16)
            return 0

        lax.fori_loop(0, rows // piece, unpack_piece, 0)
        return 0

    lax.fori_loop(0, n, unpack, 0)


def attention(place, lens, qg, mine, peer, tables, score_scale):
    n = len(qg)
    rows = qg[0].shape[0]
    tokens = n * rows
    room = tokens + KB
    bf, f32 = jnp.bfloat16, jnp.float32
    any_spec = pl.BlockSpec(memory_space=pl.ANY)
    smem = pl.BlockSpec(memory_space=pltpu.SMEM)
    vmem = pl.BlockSpec(memory_space=pltpu.VMEM)
    return pl.pallas_call(
        functools.partial(attention_kernel, n, rows, score_scale),
        out_shape=(
            jax.ShapeDtypeStruct((tokens, HD), bf),
            jax.ShapeDtypeStruct((tokens, HD), f32),
            jax.ShapeDtypeStruct((tokens, HD), bf),
        ),
        in_specs=[smem, smem] + [any_spec] * (n + 2) + [vmem] * 4,
        out_specs=(vmem, vmem, vmem),
        scratch_shapes=[
            pltpu.VMEM((room, 2 * HD), bf),
            pltpu.VMEM((room, 2 * HD), bf),
            pltpu.VMEM((HD, room), bf),
            pltpu.VMEM((room, HD), bf),
            pltpu.VMEM((room, HD), bf),
            pltpu.VMEM((room, HD), f32),
            pltpu.VMEM((room, QB), bf),
            pltpu.VMEM((room, QB), bf),
            pltpu.VMEM((room, QB), f32),
            pltpu.VMEM((room, HD), f32),
            pltpu.VMEM((room, HD), f32),
            pltpu.VMEM((room, HD), f32),
            pltpu.VMEM((HD, QB), f32),
            pltpu.VMEM((2 * HD, QB), bf),
            pltpu.VMEM((HD, QB), bf),
            pltpu.SemaphoreType.DMA((3, n)),
        ],
        compiler_params=pltpu.CompilerParams(vmem_limit_bytes=46 * MIB),
        cost_estimate=pl.CostEstimate(
            flops=12 * tokens * tokens * HD, bytes_accessed=16 * tokens * HD, transcendentals=tokens * tokens
        ),
        name="attention",
    )(place, lens, *qg, mine, peer, *tables)


def tables(rows, shards):
    half = HD // 2
    freq = 10000.0 ** (-(jnp.arange(half, dtype=jnp.float32) * (2.0 / HD)))
    freq = jnp.concatenate([freq, freq])[None, :]
    within = jnp.arange(rows, dtype=jnp.float32)[:, None] * freq
    start = (jnp.arange(shards, dtype=jnp.float32) * rows)[:, None] * freq
    return jnp.cos(within), jnp.sin(within), jnp.cos(start), jnp.sin(start)


def pack_kernel(place, q, k, v, g, *refs):
    n = len(refs) // 2
    qg, kv = refs[:n], refs[n:]
    for m in range(n):
        to = place[1 + m]
        cols = pl.ds(pl.multiple_of(to * HD, HD), HD)
        kv_cols = pl.ds(pl.multiple_of((to // 2) * HD, HD), HD)
        qg[m][:, :HD] = q[:, cols]
        qg[m][:, HD:] = g[:, cols]
        kv[m][...] = jnp.where(lax.rem(to, 2) == 0, k[:, kv_cols], v[:, kv_cols])


def pack(place, q, k, v, g, n):
    rows = q.shape[0]
    out = pl.pallas_call(
        pack_kernel,
        out_shape=[jax.ShapeDtypeStruct((rows, 2 * HD), q.dtype)] * n + [jax.ShapeDtypeStruct((rows, HD), q.dtype)] * n,
        grid=(rows // PACK_ROWS,),
        in_specs=[pl.BlockSpec(memory_space=pltpu.SMEM)]
        + [pl.BlockSpec((PACK_ROWS, x.shape[1]), lambda i: (i, 0)) for x in (q, k, v, g)],
        out_specs=[pl.BlockSpec((PACK_ROWS, w), lambda i: (i, 0)) for w in [2 * HD] * n + [HD] * n],
        compiler_params=pltpu.CompilerParams(vmem_limit_bytes=8 * MIB),
        name="pack",
    )(place, q, k, v, g)
    return out[:n], out[n:]


def line_up_kernel(place, *refs):
    n = (len(refs) - 1) // 2
    left, right, out = refs[:n], refs[n : 2 * n], refs[2 * n]
    for m in range(n):
        chip = place[1 + 2 * m] // 2
        for which, src in ((0, left), (1, right)):
            cols = pl.ds(pl.multiple_of((which * n + chip) * HD, HD), HD)
            out[:, cols] = src[m][...]


def line_up(place, left, right):
    n = len(left)
    vmem = pl.BlockSpec(memory_space=pltpu.VMEM)
    return pl.pallas_call(
        line_up_kernel,
        out_shape=jax.ShapeDtypeStruct((left[0].shape[0], 2 * n * HD), left[0].dtype),
        in_specs=[pl.BlockSpec(memory_space=pltpu.SMEM)] + [vmem] * (2 * n),
        out_specs=vmem,
        compiler_params=pltpu.CompilerParams(vmem_limit_bytes=8 * MIB),
        name="line_up",
    )(place, *left, *right)


def finish_kernel(place, *refs):
    left_mine, left_last, left_other, left_cross = refs[:4]
    right_mine, right_last, right_other, right_cross = refs[4:8]
    grad_wq, grad_wk, grad_wv = refs[8:]
    core = lax.rem(place[0], 2)
    half = left_mine.shape[1]

    def add(a, b, cols):
        return (a[:, cols].astype(jnp.float32) + b[:, cols].astype(jnp.float32)).astype(jnp.bfloat16)

    for h in range(half // HD):
        cols = slice(h * HD, (h + 1) * HD)
        mine, other = add(left_mine, left_last, cols), add(left_other, left_cross, cols)
        grad_wq[:, 2 * h * HD : (2 * h + 1) * HD] = jnp.where(core == 0, mine, other)
        grad_wq[:, (2 * h + 1) * HD : (2 * h + 2) * HD] = jnp.where(core == 0, other, mine)
        mine, other = add(right_mine, right_last, cols), add(right_other, right_cross, cols)
        grad_wk[:, cols] = jnp.where(core == 0, mine, other)
        grad_wv[:, cols] = jnp.where(core == 0, other, mine)


def finish(place, *shares):
    rows, half = shares[0].shape
    vmem = pl.BlockSpec(memory_space=pltpu.VMEM)
    return pl.pallas_call(
        finish_kernel,
        out_shape=[jax.ShapeDtypeStruct((rows, w), jnp.bfloat16) for w in (2 * half, half, half)],
        in_specs=[pl.BlockSpec(memory_space=pltpu.SMEM)] + [vmem] * 8,
        out_specs=[vmem] * 3,
        compiler_params=pltpu.CompilerParams(vmem_limit_bytes=12 * MIB),
        name="finish",
    )(place, *shares)


def swap(value, axis, by):
    size = lax.axis_size(axis)
    return lax.ppermute(value, axis, [(i, i ^ by) for i in range(size)])


def middle_swap(value):
    return lax.ppermute(value, "head", [(1, 2), (2, 1)])


def wide(value):
    return value.astype(jnp.float32)


def turn_kernel(place, own, peer, out):
    core = lax.rem(place[0], 2)
    rows = own.shape[0]
    strip = out.shape[0] // 2
    for which, src in ((0, own), (1, peer)):
        cols = slice(which * rows, (which + 1) * rows)
        turned = src[...].T

        @pl.when(core == 0)
        def _():
            out[:, cols] = turned

        @pl.when(core == 1)
        def _():
            out[:strip, cols] = turned[strip:]
            out[strip:, cols] = turned[:strip]


def turn(place, own, peer, m, strip):
    rows = own.shape[0]
    spec = pl.BlockSpec((rows, strip), lambda i, place: (0, place[1 + 2 * m] // 2))
    return pl.pallas_call(
        turn_kernel,
        out_shape=jax.ShapeDtypeStruct((strip, 2 * rows), own.dtype),
        grid_spec=pltpu.PrefetchScalarGridSpec(
            num_scalar_prefetch=1,
            grid=(1,),
            in_specs=[spec, spec],
            out_specs=pl.BlockSpec((strip, 2 * rows), lambda i, place: (0, 0)),
        ),
        compiler_params=pltpu.CompilerParams(vmem_limit_bytes=16 * MIB),
        name="turn",
    )(place, own, peer)


def share_kernel(at, mine, other, w_query, w_key, w_value, out, x):
    core = at[1]
    half = mine.shape[1] // 2

    @pl.when(pl.program_id(0) == 0)
    def _():
        for h in range(half // HD):
            cols = slice(h * HD, (h + 1) * HD)
            x[:, pl.ds(pl.multiple_of((2 * h + core) * HD, HD), HD)] = mine[:, cols]
            x[:, pl.ds(pl.multiple_of((2 * h + 1 - core) * HD, HD), HD)] = other[:, cols]
        x[:, pl.ds(pl.multiple_of((2 + core) * half, HD), half)] = mine[:, half:]
        x[:, pl.ds(pl.multiple_of((3 - core) * half, HD), half)] = other[:, half:]

    total = dot(x[:, : 2 * half], w_query[...], NT)
    total += dot(x[:, 2 * half : 3 * half], w_key[...], NT)
    total += dot(x[:, 3 * half :], w_value[...], NT)
    out[...] = total.astype(out.dtype)


def share(at, mine, other, w_query, w_key, w_value, width):
    rows, cols = mine.shape
    steps = width // SHARE_COLS
    whole = pl.BlockSpec((rows, cols), lambda j, at: (0, 0))
    return pl.pallas_call(
        share_kernel,
        out_shape=jax.ShapeDtypeStruct((rows, width), mine.dtype),
        grid_spec=pltpu.PrefetchScalarGridSpec(
            num_scalar_prefetch=1,
            grid=(steps,),
            in_specs=[whole, whole]
            + [pl.BlockSpec((SHARE_COLS, w.shape[1]), lambda j, at: (at[0] * steps + j, 0)) for w in (w_query, w_key, w_value)],
            out_specs=pl.BlockSpec((rows, SHARE_COLS), lambda j, at: (0, j)),
            scratch_shapes=[pltpu.VMEM((rows, 2 * cols), mine.dtype)],
        ),
        compiler_params=pltpu.CompilerParams(vmem_limit_bytes=14 * MIB),
        cost_estimate=pl.CostEstimate(flops=4 * rows * cols * width, bytes_accessed=4 * cols * width, transcendentals=0),
        name="share",
    )(at, mine, other, w_query, w_key, w_value)


BLOCK_ORDER = ((3, 2, 1, 0), (0, 3, 2, 1), (3, 0, 1, 2), (0, 1, 2, 3))


def block_body(queries, keys, values, out_grad, normed, w_query, w_key, w_value, valid_len):
    bf = jnp.bfloat16
    seq_size = lax.axis_size("seq")
    rows = queries.shape[0]
    score_scale = (D // H) ** (-0.5)
    me = lax.axis_index("seq")
    core = me % 2
    chip = me // 2
    level = lax.axis_index("head")
    chips = seq_size // 2
    place = jnp.stack([me] + [me ^ m for m in range(seq_size)]).astype(jnp.int32)

    qg, kv = pack(place, queries, keys, values, out_grad, seq_size)
    normed_peer = swap(normed, "seq", 1)
    kv = jnp.stack([kv[0]] + [swap(kv[m], "seq", m) for m in range(1, seq_size)])
    kv_peer = swap(kv, "seq", 1)
    normed, normed_peer, kv = lax.optimization_barrier((normed, normed_peer, kv))
    qg = [qg[0]] + [swap(qg[m], "seq", m) for m in range(1, seq_size)]
    width = normed.shape[1]
    own_rows = width // seq_size
    strips = [turn(place, normed, normed_peer, m, 2 * own_rows) for m in range(chips)]
    strips, qg, kv_peer = lax.optimization_barrier((strips, qg, kv_peer))

    dq, keep, give = attention(place, valid_len, qg, kv, kv_peer, tables(rows, seq_size), score_scale)
    dkv = (keep + wide(swap(give, "seq", 1))).astype(bf)
    dq_parts = [dq[2 * rows * m : 2 * rows * (m + 1)] for m in range(chips)]
    dkv_parts = [dkv[2 * rows * m : 2 * rows * (m + 1)] for m in range(chips)]
    dq_parts = [dq_parts[0]] + [swap(dq_parts[m], "seq", 2 * m) for m in range(1, chips)]
    dkv_parts = [dkv_parts[0]] + [swap(dkv_parts[m], "seq", 2 * m) for m in range(1, chips)]
    lined = line_up(place, dq_parts, dkv_parts)
    half = chips * HD

    mine = lined[:rows]
    other = swap(lined[rows:], "seq", 1)
    block_width = width // lax.axis_size("head")
    order = jnp.array(BLOCK_ORDER, jnp.int32)[level]
    parts = [
        share(jnp.stack([order[i], core]).astype(jnp.int32), mine, other, w_query, w_key, w_value, block_width)
        for i in range(len(BLOCK_ORDER))
    ]
    left = [jnp.dot(strips[m], lined[:, :half], preferred_element_type=jnp.float32) for m in range(chips)]
    right = [jnp.dot(strips[m], lined[:, half:], preferred_element_type=jnp.float32) for m in range(chips)]
    inner = (level == 1) | (level == 2)

    first_in = swap(parts[0], "head", 1)
    left3, right3 = swap(left[3].astype(bf), "seq", 2), swap(right[3].astype(bf), "seq", 4)
    left1, right2 = swap(left[1].astype(bf), "seq", 2), swap(right[2].astype(bf), "seq", 4)
    first_in, second_out = lax.optimization_barrier((first_in, parts[1]))
    second_in = swap(second_out, "head", 1)
    first_mid = middle_swap((wide(second_out) + wide(first_in)).astype(bf))
    second_in, first_mid, left3, right3, third = lax.optimization_barrier((second_in, first_mid, left3, right3, parts[2]))
    left_out = (left[2] + wide(left3)).astype(bf)
    right_out = (right[1] + wide(right3)).astype(bf)
    third_in = swap(jnp.where(inner, first_mid, third), "head", 1)
    left_last, left_cross = swap(left_out[:own_rows], "seq", 4), swap(left_out[own_rows:], "seq", 5)
    right_last, right_cross = swap(right_out[:own_rows], "seq", 2), swap(right_out[own_rows:], "seq", 3)
    second_mid = middle_swap((wide(third) + wide(second_in)).astype(bf))
    grad_x = (wide(parts[3]) + wide(third_in) + wide(jnp.where(inner, second_mid, first_in))).astype(bf)

    left_sum = (left[0] + wide(left1)).astype(bf)
    right_sum = (right[0] + wide(right2)).astype(bf)
    left_other = swap(left_sum[own_rows:], "seq", 1)
    right_other = swap(right_sum[own_rows:], "seq", 1)
    grad_wq, grad_wk, grad_wv = finish(
        place, left_sum[:own_rows], left_last, left_other, left_cross,
        right_sum[:own_rows], right_last, right_other, right_cross,
    )
    return (grad_x, grad_wq, grad_wk, grad_wv)


def solution(mesh):
    square = mesh.shape["seq"] == 8 and mesh.shape["head"] == 4
    body = block_body if square else general_body
    placed = (
        P("seq", "head"),
        P("seq", "head"),
        P("seq", "head"),
        P("seq", "head"),
        P("seq", None),
        P(None, "head"),
        P(None, "head"),
        P(None, "head"),
        P(),
    )
    return jax.shard_map(
        body,
        mesh=mesh,
        in_specs=placed,
        out_specs=(P("seq", "head"), P("seq", "head"), P("seq", "head"), P("seq", "head")),
        check_vma=False,
    )
```

```python
import functools
import math

import jax
import jax.numpy as jnp
from jax import lax
from jax.experimental import pallas as pl
from jax.experimental.pallas import tpu as pltpu
from jax.sharding import PartitionSpec as P

D = 4608
H = 32
HD = 128
WINDOW = 4096


SOFT_CAP = 50.0
ROPE_BASE = 10000.0


def passed_along(value, axis, by):
    size = lax.axis_size(axis)
    pairs = [(i, i + by) for i in range(size) if 0 <= i + by < size]
    return lax.ppermute(value, axis, pairs)


def rotate_back(gradient, positions, head_count):
    row_count = gradient.shape[0]
    half_width = HD // 2
    inverse_freq = ROPE_BASE ** (-(jnp.arange(half_width, dtype=jnp.float32) * (2.0 / HD)))
    angles = positions.astype(jnp.float32)[:, None] * inverse_freq[None, :]
    cosine = jnp.cos(angles)[:, None, :]
    sine_part = jnp.sin(angles)[:, None, :]
    per_head = gradient.reshape(row_count, head_count, HD)
    leading = per_head[:, :, :half_width]
    trailing = per_head[:, :, half_width:]
    rotated = jnp.concatenate(
        [leading * cosine + trailing * sine_part, trailing * cosine - leading * sine_part], axis=2
    )
    return rotated.reshape(row_count, head_count * HD)


def times_t(left, right):
    return lax.dot_general(
        left, right, (((1,), (1,)), ((), ())), preferred_element_type=jnp.float32
    )


def inner_rows(left, right):
    return lax.dot_general(
        left, right, (((0,), (0,)), ((), ())), preferred_element_type=jnp.float32
    )


def general_body(queries, keys, values, out_grad, normed, w_query, w_key, w_value, valid_len):
    row_count = queries.shape[0]
    kv_heads = keys.shape[1] // HD
    head_count = queries.shape[1] // HD
    group_size = head_count // kv_heads
    kv_width = kv_heads * HD
    hop_count = WINDOW // row_count
    score_scale = (D // H) ** (-0.5)
    shard_index = lax.axis_index("seq")
    last_shard = valid_len.shape[0] - 1
    row_iota = jnp.arange(row_count, dtype=jnp.int32)
    query_pos = shard_index * row_count + row_iota
    own_valid = row_iota < valid_len[shard_index]
    grad_rows = jnp.where(own_valid[:, None], out_grad, jnp.zeros_like(out_grad))
    query_blocks = queries.reshape(row_count, kv_heads, group_size, HD)
    grad_blocks = grad_rows.reshape(row_count, kv_heads, group_size, HD)
    key_value = jnp.concatenate([keys, values], axis=1)
    arrived = [key_value]
    moving = key_value
    for distance in range(1, hop_count + 1):
        moving = passed_along(moving, "seq", 1)
        arrived.append(moving)
    allowed_list = []
    capped_list = []
    running = jnp.zeros((kv_heads, group_size, row_count), jnp.float32)
    for distance in range(hop_count + 1):
        key_pos = (shard_index - distance) * row_count + row_iota
        owner = jnp.clip(shard_index - distance, 0, last_shard)
        key_valid = row_iota < valid_len[owner]
        offset_gap = query_pos[:, None] - key_pos[None, :]
        allowed = (
            (offset_gap >= 0)
            & (offset_gap < WINDOW)
            & (key_pos[None, :] >= 0)
            & (key_valid[None, :] | (offset_gap == 0))
        )
        key_block = arrived[distance][:, :kv_width].reshape(row_count, kv_heads, HD)
        raw_scores = (
            jnp.einsum(
                "qhgd,khd->hgqk", query_blocks, key_block, preferred_element_type=jnp.float32
            )
            * score_scale
        )
        capped = SOFT_CAP * jnp.tanh(raw_scores / SOFT_CAP)
        running = running + jnp.sum(jnp.where(allowed, jnp.exp(capped), 0.0), axis=-1)
        allowed_list.append(allowed)
        capped_list.append(capped)
    log_total = jnp.log(running)[..., None]
    attended = jnp.zeros((row_count, kv_heads, group_size, HD), jnp.float32)
    for distance in range(hop_count + 1):
        value_block = arrived[distance][:, kv_width:].reshape(row_count, kv_heads, HD)
        rounded = jnp.where(
            allowed_list[distance], jnp.exp(capped_list[distance] - log_total), 0.0
        ).astype(jnp.bfloat16)
        attended = attended + jnp.einsum(
            "hgqk,khd->qhgd", rounded, value_block, preferred_element_type=jnp.float32
        )
    row_delta = jnp.sum(grad_blocks.astype(jnp.float32) * attended, axis=-1)
    delta_cols = jnp.transpose(row_delta, (1, 2, 0))[..., None]
    query_grad = jnp.zeros((row_count, kv_heads, group_size, HD), jnp.float32)
    partials = [None] * (hop_count + 1)
    for distance in range(hop_count, -1, -1):
        key_block = arrived[distance][:, :kv_width].reshape(row_count, kv_heads, HD)
        value_block = arrived[distance][:, kv_width:].reshape(row_count, kv_heads, HD)
        capped = capped_list[distance]
        exact = jnp.where(allowed_list[distance], jnp.exp(capped - log_total), 0.0)
        rounded = exact.astype(jnp.bfloat16)
        grad_probs = jnp.einsum(
            "qhgd,khd->hgqk", grad_blocks, value_block, preferred_element_type=jnp.float32
        )
        grad_scores = (exact * (grad_probs - delta_cols) * (1.0 - (capped / SOFT_CAP) ** 2)).astype(
            jnp.bfloat16
        )
        query_grad = (
            query_grad
            + jnp.einsum(
                "hgqk,khd->qhgd", grad_scores, key_block, preferred_element_type=jnp.float32
            )
            * score_scale
        )
        key_grad = (
            jnp.einsum(
                "hgqk,qhgd->khd", grad_scores, query_blocks, preferred_element_type=jnp.float32
            )
            * score_scale
        )
        value_grad = jnp.einsum(
            "hgqk,qhgd->khd", rounded, grad_blocks, preferred_element_type=jnp.float32
        )
        partials[distance] = jnp.concatenate(
            [key_grad.reshape(row_count, kv_width), value_grad.reshape(row_count, kv_width)], axis=1
        )
    carried = partials[hop_count]
    for distance in range(hop_count - 1, -1, -1):
        carried = (
            passed_along(carried.astype(jnp.bfloat16), "seq", -1).astype(carried.dtype)
            + partials[distance]
        )
    query_pre = rotate_back(
        query_grad.reshape(row_count, head_count * HD), query_pos, head_count
    ).astype(jnp.bfloat16)
    key_pre = rotate_back(carried[:, :kv_width], query_pos, kv_heads).astype(jnp.bfloat16)
    value_pre = carried[:, kv_width:].astype(jnp.bfloat16)
    input_terms = (
        times_t(query_pre, w_query) + times_t(key_pre, w_key) + times_t(value_pre, w_value)
    )
    grad_x = lax.psum_scatter(
        input_terms.astype(jnp.bfloat16), "head", scatter_dimension=1, tiled=True
    )
    stacked = jnp.concatenate([query_pre, key_pre, value_pre], axis=1)
    weight_total = lax.psum_scatter(
        inner_rows(normed, stacked).astype(jnp.bfloat16), "seq", scatter_dimension=0, tiled=True
    ).astype(jnp.float32)
    query_cols = head_count * HD
    grad_wq = weight_total[:, :query_cols].astype(jnp.bfloat16)
    grad_wk = weight_total[:, query_cols : query_cols + kv_width].astype(jnp.bfloat16)
    grad_wv = weight_total[:, query_cols + kv_width :].astype(jnp.bfloat16)
    return (grad_x, grad_wq, grad_wk, grad_wv)
QB = 512
KB = 512
PACK_ROWS = 128
SHARE_COLS = 384
MIB = 1024 * 1024
NT = (((1,), (1,)), ((), ()))
NN = (((1,), (0,)), ((), ()))


def dot(a, b, dims):
    return lax.dot_general(a, b, dims, preferred_element_type=jnp.float32)


def attention_kernel(shards, rows, score_scale, place, lens, *refs):
    n = shards
    qg_in, mine_in, peer_in = refs[:3]
    cos_r, sin_r, cos_s, sin_s = refs[3:7]
    dq_out, keep_out, give_out = refs[7:10]
    (q2, k2, kT, gx, vx, alive, probs, slopes, dps, dq, dk, dv, dqT, qT, gT, sems) = refs[10:]
    me = place[0]
    core = lax.rem(me, 2)
    copies = []
    mine_at = pl.ds(pl.multiple_of((2 + core) * HD, HD), HD)
    peer_at = pl.ds(pl.multiple_of((3 - core) * HD, HD), HD)
    for m in range(n):
        to = pl.ds(m * rows, rows)
        copies.append(pltpu.make_async_copy(qg_in.at[m], probs.at[to, pl.ds(0, 2 * HD)], sems.at[0, m]))
        copies.append(pltpu.make_async_copy(mine_in.at[m], probs.at[to, mine_at], sems.at[1, m]))
        copies.append(pltpu.make_async_copy(peer_in.at[m], probs.at[to, peer_at], sems.at[2, m]))
    for copy in copies:
        copy.start()
    dk[...] = jnp.zeros_like(dk)
    dv[...] = jnp.zeros_like(dv)
    for copy in copies:
        copy.wait()

    piece = 128
    lane = lax.broadcasted_iota(jnp.int32, (piece, HD), 1)

    def pack_shard(shard, offset):
        valid = lens[shard]

        def pack_piece(i, _):
            src = pl.multiple_of(i * piece, piece)
            dst = pl.multiple_of(offset + i * piece, 16)
            live = (lax.broadcasted_iota(jnp.int32, (piece, HD), 0) + src) < valid
            at = pl.ds(pl.multiple_of(shard * rows + src, piece), piece)
            to = pl.ds(dst, piece)
            q = jnp.where(live, probs[at, :HD].astype(jnp.float32), 0.0) * (score_scale / SOFT_CAP)
            hi = q.astype(jnp.bfloat16)
            q2[to, :HD] = hi
            q2[to, HD:] = (q - hi.astype(jnp.float32)).astype(jnp.bfloat16)
            zero = jnp.zeros((piece, HD), jnp.bfloat16)
            gx[to, :] = jnp.where(live, probs[at, HD : 2 * HD], zero)
            k = jnp.where(live, probs[at, 2 * HD : 3 * HD], zero)
            k2[to, :HD] = k
            k2[to, HD:] = k
            vx[to, :] = jnp.where(live, probs[at, 3 * HD : 4 * HD], zero)
            alive[to, :] = jnp.where(live, 1.0, 0.0)
            return 0

        lax.fori_loop(0, rows // piece, pack_piece, 0)
        return offset + ((valid + 15) // 16) * 16

    end = lax.fori_loop(0, n, pack_shard, jnp.int32(0))
    tail = pl.ds(pl.multiple_of(end, 16), KB)
    for ref in (q2, k2, gx, vx, alive):
        ref[tail, :] = jnp.zeros((KB, ref.shape[1]), ref.dtype)
    blocks = pl.cdiv(end, QB)

    def turn(i, _):
        at = pl.ds(pl.multiple_of(i * KB, KB), KB)
        kT[:, at] = k2[at, :HD].T
        return 0

    lax.fori_loop(0, pl.cdiv(end, KB), turn, 0)

    def block(b, _):
        first = pl.multiple_of(b * QB, QB)
        own = pl.ds(first, QB)
        full = first // KB
        qT[...] = q2[own, :].T
        gT[...] = gx[own, :].T
        dqT[...] = jnp.zeros_like(dqT)

        def forward(c, sums, masked):
            at = pl.ds(pl.multiple_of(c * KB, KB), KB)
            t = jnp.tanh(dot(k2[at, :], qT[...], NN))
            dp = dot(vx[at, :], gT[...], NN)
            e = jnp.exp2(t * (SOFT_CAP * math.log2(math.e)))
            e = e * jnp.concatenate([alive[at, :]] * (QB // HD), axis=1)
            if masked:
                key = lax.broadcasted_iota(jnp.int32, (KB, QB), 0) + c * KB
                query = lax.broadcasted_iota(jnp.int32, (KB, QB), 1) + first
                e = jnp.where(key <= query, e, 0.0)
            probs[at, :] = e.astype(jnp.bfloat16)
            slopes[at, :] = (e * (1.0 - t * t)).astype(jnp.bfloat16)
            dps[at, :] = dp
            total, weighted = sums
            return total + jnp.sum(e, axis=0, keepdims=True), weighted + jnp.sum(e * dp, axis=0, keepdims=True)

        zero = jnp.zeros((1, QB), jnp.float32)
        sums = lax.fori_loop(0, full, lambda c, sums: forward(c, sums, False), (zero, zero))
        total, weighted = forward(full, sums, True)
        inv = 1.0 / total
        delta = weighted * inv
        gs = (gT[...].astype(jnp.float32) * inv).astype(jnp.bfloat16).T
        q = qT[:HD, :].astype(jnp.float32) + qT[HD:, :].astype(jnp.float32)
        qs = (q * (inv * SOFT_CAP)).astype(jnp.bfloat16).T

        def backward(c, _):
            at = pl.ds(pl.multiple_of(c * KB, KB), KB)
            ds = slopes[at, :] * (dps[at, :] - delta).astype(jnp.bfloat16)
            dqT[...] += dot(kT[:, at], ds, NN)
            dk[at, :] += dot(ds, qs, NN)
            dv[at, :] += dot(probs[at, :], gs, NN)
            return 0

        lax.fori_loop(0, full + 1, backward, 0)
        dq[own, :] = (dqT[...] * (inv * score_scale)).T
        return 0

    lax.fori_loop(0, blocks, block, 0)

    def unpack(j, _):
        shard = place[1 + j]
        offset = lax.fori_loop(0, shard, lambda s, o: o + ((lens[s] + 15) // 16) * 16, jnp.int32(0))
        valid = lens[shard]
        ca, sa = cos_s[pl.ds(shard, 1), :], sin_s[pl.ds(shard, 1), :]

        def unpack_piece(i, _):
            dst = pl.multiple_of(i * piece, piece)
            src = pl.ds(pl.multiple_of(offset + i * piece, 16), piece)
            live = (lax.broadcasted_iota(jnp.int32, (piece, HD), 0) + dst) < valid
            cb, sb = cos_r[pl.ds(dst, piece), :], sin_r[pl.ds(dst, piece), :]
            cosine = ca * cb - sa * sb
            sine = sa * cb + ca * sb
            sine = jnp.where(lane < HD // 2, sine, -sine)

            def rotate(x):
                return x * cosine + pltpu.roll(x, HD // 2, 1) * sine

            to = pl.ds(pl.multiple_of(j * rows + i * piece, piece), piece)
            dq_out[to, :] = jnp.where(live, rotate(dq[src, :]), 0.0).astype(jnp.bfloat16)
            key_part = jnp.where(live, rotate(dk[src, :]), 0.0)
            value_part = jnp.where(live, dv[src, :], 0.0)
            keep_out[to, :] = jnp.where(core == 0, key_part, value_part)
            swapped = j + 1 - 2 * lax.rem(j, 2)
            to = pl.ds(pl.multiple_of(swapped * rows + i * piece, piece), piece)
            give_out[to, :] = jnp.where(core == 0, value_part, key_part).astype(jnp.bfloat16)
            return 0

        lax.fori_loop(0, rows // piece, unpack_piece, 0)
        return 0

    lax.fori_loop(0, n, unpack, 0)


def attention(place, lens, qg, mine, peer, tables, score_scale):
    n, rows = qg.shape[:2]
    tokens = n * rows
    room = tokens + KB
    bf, f32 = jnp.bfloat16, jnp.float32
    any_spec = pl.BlockSpec(memory_space=pl.ANY)
    smem = pl.BlockSpec(memory_space=pltpu.SMEM)
    vmem = pl.BlockSpec(memory_space=pltpu.VMEM)
    return pl.pallas_call(
        functools.partial(attention_kernel, n, rows, score_scale),
        out_shape=(
            jax.ShapeDtypeStruct((tokens, HD), bf),
            jax.ShapeDtypeStruct((tokens, HD), f32),
            jax.ShapeDtypeStruct((tokens, HD), bf),
        ),
        in_specs=[smem, smem] + [any_spec] * 3 + [vmem] * 4,
        out_specs=(vmem, vmem, vmem),
        scratch_shapes=[
            pltpu.VMEM((room, 2 * HD), bf),
            pltpu.VMEM((room, 2 * HD), bf),
            pltpu.VMEM((HD, room), bf),
            pltpu.VMEM((room, HD), bf),
            pltpu.VMEM((room, HD), bf),
            pltpu.VMEM((room, HD), f32),
            pltpu.VMEM((room, QB), bf),
            pltpu.VMEM((room, QB), bf),
            pltpu.VMEM((room, QB), f32),
            pltpu.VMEM((room, HD), f32),
            pltpu.VMEM((room, HD), f32),
            pltpu.VMEM((room, HD), f32),
            pltpu.VMEM((HD, QB), f32),
            pltpu.VMEM((2 * HD, QB), bf),
            pltpu.VMEM((HD, QB), bf),
            pltpu.SemaphoreType.DMA((3, n)),
        ],
        compiler_params=pltpu.CompilerParams(vmem_limit_bytes=42 * MIB),
        cost_estimate=pl.CostEstimate(
            flops=12 * tokens * tokens * HD, bytes_accessed=16 * tokens * HD, transcendentals=tokens * tokens
        ),
        name="attention",
    )(place, lens, qg, mine, peer, *tables)


def tables(rows, shards):
    half = HD // 2
    freq = 10000.0 ** (-(jnp.arange(half, dtype=jnp.float32) * (2.0 / HD)))
    freq = jnp.concatenate([freq, freq])[None, :]
    within = jnp.arange(rows, dtype=jnp.float32)[:, None] * freq
    start = (jnp.arange(shards, dtype=jnp.float32) * rows)[:, None] * freq
    return jnp.cos(within), jnp.sin(within), jnp.cos(start), jnp.sin(start)


def pack_kernel(q, k, v, g, qg, kv, sems):
    n = qg.shape[0]
    copies = []
    for to in range(n):
        cols, kv_cols = pl.ds(to * HD, HD), pl.ds((to // 2) * HD, HD)
        copies.append(pltpu.make_async_copy((k, v)[to % 2].at[:, kv_cols], kv.at[to], sems.at[0, to]))
        copies.append(pltpu.make_async_copy(q.at[:, cols], qg.at[to, :, pl.ds(0, HD)], sems.at[1, to]))
        copies.append(pltpu.make_async_copy(g.at[:, cols], qg.at[to, :, pl.ds(HD, HD)], sems.at[2, to]))
    for copy in copies:
        copy.start()
    for copy in copies:
        copy.wait()


def pack(q, k, v, g, n):
    rows = q.shape[0]
    vmem = pl.BlockSpec(memory_space=pltpu.VMEM)
    return pl.pallas_call(
        pack_kernel,
        out_shape=(jax.ShapeDtypeStruct((n, rows, 2 * HD), q.dtype), jax.ShapeDtypeStruct((n, rows, HD), q.dtype)),
        in_specs=[pl.BlockSpec(memory_space=pltpu.HBM)] * 4,
        out_specs=(vmem, vmem),
        scratch_shapes=[pltpu.SemaphoreType.DMA((3, n))],
        compiler_params=pltpu.CompilerParams(vmem_limit_bytes=60 * MIB),
        name="pack",
    )(q, k, v, g)


def line_up_kernel(place, *refs):
    parts, out, theirs = refs[:-2], refs[-2], refs[-1]
    rows = theirs.shape[0]
    for m, src in enumerate(parts):
        chip = place[1 + 2 * m] // 2
        cols = pl.ds(pl.multiple_of(chip * HD, HD), HD)
        out[:, cols] = src[...]
        theirs[:, cols] = src[rows:, :]


def line_up(place, parts):
    rows = parts[0].shape[0]
    cols = len(parts) * HD
    vmem = pl.BlockSpec(memory_space=pltpu.VMEM)
    return pl.pallas_call(
        line_up_kernel,
        out_shape=[jax.ShapeDtypeStruct((r, cols), parts[0].dtype) for r in (rows, rows // 2)],
        in_specs=[pl.BlockSpec(memory_space=pltpu.SMEM)] + [vmem] * len(parts),
        out_specs=[vmem, vmem],
        compiler_params=pltpu.CompilerParams(vmem_limit_bytes=8 * MIB),
        name="line_up",
    )(place, *parts)


def add_up_kernel(left, left_last, right, right_last, out):
    rows, half = out.shape[0], out.shape[1] // 2
    for which, (a, b) in enumerate(((left, left_last), (right, right_last))):
        total = a[rows:, :].astype(jnp.float32) + b[rows:, :].astype(jnp.float32)
        out[:, which * half : (which + 1) * half] = total.astype(out.dtype)


def add_up(*shares):
    rows, half = shares[0].shape
    vmem = pl.BlockSpec(memory_space=pltpu.VMEM)
    return pl.pallas_call(
        add_up_kernel,
        out_shape=jax.ShapeDtypeStruct((rows // 2, 2 * half), shares[0].dtype),
        in_specs=[vmem] * 4,
        out_specs=vmem,
        compiler_params=pltpu.CompilerParams(vmem_limit_bytes=12 * MIB),
        name="add_up",
    )(*shares)


def finish_kernel(place, left, left_last, right, right_last, cross, grad_wq, grad_wk, grad_wv):
    core = lax.rem(place[0], 2)
    rows, half = grad_wk.shape

    def add(a, b, cols):
        return (a[:rows, cols].astype(jnp.float32) + b[:rows, cols].astype(jnp.float32)).astype(jnp.bfloat16)

    for h in range(half // HD):
        cols = slice(h * HD, (h + 1) * HD)
        mine, other = add(left, left_last, cols), cross[:, cols]
        grad_wq[:, 2 * h * HD : (2 * h + 1) * HD] = jnp.where(core == 0, mine, other)
        grad_wq[:, (2 * h + 1) * HD : (2 * h + 2) * HD] = jnp.where(core == 0, other, mine)
        mine, other = add(right, right_last, cols), cross[:, half + h * HD : half + (h + 1) * HD]
        grad_wk[:, cols] = jnp.where(core == 0, mine, other)
        grad_wv[:, cols] = jnp.where(core == 0, other, mine)


def finish(place, left, left_last, right, right_last, cross):
    rows, half = cross.shape[0], left.shape[1]
    vmem = pl.BlockSpec(memory_space=pltpu.VMEM)
    return pl.pallas_call(
        finish_kernel,
        out_shape=[jax.ShapeDtypeStruct((rows, w), jnp.bfloat16) for w in (2 * half, half, half)],
        in_specs=[pl.BlockSpec(memory_space=pltpu.SMEM)] + [vmem] * 5,
        out_specs=[vmem] * 3,
        compiler_params=pltpu.CompilerParams(vmem_limit_bytes=14 * MIB),
        name="finish",
    )(place, left, left_last, right, right_last, cross)


def swap(value, axis, by):
    size = lax.axis_size(axis)
    return lax.ppermute(value, axis, [(i, i ^ by) for i in range(size)])


def middle_swap(value):
    levels = lax.axis_size("head")
    pairs = []
    for s in range(lax.axis_size("seq")):
        for h in range(levels):
            to = s * levels + (3 - h) if h in (1, 2) else (s ^ 1) * levels + h
            pairs.append((s * levels + h, to))
    return lax.ppermute(value, ("seq", "head"), pairs)


def wide(value):
    return value.astype(jnp.float32)


def turn_kernel(place, own, peer, out):
    core = lax.rem(place[0], 2)
    rows = own.shape[0]
    strip = out.shape[0] // 2
    for which, src in ((0, own), (1, peer)):
        cols = slice(which * rows, (which + 1) * rows)
        turned = src[...].T

        @pl.when(core == 0)
        def _():
            out[:, cols] = turned

        @pl.when(core == 1)
        def _():
            out[:strip, cols] = turned[strip:]
            out[strip:, cols] = turned[:strip]


def turn(place, own, peer, m, strip):
    rows = own.shape[0]
    spec = pl.BlockSpec((rows, strip), lambda i, place: (0, place[1 + 2 * m] // 2))
    return pl.pallas_call(
        turn_kernel,
        out_shape=jax.ShapeDtypeStruct((strip, 2 * rows), own.dtype),
        grid_spec=pltpu.PrefetchScalarGridSpec(
            num_scalar_prefetch=1,
            grid=(1,),
            in_specs=[spec, spec],
            out_specs=pl.BlockSpec((strip, 2 * rows), lambda i, place: (0, 0)),
        ),
        compiler_params=pltpu.CompilerParams(vmem_limit_bytes=16 * MIB),
        name="turn",
    )(place, own, peer)


def stand_up_queries_kernel(place, mine, other, out):
    core = lax.rem(place[0], 2)
    for h in range(mine.shape[1] // HD):
        cols = slice(h * HD, (h + 1) * HD)
        out[pl.ds(pl.multiple_of((2 * h + core) * HD, HD), HD), :] = mine[:, cols].T
        out[pl.ds(pl.multiple_of((2 * h + 1 - core) * HD, HD), HD), :] = other[:, cols].T


def stand_up_key_values_kernel(place, mine, other, out):
    core = lax.rem(place[0], 2)
    half = mine.shape[1]
    out[pl.ds(pl.multiple_of(core * half, HD), half), :] = mine[...].T
    out[pl.ds(pl.multiple_of((1 - core) * half, HD), half), :] = other[...].T


def stand_up(kernel, place, lined, other):
    rows, cols = other.shape
    spec = pl.BlockSpec((rows, cols), lambda i: (0, 0))
    return pl.pallas_call(
        kernel,
        out_shape=jax.ShapeDtypeStruct((2 * cols, rows), other.dtype),
        grid=(1,),
        in_specs=[pl.BlockSpec(memory_space=pltpu.SMEM), spec, spec],
        out_specs=pl.BlockSpec((2 * cols, rows), lambda i: (0, 0)),
        compiler_params=pltpu.CompilerParams(vmem_limit_bytes=8 * MIB),
        name="stand_up",
    )(place, lined, other)


def share_kernel(order, xq, xkv, w_query, w_key, w_value, out):
    kv_cols = w_key.shape[1]
    total = dot(w_query[...], xq[...], NN)
    total += dot(w_key[...], xkv[:kv_cols, :], NN)
    total += dot(w_value[...], xkv[kv_cols:, :], NN)
    out[...] = total.astype(out.dtype)


def share(order, i, xq, xkv, w_query, w_key, w_value, width):
    rows = xq.shape[1]
    steps = width // SHARE_COLS
    weights = (w_query, w_key, w_value)
    depth = sum(w.shape[1] for w in weights)
    return pl.pallas_call(
        share_kernel,
        out_shape=jax.ShapeDtypeStruct((width, rows), xq.dtype),
        grid_spec=pltpu.PrefetchScalarGridSpec(
            num_scalar_prefetch=1,
            grid=(steps,),
            in_specs=[pl.BlockSpec(x.shape, lambda j, order: (0, 0)) for x in (xq, xkv)]
            + [pl.BlockSpec((SHARE_COLS, w.shape[1]), lambda j, order: (order[i] * steps + j, 0)) for w in weights],
            out_specs=pl.BlockSpec((SHARE_COLS, rows), lambda j, order: (j, 0)),
        ),
        compiler_params=pltpu.CompilerParams(vmem_limit_bytes=14 * MIB),
        cost_estimate=pl.CostEstimate(flops=2 * rows * depth * width, bytes_accessed=2 * depth * width, transcendentals=0),
        name="share",
    )(order, xq, xkv, *weights)


def lay_down_kernel(a, b, c, out):
    total = a[...].astype(jnp.float32) + b[...].astype(jnp.float32) + c[...].astype(jnp.float32)
    out[...] = total.astype(out.dtype).T


def lay_down(a, b, c):
    vmem = pl.BlockSpec(memory_space=pltpu.VMEM)
    return pl.pallas_call(
        lay_down_kernel,
        out_shape=jax.ShapeDtypeStruct(a.shape[::-1], a.dtype),
        in_specs=[vmem] * 3,
        out_specs=vmem,
        compiler_params=pltpu.CompilerParams(vmem_limit_bytes=16 * MIB),
        name="lay_down",
    )(a, b, c)


BLOCK_ORDER = ((3, 2, 1, 0), (0, 3, 2, 1), (3, 0, 1, 2), (0, 1, 2, 3))


def block_body(queries, keys, values, out_grad, normed, w_query, w_key, w_value, valid_len):
    bf = jnp.bfloat16
    seq_size = lax.axis_size("seq")
    rows = queries.shape[0]
    score_scale = (D // H) ** (-0.5)
    me = lax.axis_index("seq")
    core = me % 2
    chip = me // 2
    level = lax.axis_index("head")
    chips = seq_size // 2
    place = jnp.stack([me] + [me ^ m for m in range(seq_size)]).astype(jnp.int32)

    order = jnp.array(BLOCK_ORDER, jnp.int32)[level]
    place, order = lax.optimization_barrier((place, order))
    qg, kv = pack(queries, keys, values, out_grad, seq_size)
    kv = lax.all_to_all(kv, "seq", 0, 0, tiled=True)
    kv_peer = swap(kv, "seq", 1)
    normed_peer = swap(normed, "seq", 1)
    qg, kv, normed, normed_peer = lax.optimization_barrier((qg, kv, normed, normed_peer))
    qg = lax.all_to_all(qg, "seq", 0, 0, tiled=True)
    width = normed.shape[1]
    own_rows = width // seq_size
    strips = [turn(place, normed, normed_peer, m, 2 * own_rows) for m in range(chips)]
    strips, qg = lax.optimization_barrier((strips, qg))

    dq, keep, give = attention(place, valid_len, qg, kv, kv_peer, tables(rows, seq_size), score_scale)
    dkv = (keep + wide(swap(give, "seq", 1))).astype(bf)
    dq_parts = [dq[2 * rows * m : 2 * rows * (m + 1)] for m in range(chips)]
    dkv_parts = [dkv[2 * rows * m : 2 * rows * (m + 1)] for m in range(chips)]
    dq_parts = [dq_parts[0]] + [swap(dq_parts[m], "seq", 2 * m) for m in range(1, chips)]
    dkv_parts = [dkv_parts[0]] + [swap(dkv_parts[m], "seq", 2 * m) for m in range(1, chips)]
    dq_parts, dkv_parts = lax.optimization_barrier((dq_parts, dkv_parts))
    block_width = width // lax.axis_size("head")

    def left_of(m, lined):
        return jnp.dot(strips[m], lined, preferred_element_type=jnp.float32).astype(bf)

    lined_q, theirs_q = line_up(place, dq_parts)
    lined_kv, theirs_kv = line_up(place, dkv_parts)
    theirs_q, theirs_kv = lax.optimization_barrier((theirs_q, theirs_kv))
    other_q, other_kv = swap(theirs_q, "seq", 1), swap(theirs_kv, "seq", 1)
    left3_out, right3_out = left_of(3, lined_q), left_of(3, lined_kv)
    left3, right3 = swap(left3_out, "seq", 2), swap(right3_out, "seq", 4)
    left3_out, right3_out, other_q, other_kv = lax.optimization_barrier((left3_out, right3_out, other_q, other_kv))
    xq = stand_up(stand_up_queries_kernel, place, lined_q, other_q)
    xkv = stand_up(stand_up_key_values_kernel, place, lined_kv, other_kv)
    first_out = share(order, 0, xq, xkv, w_query, w_key, w_value, block_width)
    first_in = swap(first_out, "head", 1)
    lined_q, lined_kv, xq, first_out = lax.optimization_barrier((lined_q, lined_kv, xq, first_out))
    left1_out, right2_out = left_of(1, lined_q), left_of(2, lined_kv)
    second_out = share(order, 1, xq, xkv, w_query, w_key, w_value, block_width)
    left0, left2, right0, right1 = left_of(0, lined_q), left_of(2, lined_q), left_of(0, lined_kv), left_of(1, lined_kv)
    third = share(order, 2, xq, xkv, w_query, w_key, w_value, block_width)
    left3, right3, left1_out, right2_out, second_out, third, left0, left2, right0, right1 = lax.optimization_barrier(
        (left3, right3, left1_out, right2_out, second_out, third, left0, left2, right0, right1)
    )
    left1, right2 = swap(left1_out, "seq", 2), swap(right2_out, "seq", 4)
    first_in, left1_out, right2_out, second_out, xq = lax.optimization_barrier((first_in, left1_out, right2_out, second_out, xq))
    second_in = swap(second_out, "head", 1)
    first_mid = middle_swap((wide(second_out) + wide(first_in)).astype(bf))
    left_out = (wide(left2) + wide(left3)).astype(bf)
    right_out = (wide(right1) + wide(right3)).astype(bf)
    fourth = share(order, 3, xq, xkv, w_query, w_key, w_value, block_width)
    left1, right2, left_out, right_out, fourth = lax.optimization_barrier((left1, right2, left_out, right_out, fourth))
    left_last, right_last = swap(left_out, "seq", 4), swap(right_out, "seq", 2)
    second_in, first_mid, third, left_out, right_out = lax.optimization_barrier(
        (second_in, first_mid, third, left_out, right_out)
    )
    inner = (level == 1) | (level == 2)
    third_in = swap(jnp.where(inner, first_mid, third), "head", 1)
    second_mid = middle_swap((wide(third) + wide(second_in)).astype(bf))
    left_sum = (wide(left0) + wide(left1)).astype(bf)
    right_sum = (wide(right0) + wide(right2)).astype(bf)
    cross = swap(add_up(left_sum, left_last, right_sum, right_last), "seq", 1)
    grad_x = lay_down(fourth, third_in, jnp.where(inner, second_mid, first_in))
    grad_wq, grad_wk, grad_wv = finish(place, left_sum, left_last, right_sum, right_last, cross)
    return (grad_x, grad_wq, grad_wk, grad_wv)


def solution(mesh):
    square = mesh.shape["seq"] == 8 and mesh.shape["head"] == 4
    body = block_body if square else general_body
    placed = (
        P("seq", "head"),
        P("seq", "head"),
        P("seq", "head"),
        P("seq", "head"),
        P("seq", None),
        P(None, "head"),
        P(None, "head"),
        P(None, "head"),
        P(),
    )
    return jax.shard_map(
        body,
        mesh=mesh,
        in_specs=placed,
        out_specs=(P("seq", "head"), P("seq", "head"), P("seq", "head"), P("seq", "head")),
        check_vma=False,
    )
```

```python
import functools
import math

import jax
import jax.numpy as jnp
from jax import lax
from jax.experimental import pallas as pl
from jax.experimental.pallas import tpu as pltpu
from jax.sharding import PartitionSpec as P

D = 4608
H = 32
HD = 128
WINDOW = 4096


SOFT_CAP = 50.0
ROPE_BASE = 10000.0


def passed_along(value, axis, by):
    size = lax.axis_size(axis)
    pairs = [(i, i + by) for i in range(size) if 0 <= i + by < size]
    return lax.ppermute(value, axis, pairs)


def rotate_back(gradient, positions, head_count):
    row_count = gradient.shape[0]
    half_width = HD // 2
    inverse_freq = ROPE_BASE ** (-(jnp.arange(half_width, dtype=jnp.float32) * (2.0 / HD)))
    angles = positions.astype(jnp.float32)[:, None] * inverse_freq[None, :]
    cosine = jnp.cos(angles)[:, None, :]
    sine_part = jnp.sin(angles)[:, None, :]
    per_head = gradient.reshape(row_count, head_count, HD)
    leading = per_head[:, :, :half_width]
    trailing = per_head[:, :, half_width:]
    rotated = jnp.concatenate(
        [leading * cosine + trailing * sine_part, trailing * cosine - leading * sine_part], axis=2
    )
    return rotated.reshape(row_count, head_count * HD)


def times_t(left, right):
    return lax.dot_general(
        left, right, (((1,), (1,)), ((), ())), preferred_element_type=jnp.float32
    )


def inner_rows(left, right):
    return lax.dot_general(
        left, right, (((0,), (0,)), ((), ())), preferred_element_type=jnp.float32
    )


def general_body(queries, keys, values, out_grad, normed, w_query, w_key, w_value, valid_len):
    row_count = queries.shape[0]
    kv_heads = keys.shape[1] // HD
    head_count = queries.shape[1] // HD
    group_size = head_count // kv_heads
    kv_width = kv_heads * HD
    hop_count = WINDOW // row_count
    score_scale = (D // H) ** (-0.5)
    shard_index = lax.axis_index("seq")
    last_shard = valid_len.shape[0] - 1
    row_iota = jnp.arange(row_count, dtype=jnp.int32)
    query_pos = shard_index * row_count + row_iota
    own_valid = row_iota < valid_len[shard_index]
    grad_rows = jnp.where(own_valid[:, None], out_grad, jnp.zeros_like(out_grad))
    query_blocks = queries.reshape(row_count, kv_heads, group_size, HD)
    grad_blocks = grad_rows.reshape(row_count, kv_heads, group_size, HD)
    key_value = jnp.concatenate([keys, values], axis=1)
    arrived = [key_value]
    moving = key_value
    for distance in range(1, hop_count + 1):
        moving = passed_along(moving, "seq", 1)
        arrived.append(moving)
    allowed_list = []
    capped_list = []
    running = jnp.zeros((kv_heads, group_size, row_count), jnp.float32)
    for distance in range(hop_count + 1):
        key_pos = (shard_index - distance) * row_count + row_iota
        owner = jnp.clip(shard_index - distance, 0, last_shard)
        key_valid = row_iota < valid_len[owner]
        offset_gap = query_pos[:, None] - key_pos[None, :]
        allowed = (
            (offset_gap >= 0)
            & (offset_gap < WINDOW)
            & (key_pos[None, :] >= 0)
            & (key_valid[None, :] | (offset_gap == 0))
        )
        key_block = arrived[distance][:, :kv_width].reshape(row_count, kv_heads, HD)
        raw_scores = (
            jnp.einsum(
                "qhgd,khd->hgqk", query_blocks, key_block, preferred_element_type=jnp.float32
            )
            * score_scale
        )
        capped = SOFT_CAP * jnp.tanh(raw_scores / SOFT_CAP)
        running = running + jnp.sum(jnp.where(allowed, jnp.exp(capped), 0.0), axis=-1)
        allowed_list.append(allowed)
        capped_list.append(capped)
    log_total = jnp.log(running)[..., None]
    attended = jnp.zeros((row_count, kv_heads, group_size, HD), jnp.float32)
    for distance in range(hop_count + 1):
        value_block = arrived[distance][:, kv_width:].reshape(row_count, kv_heads, HD)
        rounded = jnp.where(
            allowed_list[distance], jnp.exp(capped_list[distance] - log_total), 0.0
        ).astype(jnp.bfloat16)
        attended = attended + jnp.einsum(
            "hgqk,khd->qhgd", rounded, value_block, preferred_element_type=jnp.float32
        )
    row_delta = jnp.sum(grad_blocks.astype(jnp.float32) * attended, axis=-1)
    delta_cols = jnp.transpose(row_delta, (1, 2, 0))[..., None]
    query_grad = jnp.zeros((row_count, kv_heads, group_size, HD), jnp.float32)
    partials = [None] * (hop_count + 1)
    for distance in range(hop_count, -1, -1):
        key_block = arrived[distance][:, :kv_width].reshape(row_count, kv_heads, HD)
        value_block = arrived[distance][:, kv_width:].reshape(row_count, kv_heads, HD)
        capped = capped_list[distance]
        exact = jnp.where(allowed_list[distance], jnp.exp(capped - log_total), 0.0)
        rounded = exact.astype(jnp.bfloat16)
        grad_probs = jnp.einsum(
            "qhgd,khd->hgqk", grad_blocks, value_block, preferred_element_type=jnp.float32
        )
        grad_scores = (exact * (grad_probs - delta_cols) * (1.0 - (capped / SOFT_CAP) ** 2)).astype(
            jnp.bfloat16
        )
        query_grad = (
            query_grad
            + jnp.einsum(
                "hgqk,khd->qhgd", grad_scores, key_block, preferred_element_type=jnp.float32
            )
            * score_scale
        )
        key_grad = (
            jnp.einsum(
                "hgqk,qhgd->khd", grad_scores, query_blocks, preferred_element_type=jnp.float32
            )
            * score_scale
        )
        value_grad = jnp.einsum(
            "hgqk,qhgd->khd", rounded, grad_blocks, preferred_element_type=jnp.float32
        )
        partials[distance] = jnp.concatenate(
            [key_grad.reshape(row_count, kv_width), value_grad.reshape(row_count, kv_width)], axis=1
        )
    carried = partials[hop_count]
    for distance in range(hop_count - 1, -1, -1):
        carried = (
            passed_along(carried.astype(jnp.bfloat16), "seq", -1).astype(carried.dtype)
            + partials[distance]
        )
    query_pre = rotate_back(
        query_grad.reshape(row_count, head_count * HD), query_pos, head_count
    ).astype(jnp.bfloat16)
    key_pre = rotate_back(carried[:, :kv_width], query_pos, kv_heads).astype(jnp.bfloat16)
    value_pre = carried[:, kv_width:].astype(jnp.bfloat16)
    input_terms = (
        times_t(query_pre, w_query) + times_t(key_pre, w_key) + times_t(value_pre, w_value)
    )
    grad_x = lax.psum_scatter(
        input_terms.astype(jnp.bfloat16), "head", scatter_dimension=1, tiled=True
    )
    stacked = jnp.concatenate([query_pre, key_pre, value_pre], axis=1)
    weight_total = lax.psum_scatter(
        inner_rows(normed, stacked).astype(jnp.bfloat16), "seq", scatter_dimension=0, tiled=True
    ).astype(jnp.float32)
    query_cols = head_count * HD
    grad_wq = weight_total[:, :query_cols].astype(jnp.bfloat16)
    grad_wk = weight_total[:, query_cols : query_cols + kv_width].astype(jnp.bfloat16)
    grad_wv = weight_total[:, query_cols + kv_width :].astype(jnp.bfloat16)
    return (grad_x, grad_wq, grad_wk, grad_wv)
QB = 512
KB = 512
PACK_ROWS = 128
SHARE_COLS = 384
MIB = 1024 * 1024
NT = (((1,), (1,)), ((), ()))
NN = (((1,), (0,)), ((), ()))


def dot(a, b, dims):
    return lax.dot_general(a, b, dims, preferred_element_type=jnp.float32)


def attention_kernel(shards, rows, score_scale, place, lens, *refs):
    n = shards
    qg_in, mine_in, peer_in = refs[:3]
    cos_r, sin_r, cos_s, sin_s = refs[3:7]
    dq_out, keep_out, give_out = refs[7:10]
    (q2, k2, kT, gx, vx, alive, probs, slopes, dps, dq, dk, dv, dqT, qT, gT, sems) = refs[10:]
    me = place[0]
    core = lax.rem(me, 2)
    copies = []
    mine_at = pl.ds(pl.multiple_of((2 + core) * HD, HD), HD)
    peer_at = pl.ds(pl.multiple_of((3 - core) * HD, HD), HD)
    for m in range(n):
        to = pl.ds(m * rows, rows)
        copies.append(pltpu.make_async_copy(qg_in.at[m], probs.at[to, pl.ds(0, 2 * HD)], sems.at[0, m]))
        copies.append(pltpu.make_async_copy(mine_in.at[m], probs.at[to, mine_at], sems.at[1, m]))
        copies.append(pltpu.make_async_copy(peer_in.at[m], probs.at[to, peer_at], sems.at[2, m]))
    for copy in copies:
        copy.start()
    dk[...] = jnp.zeros_like(dk)
    dv[...] = jnp.zeros_like(dv)
    for copy in copies:
        copy.wait()

    piece = 128
    lane = lax.broadcasted_iota(jnp.int32, (piece, HD), 1)

    def pack_shard(shard, offset):
        valid = lens[shard]

        def pack_piece(i, _):
            src = pl.multiple_of(i * piece, piece)
            dst = pl.multiple_of(offset + i * piece, 16)
            live = (lax.broadcasted_iota(jnp.int32, (piece, HD), 0) + src) < valid
            at = pl.ds(pl.multiple_of(shard * rows + src, piece), piece)
            to = pl.ds(dst, piece)
            q = jnp.where(live, probs[at, :HD].astype(jnp.float32), 0.0) * (score_scale / SOFT_CAP)
            hi = q.astype(jnp.bfloat16)
            q2[to, :HD] = hi
            q2[to, HD:] = (q - hi.astype(jnp.float32)).astype(jnp.bfloat16)
            zero = jnp.zeros((piece, HD), jnp.bfloat16)
            gx[to, :] = jnp.where(live, probs[at, HD : 2 * HD], zero)
            k = jnp.where(live, probs[at, 2 * HD : 3 * HD], zero)
            k2[to, :HD] = k
            k2[to, HD:] = k
            vx[to, :] = jnp.where(live, probs[at, 3 * HD : 4 * HD], zero)
            alive[to, :] = jnp.where(live, 1.0, 0.0)
            return 0

        lax.fori_loop(0, pl.cdiv(valid, piece), pack_piece, 0)
        return offset + ((valid + 15) // 16) * 16

    end = lax.fori_loop(0, n, pack_shard, jnp.int32(0))
    tail = pl.ds(pl.multiple_of(end, 16), KB)
    for ref in (q2, k2, gx, vx, alive):
        ref[tail, :] = jnp.zeros((KB, ref.shape[1]), ref.dtype)
    blocks = pl.cdiv(end, QB)

    def turn(i, _):
        at = pl.ds(pl.multiple_of(i * KB, KB), KB)
        kT[:, at] = k2[at, :HD].T
        return 0

    lax.fori_loop(0, pl.cdiv(end, KB), turn, 0)

    def block(b, _):
        first = pl.multiple_of(b * QB, QB)
        own = pl.ds(first, QB)
        qT[...] = q2[own, :].T
        gT[...] = gx[own, :].T
        dqT[...] = jnp.zeros_like(dqT)

        def forward(at, late, sums, masked):
            size = at.size
            t = jnp.tanh(dot(k2[at, :], qT[:, late:], NN))
            dp = dot(vx[at, :], gT[:, late:], NN)
            e = jnp.exp2(t * (SOFT_CAP * math.log2(math.e)))
            e = e * jnp.concatenate([alive[at, :]] * ((QB - late) // HD), axis=1)
            if masked:
                key = lax.broadcasted_iota(jnp.int32, e.shape, 0)
                query = lax.broadcasted_iota(jnp.int32, e.shape, 1)
                e = jnp.where(key <= query, e, 0.0)
            probs[at, late:] = e.astype(jnp.bfloat16)
            slopes[at, late:] = (e * (1.0 - t * t)).astype(jnp.bfloat16)
            dps[at, late:] = dp
            new = [jnp.sum(e, axis=0, keepdims=True), jnp.sum(e * dp, axis=0, keepdims=True)]
            if late:
                new = [jnp.concatenate([jnp.zeros((1, late), jnp.float32), x], axis=1) for x in new]
            return sums[0] + new[0], sums[1] + new[1]

        def chunk(c):
            return pl.ds(pl.multiple_of(c * KB, KB), KB)

        half = QB // 2
        early_keys = pl.ds(first, half)
        late_keys = pl.ds(pl.multiple_of(first + half, half), half)
        zero = jnp.zeros((1, QB), jnp.float32)
        sums = lax.fori_loop(0, b, lambda c, sums: forward(chunk(c), 0, sums, False), (zero, zero))
        sums = forward(early_keys, 0, sums, True)
        total, weighted = forward(late_keys, half, sums, True)
        inv = 1.0 / total
        delta = weighted * inv
        gs = (gT[...].astype(jnp.float32) * inv).astype(jnp.bfloat16).T
        q = qT[:HD, :].astype(jnp.float32) + qT[HD:, :].astype(jnp.float32)
        qs = (q * (inv * SOFT_CAP)).astype(jnp.bfloat16).T

        def backward(at, late):
            ds = slopes[at, late:] * (dps[at, late:] - delta[:, late:]).astype(jnp.bfloat16)
            dqT[:, late:] += dot(kT[:, at], ds, NN)
            dk[at, :] += dot(ds, qs[late:, :], NN)
            dv[at, :] += dot(probs[at, late:], gs[late:, :], NN)

        lax.fori_loop(0, b, lambda c, _: (backward(chunk(c), 0), 0)[1], 0)
        backward(early_keys, 0)
        backward(late_keys, half)
        dq[own, :] = (dqT[...] * (inv * score_scale)).T
        return 0

    lax.fori_loop(0, blocks, block, 0)

    def unpack(j, _):
        shard = place[1 + j]
        offset = lax.fori_loop(0, shard, lambda s, o: o + ((lens[s] + 15) // 16) * 16, jnp.int32(0))
        valid = lens[shard]
        ca, sa = cos_s[pl.ds(shard, 1), :], sin_s[pl.ds(shard, 1), :]

        swapped = j + 1 - 2 * lax.rem(j, 2)

        def unpack_piece(i, _):
            dst = pl.multiple_of(i * piece, piece)
            src = pl.ds(pl.multiple_of(offset + i * piece, 16), piece)
            live = (lax.broadcasted_iota(jnp.int32, (piece, HD), 0) + dst) < valid
            cb, sb = cos_r[pl.ds(dst, piece), :], sin_r[pl.ds(dst, piece), :]
            cosine = ca * cb - sa * sb
            sine = sa * cb + ca * sb
            sine = jnp.where(lane < HD // 2, sine, -sine)

            def rotate(x):
                return x * cosine + pltpu.roll(x, HD // 2, 1) * sine

            to = pl.ds(pl.multiple_of(j * rows + i * piece, piece), piece)
            dq_out[to, :] = jnp.where(live, rotate(dq[src, :]), 0.0).astype(jnp.bfloat16)
            key_part = jnp.where(live, rotate(dk[src, :]), 0.0)
            value_part = jnp.where(live, dv[src, :], 0.0)
            keep_out[to, :] = jnp.where(core == 0, key_part, value_part)
            to = pl.ds(pl.multiple_of(swapped * rows + i * piece, piece), piece)
            give_out[to, :] = jnp.where(core == 0, value_part, key_part).astype(jnp.bfloat16)
            return 0

        def clear_piece(i, _):
            to = pl.ds(pl.multiple_of(j * rows + i * piece, piece), piece)
            dq_out[to, :] = jnp.zeros((piece, HD), jnp.bfloat16)
            keep_out[to, :] = jnp.zeros((piece, HD), jnp.float32)
            to = pl.ds(pl.multiple_of(swapped * rows + i * piece, piece), piece)
            give_out[to, :] = jnp.zeros((piece, HD), jnp.bfloat16)
            return 0

        used = pl.cdiv(valid, piece)
        lax.fori_loop(0, used, unpack_piece, 0)
        lax.fori_loop(used, rows // piece, clear_piece, 0)
        return 0

    lax.fori_loop(0, n, unpack, 0)


def attention(place, lens, qg, mine, peer, tables, score_scale):
    n, rows = qg.shape[:2]
    tokens = n * rows
    room = tokens + KB
    bf, f32 = jnp.bfloat16, jnp.float32
    any_spec = pl.BlockSpec(memory_space=pl.ANY)
    smem = pl.BlockSpec(memory_space=pltpu.SMEM)
    vmem = pl.BlockSpec(memory_space=pltpu.VMEM)
    return pl.pallas_call(
        functools.partial(attention_kernel, n, rows, score_scale),
        out_shape=(
            jax.ShapeDtypeStruct((tokens, HD), bf),
            jax.ShapeDtypeStruct((tokens, HD), f32),
            jax.ShapeDtypeStruct((tokens, HD), bf),
        ),
        in_specs=[smem, smem] + [any_spec] * 3 + [vmem] * 4,
        out_specs=(vmem, vmem, vmem),
        scratch_shapes=[
            pltpu.VMEM((room, 2 * HD), bf),
            pltpu.VMEM((room, 2 * HD), bf),
            pltpu.VMEM((HD, room), bf),
            pltpu.VMEM((room, HD), bf),
            pltpu.VMEM((room, HD), bf),
            pltpu.VMEM((room, HD), f32),
            pltpu.VMEM((room, QB), bf),
            pltpu.VMEM((room, QB), bf),
            pltpu.VMEM((room, QB), f32),
            pltpu.VMEM((room, HD), f32),
            pltpu.VMEM((room, HD), f32),
            pltpu.VMEM((room, HD), f32),
            pltpu.VMEM((HD, QB), f32),
            pltpu.VMEM((2 * HD, QB), bf),
            pltpu.VMEM((HD, QB), bf),
            pltpu.SemaphoreType.DMA((3, n)),
        ],
        compiler_params=pltpu.CompilerParams(vmem_limit_bytes=42 * MIB),
        cost_estimate=pl.CostEstimate(
            flops=12 * tokens * tokens * HD, bytes_accessed=16 * tokens * HD, transcendentals=tokens * tokens
        ),
        name="attention",
    )(place, lens, qg, mine, peer, *tables)


def tables(rows, shards):
    half = HD // 2
    freq = 10000.0 ** (-(jnp.arange(half, dtype=jnp.float32) * (2.0 / HD)))
    freq = jnp.concatenate([freq, freq])[None, :]
    within = jnp.arange(rows, dtype=jnp.float32)[:, None] * freq
    start = (jnp.arange(shards, dtype=jnp.float32) * rows)[:, None] * freq
    return jnp.cos(within), jnp.sin(within), jnp.cos(start), jnp.sin(start)


def pack_kernel(q, k, v, g, qg, kv, sems):
    n = qg.shape[0]
    copies = []
    for to in range(n):
        cols, kv_cols = pl.ds(to * HD, HD), pl.ds((to // 2) * HD, HD)
        copies.append(pltpu.make_async_copy((k, v)[to % 2].at[:, kv_cols], kv.at[to], sems.at[0, to]))
        copies.append(pltpu.make_async_copy(q.at[:, cols], qg.at[to, :, pl.ds(0, HD)], sems.at[1, to]))
        copies.append(pltpu.make_async_copy(g.at[:, cols], qg.at[to, :, pl.ds(HD, HD)], sems.at[2, to]))
    for copy in copies:
        copy.start()
    for copy in copies:
        copy.wait()


def pack(q, k, v, g, n):
    rows = q.shape[0]
    vmem = pl.BlockSpec(memory_space=pltpu.VMEM)
    return pl.pallas_call(
        pack_kernel,
        out_shape=(jax.ShapeDtypeStruct((n, rows, 2 * HD), q.dtype), jax.ShapeDtypeStruct((n, rows, HD), q.dtype)),
        in_specs=[pl.BlockSpec(memory_space=pltpu.HBM)] * 4,
        out_specs=(vmem, vmem),
        scratch_shapes=[pltpu.SemaphoreType.DMA((3, n))],
        compiler_params=pltpu.CompilerParams(vmem_limit_bytes=60 * MIB),
        name="pack",
    )(q, k, v, g)


def line_up_kernel(place, *refs):
    n = (len(refs) - 4) // 2
    for parts, out, theirs in ((refs[:n], refs[-4], refs[-2]), (refs[n : 2 * n], refs[-3], refs[-1])):
        rows = theirs.shape[0]
        for m, src in enumerate(parts):
            chip = place[1 + 2 * m] // 2
            cols = pl.ds(pl.multiple_of(chip * HD, HD), HD)
            theirs[:, cols] = src[rows:, :]
            out[:, cols] = src[...]


def line_up(place, left, right):
    rows = left[0].shape[0]
    cols = len(left) * HD
    vmem = pl.BlockSpec(memory_space=pltpu.VMEM)
    return pl.pallas_call(
        line_up_kernel,
        out_shape=[jax.ShapeDtypeStruct((r, cols), left[0].dtype) for r in (rows, rows, rows // 2, rows // 2)],
        in_specs=[pl.BlockSpec(memory_space=pltpu.SMEM)] + [vmem] * (2 * len(left)),
        out_specs=[vmem] * 4,
        compiler_params=pltpu.CompilerParams(vmem_limit_bytes=12 * MIB),
        name="line_up",
    )(place, *left, *right)


def add_up_kernel(left, left_last, right, right_last, out):
    rows, half = out.shape[0], out.shape[1] // 2
    for which, (a, b) in enumerate(((left, left_last), (right, right_last))):
        total = a[rows:, :].astype(jnp.float32) + b[rows:, :].astype(jnp.float32)
        out[:, which * half : (which + 1) * half] = total.astype(out.dtype)


def add_up(*shares):
    rows, half = shares[0].shape
    vmem = pl.BlockSpec(memory_space=pltpu.VMEM)
    return pl.pallas_call(
        add_up_kernel,
        out_shape=jax.ShapeDtypeStruct((rows // 2, 2 * half), shares[0].dtype),
        in_specs=[vmem] * 4,
        out_specs=vmem,
        compiler_params=pltpu.CompilerParams(vmem_limit_bytes=12 * MIB),
        name="add_up",
    )(*shares)


def finish_kernel(place, left, left_last, right, right_last, cross, grad_wq, grad_wk, grad_wv):
    core = lax.rem(place[0], 2)
    rows, half = grad_wk.shape

    def add(a, b, cols):
        return (a[:rows, cols].astype(jnp.float32) + b[:rows, cols].astype(jnp.float32)).astype(jnp.bfloat16)

    for h in range(half // HD):
        cols = slice(h * HD, (h + 1) * HD)
        mine, other = add(left, left_last, cols), cross[:, cols]
        grad_wq[:, 2 * h * HD : (2 * h + 1) * HD] = jnp.where(core == 0, mine, other)
        grad_wq[:, (2 * h + 1) * HD : (2 * h + 2) * HD] = jnp.where(core == 0, other, mine)
        mine, other = add(right, right_last, cols), cross[:, half + h * HD : half + (h + 1) * HD]
        grad_wk[:, cols] = jnp.where(core == 0, mine, other)
        grad_wv[:, cols] = jnp.where(core == 0, other, mine)


def finish(place, left, left_last, right, right_last, cross):
    rows, half = cross.shape[0], left.shape[1]
    vmem = pl.BlockSpec(memory_space=pltpu.VMEM)
    return pl.pallas_call(
        finish_kernel,
        out_shape=[jax.ShapeDtypeStruct((rows, w), jnp.bfloat16) for w in (2 * half, half, half)],
        in_specs=[pl.BlockSpec(memory_space=pltpu.SMEM)] + [vmem] * 5,
        out_specs=[vmem] * 3,
        compiler_params=pltpu.CompilerParams(vmem_limit_bytes=14 * MIB),
        name="finish",
    )(place, left, left_last, right, right_last, cross)


def swap(value, axis, by):
    size = lax.axis_size(axis)
    return lax.ppermute(value, axis, [(i, i ^ by) for i in range(size)])


def middle_swap(value):
    levels = lax.axis_size("head")
    pairs = []
    for s in range(lax.axis_size("seq")):
        for h in range(levels):
            to = s * levels + (3 - h) if h in (1, 2) else (s ^ 1) * levels + h
            pairs.append((s * levels + h, to))
    return lax.ppermute(value, ("seq", "head"), pairs)


def wide(value):
    return value.astype(jnp.float32)


def turn_kernel(place, own, peer, out):
    core = lax.rem(place[0], 2)
    rows = own.shape[0]
    strip = out.shape[0] // 2
    for which, src in ((0, own), (1, peer)):
        cols = slice(which * rows, (which + 1) * rows)
        turned = src[...].T

        @pl.when(core == 0)
        def _():
            out[:, cols] = turned

        @pl.when(core == 1)
        def _():
            out[:strip, cols] = turned[strip:]
            out[strip:, cols] = turned[:strip]


def turn(place, own, peer, m, strip):
    rows = own.shape[0]
    spec = pl.BlockSpec((rows, strip), lambda i, place: (0, place[1 + 2 * m] // 2))
    return pl.pallas_call(
        turn_kernel,
        out_shape=jax.ShapeDtypeStruct((strip, 2 * rows), own.dtype),
        grid_spec=pltpu.PrefetchScalarGridSpec(
            num_scalar_prefetch=1,
            grid=(1,),
            in_specs=[spec, spec],
            out_specs=pl.BlockSpec((strip, 2 * rows), lambda i, place: (0, 0)),
        ),
        compiler_params=pltpu.CompilerParams(vmem_limit_bytes=16 * MIB),
        name="turn",
    )(place, own, peer)


def stand_up_queries_kernel(place, mine, other, out):
    core = lax.rem(place[0], 2)
    for h in range(mine.shape[1] // HD):
        cols = slice(h * HD, (h + 1) * HD)
        out[pl.ds(pl.multiple_of((2 * h + core) * HD, HD), HD), :] = mine[:, cols].T
        out[pl.ds(pl.multiple_of((2 * h + 1 - core) * HD, HD), HD), :] = other[:, cols].T


def stand_up_key_values_kernel(place, mine, other, out):
    core = lax.rem(place[0], 2)
    half = mine.shape[1]
    out[pl.ds(pl.multiple_of(core * half, HD), half), :] = mine[...].T
    out[pl.ds(pl.multiple_of((1 - core) * half, HD), half), :] = other[...].T


def stand_up(kernel, place, lined, other):
    rows, cols = other.shape
    spec = pl.BlockSpec((rows, cols), lambda i: (0, 0))
    return pl.pallas_call(
        kernel,
        out_shape=jax.ShapeDtypeStruct((2 * cols, rows), other.dtype),
        grid=(1,),
        in_specs=[pl.BlockSpec(memory_space=pltpu.SMEM), spec, spec],
        out_specs=pl.BlockSpec((2 * cols, rows), lambda i: (0, 0)),
        compiler_params=pltpu.CompilerParams(vmem_limit_bytes=8 * MIB),
        name="stand_up",
    )(place, lined, other)


def share_kernel(order, xq, xkv, w_query, w_key, w_value, out):
    kv_cols = w_key.shape[1]
    total = dot(w_query[...], xq[...], NN)
    total += dot(w_key[...], xkv[:kv_cols, :], NN)
    total += dot(w_value[...], xkv[kv_cols:, :], NN)
    out[...] = total.astype(out.dtype)


def share(order, i, xq, xkv, w_query, w_key, w_value, width):
    rows = xq.shape[1]
    steps = width // SHARE_COLS
    weights = (w_query, w_key, w_value)
    depth = sum(w.shape[1] for w in weights)
    return pl.pallas_call(
        share_kernel,
        out_shape=jax.ShapeDtypeStruct((width, rows), xq.dtype),
        grid_spec=pltpu.PrefetchScalarGridSpec(
            num_scalar_prefetch=1,
            grid=(steps,),
            in_specs=[pl.BlockSpec(x.shape, lambda j, order: (0, 0)) for x in (xq, xkv)]
            + [pl.BlockSpec((SHARE_COLS, w.shape[1]), lambda j, order: (order[i] * steps + j, 0)) for w in weights],
            out_specs=pl.BlockSpec((SHARE_COLS, rows), lambda j, order: (j, 0)),
        ),
        compiler_params=pltpu.CompilerParams(vmem_limit_bytes=14 * MIB),
        cost_estimate=pl.CostEstimate(flops=2 * rows * depth * width, bytes_accessed=2 * depth * width, transcendentals=0),
        name="share",
    )(order, xq, xkv, *weights)


def lay_down_kernel(a, b, c, out):
    total = a[...].astype(jnp.float32) + b[...].astype(jnp.float32) + c[...].astype(jnp.float32)
    out[...] = total.astype(out.dtype).T


def lay_down(a, b, c):
    vmem = pl.BlockSpec(memory_space=pltpu.VMEM)
    return pl.pallas_call(
        lay_down_kernel,
        out_shape=jax.ShapeDtypeStruct(a.shape[::-1], a.dtype),
        in_specs=[vmem] * 3,
        out_specs=vmem,
        compiler_params=pltpu.CompilerParams(vmem_limit_bytes=16 * MIB),
        name="lay_down",
    )(a, b, c)


BLOCK_ORDER = ((3, 2, 1, 0), (0, 3, 2, 1), (3, 0, 1, 2), (0, 1, 2, 3))


def block_body(queries, keys, values, out_grad, normed, w_query, w_key, w_value, valid_len):
    bf = jnp.bfloat16
    seq_size = lax.axis_size("seq")
    rows = queries.shape[0]
    score_scale = (D // H) ** (-0.5)
    me = lax.axis_index("seq")
    core = me % 2
    chip = me // 2
    level = lax.axis_index("head")
    chips = seq_size // 2
    place = jnp.stack([me] + [me ^ m for m in range(seq_size)]).astype(jnp.int32)

    order = jnp.array(BLOCK_ORDER, jnp.int32)[level]
    place, order = lax.optimization_barrier((place, order))
    qg, kv = pack(queries, keys, values, out_grad, seq_size)
    kv = lax.all_to_all(kv, "seq", 0, 0, tiled=True)
    kv_peer = swap(kv, "seq", 1)
    normed_peer = swap(normed, "seq", 1)
    qg, kv, normed, normed_peer = lax.optimization_barrier((qg, kv, normed, normed_peer))
    qg = lax.all_to_all(qg, "seq", 0, 0, tiled=True)
    width = normed.shape[1]
    own_rows = width // seq_size
    strips = [turn(place, normed, normed_peer, m, 2 * own_rows) for m in range(3)]
    strips, qg = lax.optimization_barrier((strips, qg))

    dq, keep, give = attention(place, valid_len, qg, kv, kv_peer, tables(rows, seq_size), score_scale)
    dkv = (keep + wide(swap(give, "seq", 1))).astype(bf)
    dq_parts = [dq[2 * rows * m : 2 * rows * (m + 1)] for m in range(chips)]
    dkv_parts = [dkv[2 * rows * m : 2 * rows * (m + 1)] for m in range(chips)]
    dq_parts = [dq_parts[0]] + [swap(dq_parts[m], "seq", 2 * m) for m in range(1, chips)]
    dkv_parts = [dkv_parts[0]] + [swap(dkv_parts[m], "seq", 2 * m) for m in range(1, chips)]
    normed, normed_peer, dq_parts[1] = lax.optimization_barrier((normed, normed_peer, dq_parts[1]))
    strips = [*strips, turn(place, normed, normed_peer, 3, 2 * own_rows)]
    strips, dq_parts, dkv_parts = lax.optimization_barrier((strips, dq_parts, dkv_parts))
    block_width = width // lax.axis_size("head")

    def left_of(m, lined):
        return jnp.dot(strips[m], lined, preferred_element_type=jnp.float32).astype(bf)

    lined_q, lined_kv, theirs_q, theirs_kv = line_up(place, dq_parts, dkv_parts)
    other_q, other_kv = swap(theirs_q, "seq", 1), swap(theirs_kv, "seq", 1)
    left3_out, right3_out = left_of(3, lined_q), left_of(3, lined_kv)
    left3, right3 = swap(left3_out, "seq", 2), swap(right3_out, "seq", 4)
    left3_out, right3_out, other_q, other_kv = lax.optimization_barrier((left3_out, right3_out, other_q, other_kv))
    xq = stand_up(stand_up_queries_kernel, place, lined_q, other_q)
    xkv = stand_up(stand_up_key_values_kernel, place, lined_kv, other_kv)
    first_out = share(order, 0, xq, xkv, w_query, w_key, w_value, block_width)
    first_in = swap(first_out, "head", 1)
    lined_q, lined_kv, xq, first_out = lax.optimization_barrier((lined_q, lined_kv, xq, first_out))
    left1_out, right2_out = left_of(1, lined_q), left_of(2, lined_kv)
    second_out = share(order, 1, xq, xkv, w_query, w_key, w_value, block_width)
    left3, right3, left1_out, right2_out, second_out, lined_q, lined_kv, xq = lax.optimization_barrier(
        (left3, right3, left1_out, right2_out, second_out, lined_q, lined_kv, xq)
    )
    left1, right2 = swap(left1_out, "seq", 2), swap(right2_out, "seq", 4)
    first_in, left1_out, right2_out, second_out, xq, lined_q, lined_kv = lax.optimization_barrier(
        (first_in, left1_out, right2_out, second_out, xq, lined_q, lined_kv)
    )
    second_in = swap(second_out, "head", 1)
    first_mid = middle_swap((wide(second_out) + wide(first_in)).astype(bf))
    left_out = (wide(left_of(2, lined_q)) + wide(left3)).astype(bf)
    right_out = (wide(left_of(1, lined_kv)) + wide(right3)).astype(bf)
    third = share(order, 2, xq, xkv, w_query, w_key, w_value, block_width)
    left1, right2, left_out, right_out, lined_q, lined_kv, xq = lax.optimization_barrier(
        (left1, right2, left_out, right_out, lined_q, lined_kv, xq)
    )
    left_last, right_last = swap(left_out, "seq", 4), swap(right_out, "seq", 2)
    second_in, first_mid, third, left_out, right_out, lined_q, lined_kv, xq = lax.optimization_barrier(
        (second_in, first_mid, third, left_out, right_out, lined_q, lined_kv, xq)
    )
    inner = (level == 1) | (level == 2)
    third_in = swap(jnp.where(inner, first_mid, third), "head", 1)
    second_mid = middle_swap((wide(third) + wide(second_in)).astype(bf))
    left_sum = (wide(left_of(0, lined_q)) + wide(left1)).astype(bf)
    right_sum = (wide(left_of(0, lined_kv)) + wide(right2)).astype(bf)
    cross = swap(add_up(left_sum, left_last, right_sum, right_last), "seq", 1)
    fourth = share(order, 3, xq, xkv, w_query, w_key, w_value, block_width)
    grad_x = lay_down(fourth, third_in, jnp.where(inner, second_mid, first_in))
    grad_wq, grad_wk, grad_wv = finish(place, left_sum, left_last, right_sum, right_last, cross)
    return (grad_x, grad_wq, grad_wk, grad_wv)


def solution(mesh):
    square = mesh.shape["seq"] == 8 and mesh.shape["head"] == 4
    body = block_body if square else general_body
    placed = (
        P("seq", "head"),
        P("seq", "head"),
        P("seq", "head"),
        P("seq", "head"),
        P("seq", None),
        P(None, "head"),
        P(None, "head"),
        P(None, "head"),
        P(),
    )
    return jax.shard_map(
        body,
        mesh=mesh,
        in_specs=placed,
        out_specs=(P("seq", "head"), P("seq", "head"), P("seq", "head"), P("seq", "head")),
        check_vma=False,
    )
```

```python
import functools
import math

import jax
import jax.numpy as jnp
from jax import lax
from jax.experimental import pallas as pl
from jax.experimental.pallas import tpu as pltpu
from jax.sharding import PartitionSpec as P

D = 4608
H = 32
HD = 128
WINDOW = 4096


SOFT_CAP = 50.0
ROPE_BASE = 10000.0


def passed_along(value, axis, by):
    size = lax.axis_size(axis)
    pairs = [(i, i + by) for i in range(size) if 0 <= i + by < size]
    return lax.ppermute(value, axis, pairs)


def rotate_back(gradient, positions, head_count):
    row_count = gradient.shape[0]
    half_width = HD // 2
    inverse_freq = ROPE_BASE ** (-(jnp.arange(half_width, dtype=jnp.float32) * (2.0 / HD)))
    angles = positions.astype(jnp.float32)[:, None] * inverse_freq[None, :]
    cosine = jnp.cos(angles)[:, None, :]
    sine_part = jnp.sin(angles)[:, None, :]
    per_head = gradient.reshape(row_count, head_count, HD)
    leading = per_head[:, :, :half_width]
    trailing = per_head[:, :, half_width:]
    rotated = jnp.concatenate(
        [leading * cosine + trailing * sine_part, trailing * cosine - leading * sine_part], axis=2
    )
    return rotated.reshape(row_count, head_count * HD)


def times_t(left, right):
    return lax.dot_general(
        left, right, (((1,), (1,)), ((), ())), preferred_element_type=jnp.float32
    )


def inner_rows(left, right):
    return lax.dot_general(
        left, right, (((0,), (0,)), ((), ())), preferred_element_type=jnp.float32
    )


def general_body(queries, keys, values, out_grad, normed, w_query, w_key, w_value, valid_len):
    row_count = queries.shape[0]
    kv_heads = keys.shape[1] // HD
    head_count = queries.shape[1] // HD
    group_size = head_count // kv_heads
    kv_width = kv_heads * HD
    hop_count = WINDOW // row_count
    score_scale = (D // H) ** (-0.5)
    shard_index = lax.axis_index("seq")
    last_shard = valid_len.shape[0] - 1
    row_iota = jnp.arange(row_count, dtype=jnp.int32)
    query_pos = shard_index * row_count + row_iota
    own_valid = row_iota < valid_len[shard_index]
    grad_rows = jnp.where(own_valid[:, None], out_grad, jnp.zeros_like(out_grad))
    query_blocks = queries.reshape(row_count, kv_heads, group_size, HD)
    grad_blocks = grad_rows.reshape(row_count, kv_heads, group_size, HD)
    key_value = jnp.concatenate([keys, values], axis=1)
    arrived = [key_value]
    moving = key_value
    for distance in range(1, hop_count + 1):
        moving = passed_along(moving, "seq", 1)
        arrived.append(moving)
    allowed_list = []
    capped_list = []
    running = jnp.zeros((kv_heads, group_size, row_count), jnp.float32)
    for distance in range(hop_count + 1):
        key_pos = (shard_index - distance) * row_count + row_iota
        owner = jnp.clip(shard_index - distance, 0, last_shard)
        key_valid = row_iota < valid_len[owner]
        offset_gap = query_pos[:, None] - key_pos[None, :]
        allowed = (
            (offset_gap >= 0)
            & (offset_gap < WINDOW)
            & (key_pos[None, :] >= 0)
            & (key_valid[None, :] | (offset_gap == 0))
        )
        key_block = arrived[distance][:, :kv_width].reshape(row_count, kv_heads, HD)
        raw_scores = (
            jnp.einsum(
                "qhgd,khd->hgqk", query_blocks, key_block, preferred_element_type=jnp.float32
            )
            * score_scale
        )
        capped = SOFT_CAP * jnp.tanh(raw_scores / SOFT_CAP)
        running = running + jnp.sum(jnp.where(allowed, jnp.exp(capped), 0.0), axis=-1)
        allowed_list.append(allowed)
        capped_list.append(capped)
    log_total = jnp.log(running)[..., None]
    attended = jnp.zeros((row_count, kv_heads, group_size, HD), jnp.float32)
    for distance in range(hop_count + 1):
        value_block = arrived[distance][:, kv_width:].reshape(row_count, kv_heads, HD)
        rounded = jnp.where(
            allowed_list[distance], jnp.exp(capped_list[distance] - log_total), 0.0
        ).astype(jnp.bfloat16)
        attended = attended + jnp.einsum(
            "hgqk,khd->qhgd", rounded, value_block, preferred_element_type=jnp.float32
        )
    row_delta = jnp.sum(grad_blocks.astype(jnp.float32) * attended, axis=-1)
    delta_cols = jnp.transpose(row_delta, (1, 2, 0))[..., None]
    query_grad = jnp.zeros((row_count, kv_heads, group_size, HD), jnp.float32)
    partials = [None] * (hop_count + 1)
    for distance in range(hop_count, -1, -1):
        key_block = arrived[distance][:, :kv_width].reshape(row_count, kv_heads, HD)
        value_block = arrived[distance][:, kv_width:].reshape(row_count, kv_heads, HD)
        capped = capped_list[distance]
        exact = jnp.where(allowed_list[distance], jnp.exp(capped - log_total), 0.0)
        rounded = exact.astype(jnp.bfloat16)
        grad_probs = jnp.einsum(
            "qhgd,khd->hgqk", grad_blocks, value_block, preferred_element_type=jnp.float32
        )
        grad_scores = (exact * (grad_probs - delta_cols) * (1.0 - (capped / SOFT_CAP) ** 2)).astype(
            jnp.bfloat16
        )
        query_grad = (
            query_grad
            + jnp.einsum(
                "hgqk,khd->qhgd", grad_scores, key_block, preferred_element_type=jnp.float32
            )
            * score_scale
        )
        key_grad = (
            jnp.einsum(
                "hgqk,qhgd->khd", grad_scores, query_blocks, preferred_element_type=jnp.float32
            )
            * score_scale
        )
        value_grad = jnp.einsum(
            "hgqk,qhgd->khd", rounded, grad_blocks, preferred_element_type=jnp.float32
        )
        partials[distance] = jnp.concatenate(
            [key_grad.reshape(row_count, kv_width), value_grad.reshape(row_count, kv_width)], axis=1
        )
    carried = partials[hop_count]
    for distance in range(hop_count - 1, -1, -1):
        carried = (
            passed_along(carried.astype(jnp.bfloat16), "seq", -1).astype(carried.dtype)
            + partials[distance]
        )
    query_pre = rotate_back(
        query_grad.reshape(row_count, head_count * HD), query_pos, head_count
    ).astype(jnp.bfloat16)
    key_pre = rotate_back(carried[:, :kv_width], query_pos, kv_heads).astype(jnp.bfloat16)
    value_pre = carried[:, kv_width:].astype(jnp.bfloat16)
    input_terms = (
        times_t(query_pre, w_query) + times_t(key_pre, w_key) + times_t(value_pre, w_value)
    )
    grad_x = lax.psum_scatter(
        input_terms.astype(jnp.bfloat16), "head", scatter_dimension=1, tiled=True
    )
    stacked = jnp.concatenate([query_pre, key_pre, value_pre], axis=1)
    weight_total = lax.psum_scatter(
        inner_rows(normed, stacked).astype(jnp.bfloat16), "seq", scatter_dimension=0, tiled=True
    ).astype(jnp.float32)
    query_cols = head_count * HD
    grad_wq = weight_total[:, :query_cols].astype(jnp.bfloat16)
    grad_wk = weight_total[:, query_cols : query_cols + kv_width].astype(jnp.bfloat16)
    grad_wv = weight_total[:, query_cols + kv_width :].astype(jnp.bfloat16)
    return (grad_x, grad_wq, grad_wk, grad_wv)
QB = 512
KB = 512
PACK_ROWS = 128
SHARE_COLS = 384
MIB = 1024 * 1024
NT = (((1,), (1,)), ((), ()))
NN = (((1,), (0,)), ((), ()))


def dot(a, b, dims):
    return lax.dot_general(a, b, dims, preferred_element_type=jnp.float32)


def attention_kernel(shards, rows, score_scale, place, lens, *refs):
    n = shards
    chips = n // 2
    near, mate = refs[:chips], refs[chips : 2 * chips]
    refs = refs[2 * chips :]
    cos_r, sin_r, cos_s, sin_s = refs[:4]
    dq_out, keep_out, give_out = refs[4:7]
    (q2, k2, kT, gx, vx, alive, probs, slopes, dps, dq, dk, dv, dqT, qT, gT, sems) = refs[7:]
    me = place[0]
    core = lax.rem(me, 2)
    copies = []
    first_part, second_part, third_part = pl.ds(0, 2 * HD), pl.ds(2 * HD, 2 * HD), pl.ds(4 * HD, 2 * HD)
    for m in range(chips):
        own = pl.ds(pl.multiple_of(place[1 + 2 * m] * rows, rows), rows)
        other = pl.ds(pl.multiple_of(place[2 + 2 * m] * rows, rows), rows)
        copies.append(pltpu.make_async_copy(near[m].at[:, pl.ds(0, 4 * HD)], probs.at[own, :], sems.at[0, m]))
        copies.append(pltpu.make_async_copy(mate[m].at[:, second_part], probs.at[other, second_part], sems.at[1, m]))
        copies.append(pltpu.make_async_copy(mate[m].at[:, third_part], probs.at[other, first_part], sems.at[2, m]))
    for copy in copies:
        copy.start()
    dk[...] = jnp.zeros_like(dk)
    dv[...] = jnp.zeros_like(dv)
    for copy in copies:
        copy.wait()

    piece = 128
    lane = lax.broadcasted_iota(jnp.int32, (piece, HD), 1)

    def pack_shard(shard, offset):
        valid = lens[shard]

        def pack_piece(i, _):
            src = pl.multiple_of(i * piece, piece)
            dst = pl.multiple_of(offset + i * piece, 16)
            live = (lax.broadcasted_iota(jnp.int32, (piece, HD), 0) + src) < valid
            at = pl.ds(pl.multiple_of(shard * rows + src, piece), piece)
            to = pl.ds(dst, piece)
            q = jnp.where(live, probs[at, :HD].astype(jnp.float32), 0.0) * (score_scale / SOFT_CAP)
            hi = q.astype(jnp.bfloat16)
            q2[to, :HD] = hi
            q2[to, HD:] = (q - hi.astype(jnp.float32)).astype(jnp.bfloat16)
            zero = jnp.zeros((piece, HD), jnp.bfloat16)
            gx[to, :] = jnp.where(live, probs[at, HD : 2 * HD], zero)
            k = jnp.where(live, probs[at, 2 * HD : 3 * HD], zero)
            k2[to, :HD] = k
            k2[to, HD:] = k
            vx[to, :] = jnp.where(live, probs[at, 3 * HD : 4 * HD], zero)
            alive[to, :] = jnp.where(live, 1.0, 0.0)
            return 0

        lax.fori_loop(0, pl.cdiv(valid, piece), pack_piece, 0)
        return offset + ((valid + 15) // 16) * 16

    end = lax.fori_loop(0, n, pack_shard, jnp.int32(0))
    tail = pl.ds(pl.multiple_of(end, 16), KB)
    for ref in (q2, k2, gx, vx, alive):
        ref[tail, :] = jnp.zeros((KB, ref.shape[1]), ref.dtype)
    blocks = pl.cdiv(end, QB)

    def turn(i, _):
        at = pl.ds(pl.multiple_of(i * KB, KB), KB)
        kT[:, at] = k2[at, :HD].T
        return 0

    lax.fori_loop(0, pl.cdiv(end, KB), turn, 0)

    def block(b, _):
        first = pl.multiple_of(b * QB, QB)
        own = pl.ds(first, QB)
        qT[...] = q2[own, :].T
        gT[...] = gx[own, :].T
        dqT[...] = jnp.zeros_like(dqT)

        def forward(at, late, sums, masked):
            size = at.size
            t = jnp.tanh(dot(k2[at, :], qT[:, late:], NN))
            dp = dot(vx[at, :], gT[:, late:], NN)
            e = jnp.exp2(t * (SOFT_CAP * math.log2(math.e)))
            e = e * jnp.concatenate([alive[at, :]] * ((QB - late) // HD), axis=1)
            if masked:
                key = lax.broadcasted_iota(jnp.int32, e.shape, 0)
                query = lax.broadcasted_iota(jnp.int32, e.shape, 1)
                e = jnp.where(key <= query, e, 0.0)
            probs[at, late:] = e.astype(jnp.bfloat16)
            slopes[at, late:] = (e * (1.0 - t * t)).astype(jnp.bfloat16)
            dps[at, late:] = dp
            new = [jnp.sum(e, axis=0, keepdims=True), jnp.sum(e * dp, axis=0, keepdims=True)]
            if late:
                new = [jnp.concatenate([jnp.zeros((1, late), jnp.float32), x], axis=1) for x in new]
            return sums[0] + new[0], sums[1] + new[1]

        def chunk(c):
            return pl.ds(pl.multiple_of(c * KB, KB), KB)

        half = QB // 2
        early_keys = pl.ds(first, half)
        late_keys = pl.ds(pl.multiple_of(first + half, half), half)
        zero = jnp.zeros((1, QB), jnp.float32)
        sums = lax.fori_loop(0, b, lambda c, sums: forward(chunk(c), 0, sums, False), (zero, zero))
        sums = forward(early_keys, 0, sums, True)
        total, weighted = forward(late_keys, half, sums, True)
        inv = 1.0 / total
        delta = weighted * inv
        gs = (gT[...].astype(jnp.float32) * inv).astype(jnp.bfloat16).T
        q = qT[:HD, :].astype(jnp.float32) + qT[HD:, :].astype(jnp.float32)
        qs = (q * (inv * SOFT_CAP)).astype(jnp.bfloat16).T

        def backward(at, late):
            ds = slopes[at, late:] * (dps[at, late:] - delta[:, late:]).astype(jnp.bfloat16)
            dqT[:, late:] += dot(kT[:, at], ds, NN)
            dk[at, :] += dot(ds, qs[late:, :], NN)
            dv[at, :] += dot(probs[at, late:], gs[late:, :], NN)

        lax.fori_loop(0, b, lambda c, _: (backward(chunk(c), 0), 0)[1], 0)
        backward(early_keys, 0)
        backward(late_keys, half)
        dq[own, :] = (dqT[...] * (inv * score_scale)).T
        return 0

    lax.fori_loop(0, blocks, block, 0)

    def unpack(j, _):
        shard = place[1 + j]
        offset = lax.fori_loop(0, shard, lambda s, o: o + ((lens[s] + 15) // 16) * 16, jnp.int32(0))
        valid = lens[shard]
        ca, sa = cos_s[pl.ds(shard, 1), :], sin_s[pl.ds(shard, 1), :]

        swapped = j + 1 - 2 * lax.rem(j, 2)

        def unpack_piece(i, _):
            dst = pl.multiple_of(i * piece, piece)
            src = pl.ds(pl.multiple_of(offset + i * piece, 16), piece)
            live = (lax.broadcasted_iota(jnp.int32, (piece, HD), 0) + dst) < valid
            cb, sb = cos_r[pl.ds(dst, piece), :], sin_r[pl.ds(dst, piece), :]
            cosine = ca * cb - sa * sb
            sine = sa * cb + ca * sb
            sine = jnp.where(lane < HD // 2, sine, -sine)

            def rotate(x):
                return x * cosine + pltpu.roll(x, HD // 2, 1) * sine

            to = pl.ds(pl.multiple_of(j * rows + i * piece, piece), piece)
            dq_out[to, :] = jnp.where(live, rotate(dq[src, :]), 0.0).astype(jnp.bfloat16)
            key_part = jnp.where(live, rotate(dk[src, :]), 0.0)
            value_part = jnp.where(live, dv[src, :], 0.0)
            keep_out[to, :] = jnp.where(core == 0, key_part, value_part)
            to = pl.ds(pl.multiple_of(swapped * rows + i * piece, piece), piece)
            give_out[to, :] = jnp.where(core == 0, value_part, key_part).astype(jnp.bfloat16)
            return 0

        def clear_piece(i, _):
            to = pl.ds(pl.multiple_of(j * rows + i * piece, piece), piece)
            dq_out[to, :] = jnp.zeros((piece, HD), jnp.bfloat16)
            keep_out[to, :] = jnp.zeros((piece, HD), jnp.float32)
            to = pl.ds(pl.multiple_of(swapped * rows + i * piece, piece), piece)
            give_out[to, :] = jnp.zeros((piece, HD), jnp.bfloat16)
            return 0

        used = pl.cdiv(valid, piece)
        lax.fori_loop(0, used, unpack_piece, 0)
        lax.fori_loop(used, rows // piece, clear_piece, 0)
        return 0

    lax.fori_loop(0, n, unpack, 0)


def attention(place, lens, near, mate, tables, score_scale):
    chips = len(near)
    n, rows = 2 * chips, near[0].shape[0]
    tokens = n * rows
    room = tokens + KB
    bf, f32 = jnp.bfloat16, jnp.float32
    any_spec = pl.BlockSpec(memory_space=pl.ANY)
    smem = pl.BlockSpec(memory_space=pltpu.SMEM)
    vmem = pl.BlockSpec(memory_space=pltpu.VMEM)
    return pl.pallas_call(
        functools.partial(attention_kernel, n, rows, score_scale),
        out_shape=(
            jax.ShapeDtypeStruct((tokens, HD), bf),
            jax.ShapeDtypeStruct((tokens, HD), f32),
            jax.ShapeDtypeStruct((tokens, HD), bf),
        ),
        in_specs=[smem, smem] + [any_spec] * (2 * chips) + [vmem] * 4,
        out_specs=(vmem, vmem, vmem),
        scratch_shapes=[
            pltpu.VMEM((room, 2 * HD), bf),
            pltpu.VMEM((room, 2 * HD), bf),
            pltpu.VMEM((HD, room), bf),
            pltpu.VMEM((room, HD), bf),
            pltpu.VMEM((room, HD), bf),
            pltpu.VMEM((room, HD), f32),
            pltpu.VMEM((room, QB), bf),
            pltpu.VMEM((room, QB), bf),
            pltpu.VMEM((room, QB), f32),
            pltpu.VMEM((room, HD), f32),
            pltpu.VMEM((room, HD), f32),
            pltpu.VMEM((room, HD), f32),
            pltpu.VMEM((HD, QB), f32),
            pltpu.VMEM((2 * HD, QB), bf),
            pltpu.VMEM((HD, QB), bf),
            pltpu.SemaphoreType.DMA((3, chips)),
        ],
        compiler_params=pltpu.CompilerParams(vmem_limit_bytes=42 * MIB),
        cost_estimate=pl.CostEstimate(
            flops=12 * tokens * tokens * HD, bytes_accessed=16 * tokens * HD, transcendentals=tokens * tokens
        ),
        name="attention",
    )(place, lens, *near, *mate, *tables)


def tables(rows, shards):
    half = HD // 2
    freq = 10000.0 ** (-(jnp.arange(half, dtype=jnp.float32) * (2.0 / HD)))
    freq = jnp.concatenate([freq, freq])[None, :]
    within = jnp.arange(rows, dtype=jnp.float32)[:, None] * freq
    start = (jnp.arange(shards, dtype=jnp.float32) * rows)[:, None] * freq
    return jnp.cos(within), jnp.sin(within), jnp.cos(start), jnp.sin(start)


def pack_kernel(place, q, k, v, g, *refs):
    blocks, sems = refs[:-1], refs[-1]
    core = lax.rem(place[0], 2)
    copies = []
    for m, block in enumerate(blocks):
        chip = place[1 + 2 * m] // 2
        own, other = 2 * chip + core, 2 * chip + 1 - core
        for at, (src, head) in enumerate(((q, own), (g, own), (k, chip), (v, chip), (q, other), (g, other))):
            cols = pl.ds(pl.multiple_of(head * HD, HD), HD)
            copies.append(pltpu.make_async_copy(src.at[:, cols], block.at[:, pl.ds(at * HD, HD)], sems.at[m, at]))
    for started in copies:
        started.start()
    for started in copies:
        started.wait()


def pack(place, q, k, v, g, n):
    rows = q.shape[0]
    vmem = pl.BlockSpec(memory_space=pltpu.VMEM)
    return pl.pallas_call(
        pack_kernel,
        out_shape=[jax.ShapeDtypeStruct((rows, 6 * HD), q.dtype)] * n,
        in_specs=[pl.BlockSpec(memory_space=pltpu.SMEM)] + [pl.BlockSpec(memory_space=pltpu.HBM)] * 4,
        out_specs=[vmem] * n,
        scratch_shapes=[pltpu.SemaphoreType.DMA((n, 6))],
        compiler_params=pltpu.CompilerParams(vmem_limit_bytes=60 * MIB),
        name="pack",
    )(place, q, k, v, g)


def line_up_kernel(place, *refs):
    n = (len(refs) - 4) // 2
    for parts, out, theirs in ((refs[:n], refs[-4], refs[-2]), (refs[n : 2 * n], refs[-3], refs[-1])):
        rows = theirs.shape[0]
        for m, src in enumerate(parts):
            chip = place[1 + 2 * m] // 2
            cols = pl.ds(pl.multiple_of(chip * HD, HD), HD)
            theirs[:, cols] = src[rows:, :]
            out[:, cols] = src[...]


def line_up(place, left, right):
    rows = left[0].shape[0]
    cols = len(left) * HD
    vmem = pl.BlockSpec(memory_space=pltpu.VMEM)
    return pl.pallas_call(
        line_up_kernel,
        out_shape=[jax.ShapeDtypeStruct((r, cols), left[0].dtype) for r in (rows, rows, rows // 2, rows // 2)],
        in_specs=[pl.BlockSpec(memory_space=pltpu.SMEM)] + [vmem] * (2 * len(left)),
        out_specs=[vmem] * 4,
        compiler_params=pltpu.CompilerParams(vmem_limit_bytes=12 * MIB),
        name="line_up",
    )(place, *left, *right)


def add_up_kernel(left, left_last, right, right_last, out):
    rows, half = out.shape[0], out.shape[1] // 2
    for which, (a, b) in enumerate(((left, left_last), (right, right_last))):
        total = a[rows:, :].astype(jnp.float32) + b[rows:, :].astype(jnp.float32)
        out[:, which * half : (which + 1) * half] = total.astype(out.dtype)


def add_up(*shares):
    rows, half = shares[0].shape
    vmem = pl.BlockSpec(memory_space=pltpu.VMEM)
    return pl.pallas_call(
        add_up_kernel,
        out_shape=jax.ShapeDtypeStruct((rows // 2, 2 * half), shares[0].dtype),
        in_specs=[vmem] * 4,
        out_specs=vmem,
        compiler_params=pltpu.CompilerParams(vmem_limit_bytes=12 * MIB),
        name="add_up",
    )(*shares)


def finish_kernel(place, left, left_last, right, right_last, cross, grad_wq, grad_wk, grad_wv):
    core = lax.rem(place[0], 2)
    rows, half = grad_wk.shape

    def add(a, b, cols):
        return (a[:rows, cols].astype(jnp.float32) + b[:rows, cols].astype(jnp.float32)).astype(jnp.bfloat16)

    for h in range(half // HD):
        cols = slice(h * HD, (h + 1) * HD)
        mine, other = add(left, left_last, cols), cross[:, cols]
        grad_wq[:, 2 * h * HD : (2 * h + 1) * HD] = jnp.where(core == 0, mine, other)
        grad_wq[:, (2 * h + 1) * HD : (2 * h + 2) * HD] = jnp.where(core == 0, other, mine)
        mine, other = add(right, right_last, cols), cross[:, half + h * HD : half + (h + 1) * HD]
        grad_wk[:, cols] = jnp.where(core == 0, mine, other)
        grad_wv[:, cols] = jnp.where(core == 0, other, mine)


def finish(place, left, left_last, right, right_last, cross):
    rows, half = cross.shape[0], left.shape[1]
    vmem = pl.BlockSpec(memory_space=pltpu.VMEM)
    return pl.pallas_call(
        finish_kernel,
        out_shape=[jax.ShapeDtypeStruct((rows, w), jnp.bfloat16) for w in (2 * half, half, half)],
        in_specs=[pl.BlockSpec(memory_space=pltpu.SMEM)] + [vmem] * 5,
        out_specs=[vmem] * 3,
        compiler_params=pltpu.CompilerParams(vmem_limit_bytes=14 * MIB),
        name="finish",
    )(place, left, left_last, right, right_last, cross)


def swap(value, axis, by):
    size = lax.axis_size(axis)
    return lax.ppermute(value, axis, [(i, i ^ by) for i in range(size)])


def middle_swap(value):
    levels = lax.axis_size("head")
    pairs = []
    for s in range(lax.axis_size("seq")):
        for h in range(levels):
            to = s * levels + (3 - h) if h in (1, 2) else (s ^ 1) * levels + h
            pairs.append((s * levels + h, to))
    return lax.ppermute(value, ("seq", "head"), pairs)


def wide(value):
    return value.astype(jnp.float32)


def turn_kernel(place, own, peer, out):
    core = lax.rem(place[0], 2)
    rows = own.shape[0]
    strip = out.shape[0] // 2
    for which, src in ((0, own), (1, peer)):
        cols = slice(which * rows, (which + 1) * rows)
        turned = src[...].T

        @pl.when(core == 0)
        def _():
            out[:, cols] = turned

        @pl.when(core == 1)
        def _():
            out[:strip, cols] = turned[strip:]
            out[strip:, cols] = turned[:strip]


def turn(place, own, peer, m, strip):
    rows = own.shape[0]
    spec = pl.BlockSpec((rows, strip), lambda i, place: (0, place[1 + 2 * m] // 2))
    return pl.pallas_call(
        turn_kernel,
        out_shape=jax.ShapeDtypeStruct((strip, 2 * rows), own.dtype),
        grid_spec=pltpu.PrefetchScalarGridSpec(
            num_scalar_prefetch=1,
            grid=(1,),
            in_specs=[spec, spec],
            out_specs=pl.BlockSpec((strip, 2 * rows), lambda i, place: (0, 0)),
        ),
        compiler_params=pltpu.CompilerParams(vmem_limit_bytes=16 * MIB),
        name="turn",
    )(place, own, peer)


def stand_up_queries_kernel(place, mine, other, out):
    core = lax.rem(place[0], 2)
    for h in range(mine.shape[1] // HD):
        cols = slice(h * HD, (h + 1) * HD)
        out[pl.ds(pl.multiple_of((2 * h + core) * HD, HD), HD), :] = mine[:, cols].T
        out[pl.ds(pl.multiple_of((2 * h + 1 - core) * HD, HD), HD), :] = other[:, cols].T


def stand_up_key_values_kernel(place, mine, other, out):
    core = lax.rem(place[0], 2)
    half = mine.shape[1]
    out[pl.ds(pl.multiple_of(core * half, HD), half), :] = mine[...].T
    out[pl.ds(pl.multiple_of((1 - core) * half, HD), half), :] = other[...].T


def stand_up(kernel, place, lined, other):
    rows, cols = other.shape
    spec = pl.BlockSpec((rows, cols), lambda i: (0, 0))
    return pl.pallas_call(
        kernel,
        out_shape=jax.ShapeDtypeStruct((2 * cols, rows), other.dtype),
        grid=(1,),
        in_specs=[pl.BlockSpec(memory_space=pltpu.SMEM), spec, spec],
        out_specs=pl.BlockSpec((2 * cols, rows), lambda i: (0, 0)),
        compiler_params=pltpu.CompilerParams(vmem_limit_bytes=8 * MIB),
        name="stand_up",
    )(place, lined, other)


def share_kernel(order, xq, xkv, w_query, w_key, w_value, out):
    kv_cols = w_key.shape[1]
    total = dot(w_query[...], xq[...], NN)
    total += dot(w_key[...], xkv[:kv_cols, :], NN)
    total += dot(w_value[...], xkv[kv_cols:, :], NN)
    out[...] = total.astype(out.dtype)


def share(order, i, xq, xkv, w_query, w_key, w_value, width):
    rows = xq.shape[1]
    steps = width // SHARE_COLS
    weights = (w_query, w_key, w_value)
    depth = sum(w.shape[1] for w in weights)
    return pl.pallas_call(
        share_kernel,
        out_shape=jax.ShapeDtypeStruct((width, rows), xq.dtype),
        grid_spec=pltpu.PrefetchScalarGridSpec(
            num_scalar_prefetch=1,
            grid=(steps,),
            in_specs=[pl.BlockSpec(x.shape, lambda j, order: (0, 0)) for x in (xq, xkv)]
            + [pl.BlockSpec((SHARE_COLS, w.shape[1]), lambda j, order: (order[i] * steps + j, 0)) for w in weights],
            out_specs=pl.BlockSpec((SHARE_COLS, rows), lambda j, order: (j, 0)),
        ),
        compiler_params=pltpu.CompilerParams(vmem_limit_bytes=14 * MIB),
        cost_estimate=pl.CostEstimate(flops=2 * rows * depth * width, bytes_accessed=2 * depth * width, transcendentals=0),
        name="share",
    )(order, xq, xkv, *weights)


def lay_down_kernel(a, b, c, out):
    total = a[...].astype(jnp.float32) + b[...].astype(jnp.float32) + c[...].astype(jnp.float32)
    out[...] = total.astype(out.dtype).T


def lay_down(a, b, c):
    vmem = pl.BlockSpec(memory_space=pltpu.VMEM)
    return pl.pallas_call(
        lay_down_kernel,
        out_shape=jax.ShapeDtypeStruct(a.shape[::-1], a.dtype),
        in_specs=[vmem] * 3,
        out_specs=vmem,
        compiler_params=pltpu.CompilerParams(vmem_limit_bytes=16 * MIB),
        name="lay_down",
    )(a, b, c)


BLOCK_ORDER = ((3, 2, 1, 0), (0, 3, 2, 1), (3, 0, 1, 2), (0, 1, 2, 3))


def block_body(queries, keys, values, out_grad, normed, w_query, w_key, w_value, valid_len):
    bf = jnp.bfloat16
    seq_size = lax.axis_size("seq")
    rows = queries.shape[0]
    score_scale = (D // H) ** (-0.5)
    me = lax.axis_index("seq")
    core = me % 2
    chip = me // 2
    level = lax.axis_index("head")
    chips = seq_size // 2
    place = jnp.stack([me] + [me ^ m for m in range(seq_size)]).astype(jnp.int32)

    order = jnp.array(BLOCK_ORDER, jnp.int32)[level]
    place, order = lax.optimization_barrier((place, order))
    near = list(pack(place, queries, keys, values, out_grad, chips))
    normed_peer = swap(normed, "seq", 1)
    normed, normed_peer, _ = lax.optimization_barrier((normed, normed_peer, near[0]))
    near = [near[0]] + [swap(near[m], "seq", 2 * m) for m in range(1, chips)]
    width = normed.shape[1]
    own_rows = width // seq_size
    strips = [turn(place, normed, normed_peer, m, 2 * own_rows) for m in range(3)]
    for m in range(1, chips):
        strips[m - 1], near[m] = lax.optimization_barrier((strips[m - 1], near[m]))
    mate = [swap(part, "seq", 1) for part in near]
    strips, near, mate = lax.optimization_barrier((strips, near, mate))

    dq, keep, give = attention(place, valid_len, near, mate, tables(rows, seq_size), score_scale)
    dkv = (keep + wide(swap(give, "seq", 1))).astype(bf)
    dq_parts = [dq[2 * rows * m : 2 * rows * (m + 1)] for m in range(chips)]
    dkv_parts = [dkv[2 * rows * m : 2 * rows * (m + 1)] for m in range(chips)]
    dq_parts = [dq_parts[0]] + [swap(dq_parts[m], "seq", 2 * m) for m in range(1, chips)]
    dkv_parts = [dkv_parts[0]] + [swap(dkv_parts[m], "seq", 2 * m) for m in range(1, chips)]
    normed, normed_peer, dq_parts[1] = lax.optimization_barrier((normed, normed_peer, dq_parts[1]))
    strips = [*strips, turn(place, normed, normed_peer, 3, 2 * own_rows)]
    strips, dq_parts, dkv_parts = lax.optimization_barrier((strips, dq_parts, dkv_parts))
    block_width = width // lax.axis_size("head")

    def left_of(m, lined):
        return jnp.dot(strips[m], lined, preferred_element_type=jnp.float32).astype(bf)

    lined_q, lined_kv, theirs_q, theirs_kv = line_up(place, dq_parts, dkv_parts)
    other_q, other_kv = swap(theirs_q, "seq", 1), swap(theirs_kv, "seq", 1)
    left3_out, right3_out = left_of(3, lined_q), left_of(3, lined_kv)
    left3, right3 = swap(left3_out, "seq", 2), swap(right3_out, "seq", 4)
    left3_out, right3_out, other_q, other_kv = lax.optimization_barrier((left3_out, right3_out, other_q, other_kv))
    xq = stand_up(stand_up_queries_kernel, place, lined_q, other_q)
    xkv = stand_up(stand_up_key_values_kernel, place, lined_kv, other_kv)
    first_out = share(order, 0, xq, xkv, w_query, w_key, w_value, block_width)
    first_in = swap(first_out, "head", 1)
    lined_q, lined_kv, xq, first_out = lax.optimization_barrier((lined_q, lined_kv, xq, first_out))
    left1_out, right2_out = left_of(1, lined_q), left_of(2, lined_kv)
    second_out = share(order, 1, xq, xkv, w_query, w_key, w_value, block_width)
    left3, right3, left1_out, right2_out, second_out, lined_q, lined_kv, xq = lax.optimization_barrier(
        (left3, right3, left1_out, right2_out, second_out, lined_q, lined_kv, xq)
    )
    left1, right2 = swap(left1_out, "seq", 2), swap(right2_out, "seq", 4)
    first_in, left1_out, right2_out, second_out, xq, lined_q, lined_kv = lax.optimization_barrier(
        (first_in, left1_out, right2_out, second_out, xq, lined_q, lined_kv)
    )
    second_in = swap(second_out, "head", 1)
    first_mid = middle_swap((wide(second_out) + wide(first_in)).astype(bf))
    left_out = (wide(left_of(2, lined_q)) + wide(left3)).astype(bf)
    right_out = (wide(left_of(1, lined_kv)) + wide(right3)).astype(bf)
    third = share(order, 2, xq, xkv, w_query, w_key, w_value, block_width)
    left1, right2, left_out, right_out, lined_q, lined_kv, xq = lax.optimization_barrier(
        (left1, right2, left_out, right_out, lined_q, lined_kv, xq)
    )
    left_last, right_last = swap(left_out, "seq", 4), swap(right_out, "seq", 2)
    second_in, first_mid, third, left_out, right_out, lined_q, lined_kv, xq = lax.optimization_barrier(
        (second_in, first_mid, third, left_out, right_out, lined_q, lined_kv, xq)
    )
    inner = (level == 1) | (level == 2)
    third_in = swap(jnp.where(inner, first_mid, third), "head", 1)
    second_mid = middle_swap((wide(third) + wide(second_in)).astype(bf))
    left_sum = (wide(left_of(0, lined_q)) + wide(left1)).astype(bf)
    right_sum = (wide(left_of(0, lined_kv)) + wide(right2)).astype(bf)
    cross = swap(add_up(left_sum, left_last, right_sum, right_last), "seq", 1)
    fourth = share(order, 3, xq, xkv, w_query, w_key, w_value, block_width)
    grad_x = lay_down(fourth, third_in, jnp.where(inner, second_mid, first_in))
    grad_wq, grad_wk, grad_wv = finish(place, left_sum, left_last, right_sum, right_last, cross)
    return (grad_x, grad_wq, grad_wk, grad_wv)


def solution(mesh):
    square = mesh.shape["seq"] == 8 and mesh.shape["head"] == 4
    body = block_body if square else general_body
    placed = (
        P("seq", "head"),
        P("seq", "head"),
        P("seq", "head"),
        P("seq", "head"),
        P("seq", None),
        P(None, "head"),
        P(None, "head"),
        P(None, "head"),
        P(),
    )
    return jax.shard_map(
        body,
        mesh=mesh,
        in_specs=placed,
        out_specs=(P("seq", "head"), P("seq", "head"), P("seq", "head"), P("seq", "head")),
        check_vma=False,
    )
```

```python
import functools
import math

import jax
import jax.numpy as jnp
from jax import lax
from jax.experimental import pallas as pl
from jax.experimental.pallas import tpu as pltpu
from jax.sharding import PartitionSpec as P

D = 4608
H = 32
HD = 128
WINDOW = 4096


SOFT_CAP = 50.0
ROPE_BASE = 10000.0


def passed_along(value, axis, by):
    size = lax.axis_size(axis)
    pairs = [(i, i + by) for i in range(size) if 0 <= i + by < size]
    return lax.ppermute(value, axis, pairs)


def rotate_back(gradient, positions, head_count):
    row_count = gradient.shape[0]
    half_width = HD // 2
    inverse_freq = ROPE_BASE ** (-(jnp.arange(half_width, dtype=jnp.float32) * (2.0 / HD)))
    angles = positions.astype(jnp.float32)[:, None] * inverse_freq[None, :]
    cosine = jnp.cos(angles)[:, None, :]
    sine_part = jnp.sin(angles)[:, None, :]
    per_head = gradient.reshape(row_count, head_count, HD)
    leading = per_head[:, :, :half_width]
    trailing = per_head[:, :, half_width:]
    rotated = jnp.concatenate(
        [leading * cosine + trailing * sine_part, trailing * cosine - leading * sine_part], axis=2
    )
    return rotated.reshape(row_count, head_count * HD)


def times_t(left, right):
    return lax.dot_general(
        left, right, (((1,), (1,)), ((), ())), preferred_element_type=jnp.float32
    )


def inner_rows(left, right):
    return lax.dot_general(
        left, right, (((0,), (0,)), ((), ())), preferred_element_type=jnp.float32
    )


def general_body(queries, keys, values, out_grad, normed, w_query, w_key, w_value, valid_len):
    row_count = queries.shape[0]
    kv_heads = keys.shape[1] // HD
    head_count = queries.shape[1] // HD
    group_size = head_count // kv_heads
    kv_width = kv_heads * HD
    hop_count = WINDOW // row_count
    score_scale = (D // H) ** (-0.5)
    shard_index = lax.axis_index("seq")
    last_shard = valid_len.shape[0] - 1
    row_iota = jnp.arange(row_count, dtype=jnp.int32)
    query_pos = shard_index * row_count + row_iota
    own_valid = row_iota < valid_len[shard_index]
    grad_rows = jnp.where(own_valid[:, None], out_grad, jnp.zeros_like(out_grad))
    query_blocks = queries.reshape(row_count, kv_heads, group_size, HD)
    grad_blocks = grad_rows.reshape(row_count, kv_heads, group_size, HD)
    key_value = jnp.concatenate([keys, values], axis=1)
    arrived = [key_value]
    moving = key_value
    for distance in range(1, hop_count + 1):
        moving = passed_along(moving, "seq", 1)
        arrived.append(moving)
    allowed_list = []
    capped_list = []
    running = jnp.zeros((kv_heads, group_size, row_count), jnp.float32)
    for distance in range(hop_count + 1):
        key_pos = (shard_index - distance) * row_count + row_iota
        owner = jnp.clip(shard_index - distance, 0, last_shard)
        key_valid = row_iota < valid_len[owner]
        offset_gap = query_pos[:, None] - key_pos[None, :]
        allowed = (
            (offset_gap >= 0)
            & (offset_gap < WINDOW)
            & (key_pos[None, :] >= 0)
            & (key_valid[None, :] | (offset_gap == 0))
        )
        key_block = arrived[distance][:, :kv_width].reshape(row_count, kv_heads, HD)
        raw_scores = (
            jnp.einsum(
                "qhgd,khd->hgqk", query_blocks, key_block, preferred_element_type=jnp.float32
            )
            * score_scale
        )
        capped = SOFT_CAP * jnp.tanh(raw_scores / SOFT_CAP)
        running = running + jnp.sum(jnp.where(allowed, jnp.exp(capped), 0.0), axis=-1)
        allowed_list.append(allowed)
        capped_list.append(capped)
    log_total = jnp.log(running)[..., None]
    attended = jnp.zeros((row_count, kv_heads, group_size, HD), jnp.float32)
    for distance in range(hop_count + 1):
        value_block = arrived[distance][:, kv_width:].reshape(row_count, kv_heads, HD)
        rounded = jnp.where(
            allowed_list[distance], jnp.exp(capped_list[distance] - log_total), 0.0
        ).astype(jnp.bfloat16)
        attended = attended + jnp.einsum(
            "hgqk,khd->qhgd", rounded, value_block, preferred_element_type=jnp.float32
        )
    row_delta = jnp.sum(grad_blocks.astype(jnp.float32) * attended, axis=-1)
    delta_cols = jnp.transpose(row_delta, (1, 2, 0))[..., None]
    query_grad = jnp.zeros((row_count, kv_heads, group_size, HD), jnp.float32)
    partials = [None] * (hop_count + 1)
    for distance in range(hop_count, -1, -1):
        key_block = arrived[distance][:, :kv_width].reshape(row_count, kv_heads, HD)
        value_block = arrived[distance][:, kv_width:].reshape(row_count, kv_heads, HD)
        capped = capped_list[distance]
        exact = jnp.where(allowed_list[distance], jnp.exp(capped - log_total), 0.0)
        rounded = exact.astype(jnp.bfloat16)
        grad_probs = jnp.einsum(
            "qhgd,khd->hgqk", grad_blocks, value_block, preferred_element_type=jnp.float32
        )
        grad_scores = (exact * (grad_probs - delta_cols) * (1.0 - (capped / SOFT_CAP) ** 2)).astype(
            jnp.bfloat16
        )
        query_grad = (
            query_grad
            + jnp.einsum(
                "hgqk,khd->qhgd", grad_scores, key_block, preferred_element_type=jnp.float32
            )
            * score_scale
        )
        key_grad = (
            jnp.einsum(
                "hgqk,qhgd->khd", grad_scores, query_blocks, preferred_element_type=jnp.float32
            )
            * score_scale
        )
        value_grad = jnp.einsum(
            "hgqk,qhgd->khd", rounded, grad_blocks, preferred_element_type=jnp.float32
        )
        partials[distance] = jnp.concatenate(
            [key_grad.reshape(row_count, kv_width), value_grad.reshape(row_count, kv_width)], axis=1
        )
    carried = partials[hop_count]
    for distance in range(hop_count - 1, -1, -1):
        carried = (
            passed_along(carried.astype(jnp.bfloat16), "seq", -1).astype(carried.dtype)
            + partials[distance]
        )
    query_pre = rotate_back(
        query_grad.reshape(row_count, head_count * HD), query_pos, head_count
    ).astype(jnp.bfloat16)
    key_pre = rotate_back(carried[:, :kv_width], query_pos, kv_heads).astype(jnp.bfloat16)
    value_pre = carried[:, kv_width:].astype(jnp.bfloat16)
    input_terms = (
        times_t(query_pre, w_query) + times_t(key_pre, w_key) + times_t(value_pre, w_value)
    )
    grad_x = lax.psum_scatter(
        input_terms.astype(jnp.bfloat16), "head", scatter_dimension=1, tiled=True
    )
    stacked = jnp.concatenate([query_pre, key_pre, value_pre], axis=1)
    weight_total = lax.psum_scatter(
        inner_rows(normed, stacked).astype(jnp.bfloat16), "seq", scatter_dimension=0, tiled=True
    ).astype(jnp.float32)
    query_cols = head_count * HD
    grad_wq = weight_total[:, :query_cols].astype(jnp.bfloat16)
    grad_wk = weight_total[:, query_cols : query_cols + kv_width].astype(jnp.bfloat16)
    grad_wv = weight_total[:, query_cols + kv_width :].astype(jnp.bfloat16)
    return (grad_x, grad_wq, grad_wk, grad_wv)
QB = 512
KB = 512
PACK_ROWS = 128
SHARE_COLS = 384
MIB = 1024 * 1024
NT = (((1,), (1,)), ((), ()))
NN = (((1,), (0,)), ((), ()))


def dot(a, b, dims):
    return lax.dot_general(a, b, dims, preferred_element_type=jnp.float32)


def attention_kernel(shards, rows, score_scale, place, lens, *refs):
    n = shards
    chips = n // 2
    near, mate = refs[:chips], refs[chips : 2 * chips]
    refs = refs[2 * chips :]
    cos_r, sin_r, cos_s, sin_s = refs[:4]
    dq_out, keep_out, give_out = refs[4:7]
    (q2, k2, kT, gx, vx, alive, probs, slopes, dps, dq, dk, dv, dqT, qT, gT, sems) = refs[7:]
    me = place[0]
    core = lax.rem(me, 2)
    copies = []
    first_part, second_part, third_part = pl.ds(0, 2 * HD), pl.ds(2 * HD, 2 * HD), pl.ds(4 * HD, 2 * HD)
    for m in range(chips):
        own = pl.ds(pl.multiple_of(place[1 + 2 * m] * rows, rows), rows)
        other = pl.ds(pl.multiple_of(place[2 + 2 * m] * rows, rows), rows)
        copies.append(pltpu.make_async_copy(near[m].at[:, pl.ds(0, 4 * HD)], probs.at[own, :], sems.at[0, m]))
        copies.append(pltpu.make_async_copy(mate[m].at[:, second_part], probs.at[other, second_part], sems.at[1, m]))
        copies.append(pltpu.make_async_copy(mate[m].at[:, third_part], probs.at[other, first_part], sems.at[2, m]))
    for copy in copies:
        copy.start()
    dk[...] = jnp.zeros_like(dk)
    dv[...] = jnp.zeros_like(dv)
    for copy in copies:
        copy.wait()

    piece = 128
    lane = lax.broadcasted_iota(jnp.int32, (piece, HD), 1)

    def pack_shard(shard, offset):
        valid = lens[shard]

        def pack_piece(i, _):
            src = pl.multiple_of(i * piece, piece)
            dst = pl.multiple_of(offset + i * piece, 16)
            live = (lax.broadcasted_iota(jnp.int32, (piece, HD), 0) + src) < valid
            at = pl.ds(pl.multiple_of(shard * rows + src, piece), piece)
            to = pl.ds(dst, piece)
            q = jnp.where(live, probs[at, :HD].astype(jnp.float32), 0.0) * (score_scale / SOFT_CAP)
            hi = q.astype(jnp.bfloat16)
            q2[to, :HD] = hi
            q2[to, HD:] = (q - hi.astype(jnp.float32)).astype(jnp.bfloat16)
            zero = jnp.zeros((piece, HD), jnp.bfloat16)
            gx[to, :] = jnp.where(live, probs[at, HD : 2 * HD], zero)
            k = jnp.where(live, probs[at, 2 * HD : 3 * HD], zero)
            k2[to, :HD] = k
            k2[to, HD:] = k
            vx[to, :] = jnp.where(live, probs[at, 3 * HD : 4 * HD], zero)
            alive[to, :] = jnp.where(live, 1.0, 0.0)
            return 0

        lax.fori_loop(0, pl.cdiv(valid, piece), pack_piece, 0)
        return offset + ((valid + 15) // 16) * 16

    end = lax.fori_loop(0, n, pack_shard, jnp.int32(0))
    tail = pl.ds(pl.multiple_of(end, 16), KB)
    for ref in (q2, k2, gx, vx, alive):
        ref[tail, :] = jnp.zeros((KB, ref.shape[1]), ref.dtype)
    blocks = pl.cdiv(end, QB)

    def turn(i, _):
        at = pl.ds(pl.multiple_of(i * KB, KB), KB)
        kT[:, at] = k2[at, :HD].T
        return 0

    lax.fori_loop(0, pl.cdiv(end, KB), turn, 0)

    def block(b, _):
        first = pl.multiple_of(b * QB, QB)
        own = pl.ds(first, QB)
        qT[...] = q2[own, :].T
        gT[...] = gx[own, :].T
        dqT[...] = jnp.zeros_like(dqT)

        def forward(at, late, sums, masked):
            size = at.size
            t = jnp.tanh(dot(k2[at, :], qT[:, late:], NN))
            dp = dot(vx[at, :], gT[:, late:], NN)
            e = jnp.exp2(t * (SOFT_CAP * math.log2(math.e)))
            e = e * jnp.concatenate([alive[at, :]] * ((QB - late) // HD), axis=1)
            if masked:
                key = lax.broadcasted_iota(jnp.int32, e.shape, 0)
                query = lax.broadcasted_iota(jnp.int32, e.shape, 1)
                e = jnp.where(key <= query, e, 0.0)
            probs[at, late:] = e.astype(jnp.bfloat16)
            slopes[at, late:] = (e * (1.0 - t * t)).astype(jnp.bfloat16)
            dps[at, late:] = dp
            new = [jnp.sum(e, axis=0, keepdims=True), jnp.sum(e * dp, axis=0, keepdims=True)]
            if late:
                new = [jnp.concatenate([jnp.zeros((1, late), jnp.float32), x], axis=1) for x in new]
            return sums[0] + new[0], sums[1] + new[1]

        def chunk(c):
            return pl.ds(pl.multiple_of(c * KB, KB), KB)

        half = QB // 2
        early_keys = pl.ds(first, half)
        late_keys = pl.ds(pl.multiple_of(first + half, half), half)
        zero = jnp.zeros((1, QB), jnp.float32)
        sums = lax.fori_loop(0, b, lambda c, sums: forward(chunk(c), 0, sums, False), (zero, zero))
        sums = forward(early_keys, 0, sums, True)
        total, weighted = forward(late_keys, half, sums, True)
        inv = 1.0 / total
        delta = weighted * inv
        gs = (gT[...].astype(jnp.float32) * inv).astype(jnp.bfloat16).T
        q = qT[:HD, :].astype(jnp.float32) + qT[HD:, :].astype(jnp.float32)
        qs = (q * (inv * SOFT_CAP)).astype(jnp.bfloat16).T

        def backward(at, late):
            ds = slopes[at, late:] * (dps[at, late:] - delta[:, late:]).astype(jnp.bfloat16)
            dqT[:, late:] += dot(kT[:, at], ds, NN)
            dk[at, :] += dot(ds, qs[late:, :], NN)
            dv[at, :] += dot(probs[at, late:], gs[late:, :], NN)

        lax.fori_loop(0, b, lambda c, _: (backward(chunk(c), 0), 0)[1], 0)
        backward(early_keys, 0)
        backward(late_keys, half)
        dq[own, :] = (dqT[...] * (inv * score_scale)).T
        return 0

    lax.fori_loop(0, blocks, block, 0)

    def unpack(j, _):
        shard = place[1 + j]
        offset = lax.fori_loop(0, shard, lambda s, o: o + ((lens[s] + 15) // 16) * 16, jnp.int32(0))
        valid = lens[shard]
        ca, sa = cos_s[pl.ds(shard, 1), :], sin_s[pl.ds(shard, 1), :]

        swapped = j + 1 - 2 * lax.rem(j, 2)

        def unpack_piece(i, _):
            dst = pl.multiple_of(i * piece, piece)
            src = pl.ds(pl.multiple_of(offset + i * piece, 16), piece)
            live = (lax.broadcasted_iota(jnp.int32, (piece, HD), 0) + dst) < valid
            cb, sb = cos_r[pl.ds(dst, piece), :], sin_r[pl.ds(dst, piece), :]
            cosine = ca * cb - sa * sb
            sine = sa * cb + ca * sb
            sine = jnp.where(lane < HD // 2, sine, -sine)

            def rotate(x):
                return x * cosine + pltpu.roll(x, HD // 2, 1) * sine

            to = pl.ds(pl.multiple_of(j * rows + i * piece, piece), piece)
            dq_out[to, :] = jnp.where(live, rotate(dq[src, :]), 0.0).astype(jnp.bfloat16)
            key_part = jnp.where(live, rotate(dk[src, :]), 0.0)
            value_part = jnp.where(live, dv[src, :], 0.0)
            keep_out[to, :] = jnp.where(core == 0, key_part, value_part)
            to = pl.ds(pl.multiple_of(swapped * rows + i * piece, piece), piece)
            give_out[to, :] = jnp.where(core == 0, value_part, key_part).astype(jnp.bfloat16)
            return 0

        def clear_piece(i, _):
            to = pl.ds(pl.multiple_of(j * rows + i * piece, piece), piece)
            dq_out[to, :] = jnp.zeros((piece, HD), jnp.bfloat16)
            keep_out[to, :] = jnp.zeros((piece, HD), jnp.float32)
            to = pl.ds(pl.multiple_of(swapped * rows + i * piece, piece), piece)
            give_out[to, :] = jnp.zeros((piece, HD), jnp.bfloat16)
            return 0

        used = pl.cdiv(valid, piece)
        lax.fori_loop(0, used, unpack_piece, 0)
        lax.fori_loop(used, rows // piece, clear_piece, 0)
        return 0

    lax.fori_loop(0, n, unpack, 0)


def attention(place, lens, near, mate, tables, score_scale):
    chips = len(near)
    n, rows = 2 * chips, near[0].shape[0]
    tokens = n * rows
    room = tokens + KB
    bf, f32 = jnp.bfloat16, jnp.float32
    any_spec = pl.BlockSpec(memory_space=pl.ANY)
    smem = pl.BlockSpec(memory_space=pltpu.SMEM)
    vmem = pl.BlockSpec(memory_space=pltpu.VMEM)
    return pl.pallas_call(
        functools.partial(attention_kernel, n, rows, score_scale),
        out_shape=(
            jax.ShapeDtypeStruct((tokens, HD), bf),
            jax.ShapeDtypeStruct((tokens, HD), f32),
            jax.ShapeDtypeStruct((tokens, HD), bf),
        ),
        in_specs=[smem, smem] + [any_spec] * (2 * chips) + [vmem] * 4,
        out_specs=(vmem, vmem, vmem),
        scratch_shapes=[
            pltpu.VMEM((room, 2 * HD), bf),
            pltpu.VMEM((room, 2 * HD), bf),
            pltpu.VMEM((HD, room), bf),
            pltpu.VMEM((room, HD), bf),
            pltpu.VMEM((room, HD), bf),
            pltpu.VMEM((room, HD), f32),
            pltpu.VMEM((room, QB), bf),
            pltpu.VMEM((room, QB), bf),
            pltpu.VMEM((room, QB), f32),
            pltpu.VMEM((room, HD), f32),
            pltpu.VMEM((room, HD), f32),
            pltpu.VMEM((room, HD), f32),
            pltpu.VMEM((HD, QB), f32),
            pltpu.VMEM((2 * HD, QB), bf),
            pltpu.VMEM((HD, QB), bf),
            pltpu.SemaphoreType.DMA((3, chips)),
        ],
        compiler_params=pltpu.CompilerParams(vmem_limit_bytes=42 * MIB),
        cost_estimate=pl.CostEstimate(
            flops=12 * tokens * tokens * HD, bytes_accessed=16 * tokens * HD, transcendentals=tokens * tokens
        ),
        name="attention",
    )(place, lens, *near, *mate, *tables)


def tables(rows, shards):
    half = HD // 2
    freq = 10000.0 ** (-(jnp.arange(half, dtype=jnp.float32) * (2.0 / HD)))
    freq = jnp.concatenate([freq, freq])[None, :]
    within = jnp.arange(rows, dtype=jnp.float32)[:, None] * freq
    start = (jnp.arange(shards, dtype=jnp.float32) * rows)[:, None] * freq
    return jnp.cos(within), jnp.sin(within), jnp.cos(start), jnp.sin(start)


def pack_kernel(place, q, k, v, g, *refs):
    blocks, sems = refs[:-1], refs[-1]
    core = lax.rem(place[0], 2)
    copies = []
    for m, block in enumerate(blocks):
        chip = place[1 + 2 * m] // 2
        own, other = 2 * chip + core, 2 * chip + 1 - core
        for at, (src, head) in enumerate(((q, own), (g, own), (k, chip), (v, chip), (q, other), (g, other))):
            cols = pl.ds(pl.multiple_of(head * HD, HD), HD)
            copies.append(pltpu.make_async_copy(src.at[:, cols], block.at[:, pl.ds(at * HD, HD)], sems.at[m, at]))
    for started in copies:
        started.start()
    for started in copies:
        started.wait()


def pack(place, q, k, v, g, n):
    rows = q.shape[0]
    vmem = pl.BlockSpec(memory_space=pltpu.VMEM)
    return pl.pallas_call(
        pack_kernel,
        out_shape=[jax.ShapeDtypeStruct((rows, 6 * HD), q.dtype)] * n,
        in_specs=[pl.BlockSpec(memory_space=pltpu.SMEM)] + [pl.BlockSpec(memory_space=pltpu.HBM)] * 4,
        out_specs=[vmem] * n,
        scratch_shapes=[pltpu.SemaphoreType.DMA((n, 6))],
        compiler_params=pltpu.CompilerParams(vmem_limit_bytes=60 * MIB),
        name="pack",
    )(place, q, k, v, g)


def line_up_kernel(place, *refs):
    n = (len(refs) - 4) // 2
    for parts, out, theirs in ((refs[:n], refs[-4], refs[-2]), (refs[n : 2 * n], refs[-3], refs[-1])):
        rows = theirs.shape[0]
        for m, src in enumerate(parts):
            chip = place[1 + 2 * m] // 2
            cols = pl.ds(pl.multiple_of(chip * HD, HD), HD)
            theirs[:, cols] = src[rows:, :]
            out[:, cols] = src[...]


def line_up(place, left, right):
    rows = left[0].shape[0]
    cols = len(left) * HD
    vmem = pl.BlockSpec(memory_space=pltpu.VMEM)
    return pl.pallas_call(
        line_up_kernel,
        out_shape=[jax.ShapeDtypeStruct((r, cols), left[0].dtype) for r in (rows, rows, rows // 2, rows // 2)],
        in_specs=[pl.BlockSpec(memory_space=pltpu.SMEM)] + [vmem] * (2 * len(left)),
        out_specs=[vmem] * 4,
        compiler_params=pltpu.CompilerParams(vmem_limit_bytes=12 * MIB),
        name="line_up",
    )(place, *left, *right)


def add_up_kernel(left, left_last, right, right_last, out):
    rows, half = out.shape[0], out.shape[1] // 2
    for which, (a, b) in enumerate(((left, left_last), (right, right_last))):
        total = a[rows:, :].astype(jnp.float32) + b[rows:, :].astype(jnp.float32)
        out[:, which * half : (which + 1) * half] = total.astype(out.dtype)


def add_up(*shares):
    rows, half = shares[0].shape
    vmem = pl.BlockSpec(memory_space=pltpu.VMEM)
    return pl.pallas_call(
        add_up_kernel,
        out_shape=jax.ShapeDtypeStruct((rows // 2, 2 * half), shares[0].dtype),
        in_specs=[vmem] * 4,
        out_specs=vmem,
        compiler_params=pltpu.CompilerParams(vmem_limit_bytes=12 * MIB),
        name="add_up",
    )(*shares)


def finish_kernel(place, left, left_last, right, right_last, cross, grad_wq, grad_wk, grad_wv):
    core = lax.rem(place[0], 2)
    rows, half = grad_wk.shape

    def add(a, b, cols):
        return (a[:rows, cols].astype(jnp.float32) + b[:rows, cols].astype(jnp.float32)).astype(jnp.bfloat16)

    for h in range(half // HD):
        cols = slice(h * HD, (h + 1) * HD)
        mine, other = add(left, left_last, cols), cross[:, cols]
        grad_wq[:, 2 * h * HD : (2 * h + 1) * HD] = jnp.where(core == 0, mine, other)
        grad_wq[:, (2 * h + 1) * HD : (2 * h + 2) * HD] = jnp.where(core == 0, other, mine)
        mine, other = add(right, right_last, cols), cross[:, half + h * HD : half + (h + 1) * HD]
        grad_wk[:, cols] = jnp.where(core == 0, mine, other)
        grad_wv[:, cols] = jnp.where(core == 0, other, mine)


def finish(place, left, left_last, right, right_last, cross):
    rows, half = cross.shape[0], left.shape[1]
    vmem = pl.BlockSpec(memory_space=pltpu.VMEM)
    return pl.pallas_call(
        finish_kernel,
        out_shape=[jax.ShapeDtypeStruct((rows, w), jnp.bfloat16) for w in (2 * half, half, half)],
        in_specs=[pl.BlockSpec(memory_space=pltpu.SMEM)] + [vmem] * 5,
        out_specs=[vmem] * 3,
        compiler_params=pltpu.CompilerParams(vmem_limit_bytes=14 * MIB),
        name="finish",
    )(place, left, left_last, right, right_last, cross)


def swap(value, axis, by):
    size = lax.axis_size(axis)
    return lax.ppermute(value, axis, [(i, i ^ by) for i in range(size)])


def middle_swap(value):
    levels = lax.axis_size("head")
    pairs = []
    for s in range(lax.axis_size("seq")):
        for h in range(levels):
            to = s * levels + (3 - h) if h in (1, 2) else (s ^ 1) * levels + h
            pairs.append((s * levels + h, to))
    return lax.ppermute(value, ("seq", "head"), pairs)


def wide(value):
    return value.astype(jnp.float32)


def turn_kernel(place, own, peer, out):
    core = lax.rem(place[0], 2)
    rows = own.shape[0]
    strip = out.shape[0] // 2
    for which, src in ((0, own), (1, peer)):
        cols = slice(which * rows, (which + 1) * rows)
        turned = src[...].T

        @pl.when(core == 0)
        def _():
            out[:, cols] = turned

        @pl.when(core == 1)
        def _():
            out[:strip, cols] = turned[strip:]
            out[strip:, cols] = turned[:strip]


def turn(place, own, peer, m, strip):
    rows = own.shape[0]
    spec = pl.BlockSpec((rows, strip), lambda i, place: (0, place[1 + 2 * m] // 2))
    return pl.pallas_call(
        turn_kernel,
        out_shape=jax.ShapeDtypeStruct((strip, 2 * rows), own.dtype),
        grid_spec=pltpu.PrefetchScalarGridSpec(
            num_scalar_prefetch=1,
            grid=(1,),
            in_specs=[spec, spec],
            out_specs=pl.BlockSpec((strip, 2 * rows), lambda i, place: (0, 0)),
        ),
        compiler_params=pltpu.CompilerParams(vmem_limit_bytes=16 * MIB),
        name="turn",
    )(place, own, peer)


def stand_up_queries_kernel(place, mine, other, out):
    core = lax.rem(place[0], 2)
    for h in range(mine.shape[1] // HD):
        cols = slice(h * HD, (h + 1) * HD)
        out[pl.ds(pl.multiple_of((2 * h + core) * HD, HD), HD), :] = mine[:, cols].T
        out[pl.ds(pl.multiple_of((2 * h + 1 - core) * HD, HD), HD), :] = other[:, cols].T


def stand_up_key_values_kernel(place, mine, other, out):
    core = lax.rem(place[0], 2)
    half = mine.shape[1]
    out[pl.ds(pl.multiple_of(core * half, HD), half), :] = mine[...].T
    out[pl.ds(pl.multiple_of((1 - core) * half, HD), half), :] = other[...].T


def stand_up(kernel, place, lined, other):
    rows, cols = other.shape
    spec = pl.BlockSpec((rows, cols), lambda i: (0, 0))
    return pl.pallas_call(
        kernel,
        out_shape=jax.ShapeDtypeStruct((2 * cols, rows), other.dtype),
        grid=(1,),
        in_specs=[pl.BlockSpec(memory_space=pltpu.SMEM), spec, spec],
        out_specs=pl.BlockSpec((2 * cols, rows), lambda i: (0, 0)),
        compiler_params=pltpu.CompilerParams(vmem_limit_bytes=8 * MIB),
        name="stand_up",
    )(place, lined, other)


def share_kernel(order, xq, xkv, w_query, w_key, w_value, out):
    kv_cols = w_key.shape[1]
    total = dot(w_query[...], xq[...], NN)
    total += dot(w_key[...], xkv[:kv_cols, :], NN)
    total += dot(w_value[...], xkv[kv_cols:, :], NN)
    out[...] = total.astype(out.dtype)


def share(order, i, xq, xkv, w_query, w_key, w_value, width):
    rows = xq.shape[1]
    steps = width // SHARE_COLS
    weights = (w_query, w_key, w_value)
    depth = sum(w.shape[1] for w in weights)
    return pl.pallas_call(
        share_kernel,
        out_shape=jax.ShapeDtypeStruct((width, rows), xq.dtype),
        grid_spec=pltpu.PrefetchScalarGridSpec(
            num_scalar_prefetch=1,
            grid=(steps,),
            in_specs=[pl.BlockSpec(x.shape, lambda j, order: (0, 0)) for x in (xq, xkv)]
            + [pl.BlockSpec((SHARE_COLS, w.shape[1]), lambda j, order: (order[i] * steps + j, 0)) for w in weights],
            out_specs=pl.BlockSpec((SHARE_COLS, rows), lambda j, order: (j, 0)),
        ),
        compiler_params=pltpu.CompilerParams(vmem_limit_bytes=14 * MIB),
        cost_estimate=pl.CostEstimate(flops=2 * rows * depth * width, bytes_accessed=2 * depth * width, transcendentals=0),
        name="share",
    )(order, xq, xkv, *weights)


def lay_down_kernel(a, b, c, out):
    total = a[...].astype(jnp.float32) + b[...].astype(jnp.float32) + c[...].astype(jnp.float32)
    out[...] = total.astype(out.dtype).T


def lay_down(a, b, c):
    vmem = pl.BlockSpec(memory_space=pltpu.VMEM)
    return pl.pallas_call(
        lay_down_kernel,
        out_shape=jax.ShapeDtypeStruct(a.shape[::-1], a.dtype),
        in_specs=[vmem] * 3,
        out_specs=vmem,
        compiler_params=pltpu.CompilerParams(vmem_limit_bytes=16 * MIB),
        name="lay_down",
    )(a, b, c)


BLOCK_ORDER = ((3, 2, 1, 0), (0, 3, 2, 1), (3, 0, 1, 2), (0, 1, 2, 3))


def block_body(queries, keys, values, out_grad, normed, w_query, w_key, w_value, valid_len):
    bf = jnp.bfloat16
    seq_size = lax.axis_size("seq")
    rows = queries.shape[0]
    score_scale = (D // H) ** (-0.5)
    me = lax.axis_index("seq")
    core = me % 2
    chip = me // 2
    level = lax.axis_index("head")
    chips = seq_size // 2
    place = jnp.stack([me] + [me ^ m for m in range(seq_size)]).astype(jnp.int32)

    order = jnp.array(BLOCK_ORDER, jnp.int32)[level]
    place, order = lax.optimization_barrier((place, order))
    near = list(pack(place, queries, keys, values, out_grad, chips))
    normed_peer = swap(normed, "seq", 1)
    normed, normed_peer, _ = lax.optimization_barrier((normed, normed_peer, near[0]))
    near = [near[0]] + [swap(near[m], "seq", 2 * m) for m in range(1, chips)]
    width = normed.shape[1]
    own_rows = width // seq_size
    strips = [turn(place, normed, normed_peer, m, 2 * own_rows) for m in range(3)]
    for m in range(1, chips):
        strips[m - 1], near[m] = lax.optimization_barrier((strips[m - 1], near[m]))
    mate = [swap(part, "seq", 1) for part in near]
    strips, near, mate = lax.optimization_barrier((strips, near, mate))

    dq, keep, give = attention(place, valid_len, near, mate, tables(rows, seq_size), score_scale)
    dkv = (keep + wide(swap(give, "seq", 1))).astype(bf)
    dq_parts = [dq[2 * rows * m : 2 * rows * (m + 1)] for m in range(chips)]
    dkv_parts = [dkv[2 * rows * m : 2 * rows * (m + 1)] for m in range(chips)]
    dq_parts = [dq_parts[0]] + [swap(dq_parts[m], "seq", 2 * m) for m in range(1, chips)]
    dkv_parts = [dkv_parts[0]] + [swap(dkv_parts[m], "seq", 2 * m) for m in range(1, chips)]
    normed, normed_peer, dq_parts[1] = lax.optimization_barrier((normed, normed_peer, dq_parts[1]))
    strips = [*strips, turn(place, normed, normed_peer, 3, 2 * own_rows)]
    strips, dq_parts, dkv_parts = lax.optimization_barrier((strips, dq_parts, dkv_parts))
    block_width = width // lax.axis_size("head")

    def left_of(m, lined):
        return jnp.dot(strips[m], lined, preferred_element_type=jnp.float32).astype(bf)

    lined_q, lined_kv, theirs_q, theirs_kv = line_up(place, dq_parts, dkv_parts)
    other_q, other_kv = swap(theirs_q, "seq", 1), swap(theirs_kv, "seq", 1)
    left3_out, right3_out = left_of(3, lined_q), left_of(3, lined_kv)
    left3, right3 = swap(left3_out, "seq", 2), swap(right3_out, "seq", 4)
    left3_out, right3_out, other_q, other_kv = lax.optimization_barrier((left3_out, right3_out, other_q, other_kv))
    xq = stand_up(stand_up_queries_kernel, place, lined_q, other_q)
    xkv = stand_up(stand_up_key_values_kernel, place, lined_kv, other_kv)
    first_out = share(order, 0, xq, xkv, w_query, w_key, w_value, block_width)
    first_in = swap(first_out, "head", 1)
    lined_q, lined_kv, xq, first_out = lax.optimization_barrier((lined_q, lined_kv, xq, first_out))
    left1_out, right2_out = left_of(1, lined_q), left_of(2, lined_kv)
    second_out = share(order, 1, xq, xkv, w_query, w_key, w_value, block_width)
    left3, right3, left1_out, right2_out, second_out, lined_q, lined_kv, xq = lax.optimization_barrier(
        (left3, right3, left1_out, right2_out, second_out, lined_q, lined_kv, xq)
    )
    left1, right2 = swap(left1_out, "seq", 2), swap(right2_out, "seq", 4)
    first_in, left1_out, right2_out, second_out, xq, lined_q, lined_kv = lax.optimization_barrier(
        (first_in, left1_out, right2_out, second_out, xq, lined_q, lined_kv)
    )
    second_in = swap(second_out, "head", 1)
    first_mid = middle_swap((wide(second_out) + wide(first_in)).astype(bf))
    left_out = (wide(left_of(2, lined_q)) + wide(left3)).astype(bf)
    right_out = (wide(left_of(1, lined_kv)) + wide(right3)).astype(bf)
    third = share(order, 2, xq, xkv, w_query, w_key, w_value, block_width)
    fourth = share(order, 3, xq, xkv, w_query, w_key, w_value, block_width)
    left1, right2, left_out, right_out, lined_q, lined_kv, xq = lax.optimization_barrier(
        (left1, right2, left_out, right_out, lined_q, lined_kv, xq)
    )
    left_last, right_last = swap(left_out, "seq", 4), swap(right_out, "seq", 2)
    second_in, first_mid, third, fourth, left_out, right_out, lined_q, lined_kv = lax.optimization_barrier(
        (second_in, first_mid, third, fourth, left_out, right_out, lined_q, lined_kv)
    )
    inner = (level == 1) | (level == 2)
    third_in = swap(jnp.where(inner, first_mid, third), "head", 1)
    second_mid = middle_swap((wide(third) + wide(second_in)).astype(bf))
    left_sum = (wide(left_of(0, lined_q)) + wide(left1)).astype(bf)
    right_sum = (wide(left_of(0, lined_kv)) + wide(right2)).astype(bf)
    cross = swap(add_up(left_sum, left_last, right_sum, right_last), "seq", 1)
    grad_x = lay_down(fourth, third_in, jnp.where(inner, second_mid, first_in))
    grad_wq, grad_wk, grad_wv = finish(place, left_sum, left_last, right_sum, right_last, cross)
    return (grad_x, grad_wq, grad_wk, grad_wv)


def solution(mesh):
    square = mesh.shape["seq"] == 8 and mesh.shape["head"] == 4
    body = block_body if square else general_body
    placed = (
        P("seq", "head"),
        P("seq", "head"),
        P("seq", "head"),
        P("seq", "head"),
        P("seq", None),
        P(None, "head"),
        P(None, "head"),
        P(None, "head"),
        P(),
    )
    return jax.shard_map(
        body,
        mesh=mesh,
        in_specs=placed,
        out_specs=(P("seq", "head"), P("seq", "head"), P("seq", "head"), P("seq", "head")),
        check_vma=False,
    )
```
